32 devices in a mesh: dp: 4 (over y, core), seq: 8 (over z, x).
Axes of the slice: x: 2, y: 2, z: 4, core: 2. Of those that a mesh axis runs over, the one named last changes fastest.
Arguments:
- decoder_in: bfloat16 [4, 3072, 768], P('dp', 'seq'), may hold values from -6 to 6
- encoder_states: bfloat16 [4, 2048, 768], P('dp', 'seq'), may hold values from -6 to 6
- encoder_doc: int32 [4, 2048], P('dp', 'seq'), may hold values from 0 to 3, as said below
- decoder_doc: int32 [4, 24], P('dp'), may hold values from 0 to 3, as said below
- cotangent: bfloat16 [4, 3072, 768], P('dp', 'seq'), may hold values from -6 to 6
- gain_self: float32 [768], replicated, may hold values from 0.5 to 1.5
- gain_cross: float32 [768], replicated, may hold values from 0.5 to 1.5
- gain_ffn: float32 [768], replicated, may hold values from 0.5 to 1.5
- self_query: bfloat16 [768, 768], replicated, may hold values from -0.21875 to 0.21875
- self_key: bfloat16 [768, 768], replicated, may hold values from -0.21875 to 0.21875
- self_value: bfloat16 [768, 768], replicated, may hold values from -0.21875 to 0.21875
- self_out: bfloat16 [768, 768], replicated, may hold values from -0.625 to 0.625
- bias_table: float32 [32, 12], replicated, may hold values from -4 to 4
- cross_query: bfloat16 [768, 768], replicated, may hold values from -0.21875 to 0.21875
- cross_key: bfloat16 [768, 768], replicated, may hold values from -0.21875 to 0.21875
- cross_value: bfloat16 [768, 768], replicated, may hold values from -0.21875 to 0.21875
- cross_out: bfloat16 [768, 768], replicated, may hold values from -0.875 to 0.875
- ff_in: bfloat16 [768, 3072], replicated, may hold values from -0.21875 to 0.21875
- ff_out: bfloat16 [3072, 768], replicated, may hold values from -0.15625 to 0.15625
Outputs:
- output: bfloat16 [4, 3072, 768], P('dp', 'seq')
- input_grad: float32 [4, 3072, 768], P('dp', 'seq')
- encoder_grad: float32 [4, 2048, 768], P('dp', 'seq')
- gain_self_grad: float32 [768], P('seq')
- gain_cross_grad: float32 [768], P('seq')
- gain_ffn_grad: float32 [768], P('seq')
- self_query_grad: float32 [768, 768], P('seq', 'dp')
- self_key_grad: float32 [768, 768], P('seq', 'dp')
- self_value_grad: float32 [768, 768], P('seq', 'dp')
- self_out_grad: float32 [768, 768], P('seq', 'dp')
- bias_grad: float32 [32, 12], P('seq')
- cross_query_grad: float32 [768, 768], P('seq', 'dp')
- cross_key_grad: float32 [768, 768], P('seq', 'dp')
- cross_value_grad: float32 [768, 768], P('seq', 'dp')
- cross_out_grad: float32 [768, 768], P('seq', 'dp')
- ff_in_grad: float32 [768, 3072], P('seq', 'dp')
- ff_out_grad: float32 [3072, 768], P('seq', 'dp')
The draws below stay inside these ranges and needn't reach their ends.
Inputs may be any that keep to these rules, and one draw needn't show every extreme that they name: Within each group, encoder_doc never falls along the tokens and each of the 4 documents has at least one encoder token; one document, which one drawn from the seed, has encoder tokens in the shard of every device of seq. `decoder_doc`: every document of a group is read by at least one of its decoder sequences.
All inputs are finite; a program needn't handle non-finite values.
Results may differ from the reference program's by a relative error of at most 0.04.
Values may be sent and summed in bfloat16 or wider, within the bound.
No kernel may reach another device: no remote copies, remote signals or barrier semaphores. Data moves between devices by JAX's collectives and lax.ppermute only.
A program may use at most 256 MiB of HBM per device.

```python
import math
from functools import partial
import jax
import jax.numpy as jnp
from jax import lax

D = 768
HEADS = 12
HEAD = 64
FF = 3072
BUCKETS = 32
MAX_REACH = 128
DEC_LEN = 128
DOC_DEV = 3
ENC_DEV = 256
DOCS = 24
GROUP_ENC = 2048
GROUP_DEC = 3072
N_DP = 4


def group_documents(key):
    short_count = DOC_DEV
    doc_total = short_count + 1
    short_most = (ENC_DEV - 1) // short_count
    short_least = max(1, short_most // 2)
    pick_key, length_key, order_key = jax.random.split(key, 3)
    chosen = jax.random.randint(pick_key, (), 0, doc_total, dtype=jnp.int32)
    lengths = jax.random.randint(length_key, (doc_total,), short_least, short_most + 1, dtype=jnp.int32)
    index = jnp.arange(doc_total, dtype=jnp.int32)
    before = jnp.where(index < chosen, lengths, 0)
    after = jnp.where(index > chosen, lengths, 0)
    ends_before = jnp.cumsum(before)
    after_total = jnp.sum(after)
    starts_after = GROUP_ENC - after_total + jnp.cumsum(after) - after
    tokens = jnp.arange(GROUP_ENC, dtype=jnp.int32)
    count_before = jnp.sum(((index[:, None] < chosen) & (ends_before[:, None] <= tokens[None, :])).astype(jnp.int32), axis=0)
    count_after = jnp.sum(((index[:, None] > chosen) & (starts_after[:, None] <= tokens[None, :])).astype(jnp.int32), axis=0)
    encoder_row = (count_before + count_after).astype(jnp.int32)
    order = jax.random.permutation(order_key, DOCS).astype(jnp.int32)
    rank = jnp.zeros((DOCS,), jnp.int32).at[order].set(jnp.arange(DOCS, dtype=jnp.int32))
    short_id = rank + (rank >= chosen).astype(jnp.int32)
    decoder_row = jnp.where(rank < short_count, short_id, chosen).astype(jnp.int32)
    return (encoder_row, decoder_row)


def draw_encoder_doc(key, part):
    shared = jax.vmap(group_documents)(jax.random.split(key, N_DP))
    return shared[0]


def draw_decoder_doc(key, part):
    shared = jax.vmap(group_documents)(jax.random.split(key, N_DP))
    return shared[1]


def draw_cotangent(key, part):
    key = jax.random.fold_in(key, 23)
    shape = (N_DP, GROUP_DEC, D)
    values = jax.random.normal(key, shape, jnp.float32)
    return jnp.clip(values, -6.0, 6.0).astype(jnp.bfloat16)


def shard_levels(own_key, extent, cuts, low, high):
    loudness = 1.0
    for dim, parts in cuts:
        heights = jax.random.uniform(jax.random.fold_in(jax.random.fold_in(own_key, 6), dim), (parts,), jnp.float32, low / len(cuts), high / len(cuts))
        loudness = loudness * jnp.repeat(jnp.exp(heights), extent[dim] // parts).reshape((-1,) + (1,) * (len(extent) - 1 - dim))
    return loudness


def bell_draw(rng, shape, deviation, reach, shards=(), kind=jnp.bfloat16):
    factor_of = shard_levels(rng, shape, shards, -0.22, 0.18) if shards else 1.0
    array = jax.random.normal(rng, shape, jnp.float32) * deviation * factor_of
    return jnp.minimum(jnp.maximum(array, -reach), reach).astype(kind)


def setup_inputs(seed: int = 0) -> dict:
    splits = jax.random.split(jax.random.key(seed), 20)
    decoder_in = bell_draw(splits[0], (N_DP, GROUP_DEC, D), 1.0, 6.0, ((0, 4), (1, 8)))
    encoder_states = bell_draw(splits[1], (N_DP, GROUP_ENC, D), 1.0, 6.0, ((0, 4), (1, 8)))
    encoder_doc = draw_encoder_doc(jax.random.fold_in(splits[19], 71), 0)
    decoder_doc = draw_decoder_doc(jax.random.fold_in(splits[19], 71), 0)
    cotangent = draw_cotangent(jax.random.fold_in(splits[19], 71), 0)
    gain_self = jnp.clip(1.0 + 0.1 * jax.random.normal(splits[5], (D,), jnp.float32), 0.5, 1.5)
    gain_cross = jnp.clip(1.0 + 0.1 * jax.random.normal(splits[6], (D,), jnp.float32), 0.5, 1.5)
    gain_ffn = jnp.clip(1.0 + 0.1 * jax.random.normal(splits[7], (D,), jnp.float32), 0.5, 1.5)
    self_query = bell_draw(splits[8], (D, D), D ** -0.5, 0.21875)
    self_key = bell_draw(splits[9], (D, D), D ** -0.5, 0.21875)
    self_value = bell_draw(splits[10], (D, D), D ** -0.5, 0.21875)
    self_out = bell_draw(splits[11], (D, D), (D // 8) ** -0.5, 0.625)
    bias_table = bell_draw(splits[12], (BUCKETS, HEADS), 1.0, 4.0, (), jnp.float32)
    cross_query = bell_draw(splits[13], (D, D), D ** -0.5, 0.21875)
    cross_key = bell_draw(splits[14], (D, D), D ** -0.5, 0.21875)
    cross_value = bell_draw(splits[15], (D, D), D ** -0.5, 0.21875)
    cross_out = bell_draw(splits[16], (D, D), (D // 16) ** -0.5, 0.875)
    ff_in = bell_draw(splits[17], (D, FF), D ** -0.5, 0.21875)
    ff_out = bell_draw(splits[18], (FF, D), (FF // 2) ** -0.5, 0.15625)
    return {"decoder_in": decoder_in, "encoder_states": encoder_states, "encoder_doc": encoder_doc, "decoder_doc": decoder_doc, "cotangent": cotangent, "gain_self": gain_self, "gain_cross": gain_cross, "gain_ffn": gain_ffn, "self_query": self_query, "self_key": self_key, "self_value": self_value, "self_out": self_out, "bias_table": bias_table, "cross_query": cross_query, "cross_key": cross_key, "cross_value": cross_value, "cross_out": cross_out, "ff_in": ff_in, "ff_out": ff_out}


@jax.custom_vjp
def low(v):
    return lax.optimization_barrier(v.astype(jnp.bfloat16)).astype(jnp.float32)

@jax.custom_vjp
def low_back(v):
    return v

def low_keep(v):
    return (low(v), None)

def low_pass(kept, grad):
    return (grad,)

def back_keep(v):
    return (v, None)

def back_low(kept, grad):
    return (low(grad),)
low.defvjp(low_keep, low_pass)
low_back.defvjp(back_keep, back_low)
epsilon = 1e-06
highest = lax.Precision.HIGHEST
masked_fill = -1e+30

def matmul(left_side, right_side):
    return jnp.dot(left_side, right_side, precision=highest, preferred_element_type=jnp.float32)

def bucket_table(length, buckets, max_reach):
    exact_span = buckets // 2
    places = jnp.arange(length, dtype=jnp.int32)
    distance = jnp.maximum(places[:, None] - places[None, :], 0)
    passed = jnp.zeros_like(distance)
    for threshold_index in range(1, buckets - exact_span):
        threshold = int(math.ceil(exact_span * (max_reach / exact_span) ** (threshold_index / (buckets - exact_span))))
        passed = passed + (distance >= threshold).astype(jnp.int32)
    bucket_of = jnp.where(distance < exact_span, distance, exact_span + passed)
    return (bucket_of[:, :, None] == jnp.arange(buckets, dtype=jnp.int32)[None, None, :]).astype(jnp.float32)

def rms_norm(values, gain_row):
    return values * lax.rsqrt(lax.optimization_barrier(jnp.mean(values * values, axis=-1, keepdims=True)) + epsilon) * gain_row

def self_branch(normed, self_query, self_key, self_value, self_out, bias_table, onehot):
    doc_count = normed.shape[0] // DEC_LEN
    split = (doc_count, DEC_LEN, HEADS, HEAD)
    query_rows = low(low_back(matmul(normed, self_query))).reshape(split)
    key_rows = low(low_back(matmul(normed, self_key))).reshape(split)
    value_rows = low(low_back(matmul(normed, self_value))).reshape(split)
    position_bias = jnp.einsum('qkb,bh->hqk', onehot, bias_table, precision=highest)
    scores = jnp.einsum('dqhe,dkhe->dhqk', query_rows, key_rows, precision=highest) * HEAD ** (-0.5) + position_bias[None]
    scores = low_back(scores)
    places = jnp.arange(DEC_LEN, dtype=jnp.int32)
    causal = places[:, None] >= places[None, :]
    weights = jax.nn.softmax(jnp.where(causal, scores, masked_fill), axis=-1)
    mixed = jnp.einsum('dhqk,dkhe->dqhe', low(weights), value_rows, precision=highest).reshape(normed.shape)
    mixed = low(low_back(mixed))
    return low_back(matmul(mixed, self_out))

def cross_branch(normed, encoded, key_docs, query_docs, cross_query, cross_key, cross_value, cross_out):
    query_count = normed.shape[0]
    block_rows = min(512, query_count)
    blocks = query_count // block_rows
    query_rows = low(low_back(matmul(normed, cross_query))).reshape(blocks, block_rows, HEADS, HEAD)
    doc_rows = jnp.repeat(query_docs, DEC_LEN, total_repeat_length=query_count).reshape(blocks, block_rows)
    key_rows = low(low_back(matmul(encoded, cross_key))).reshape(-1, HEADS, HEAD)
    value_rows = low(low_back(matmul(encoded, cross_value))).reshape(-1, HEADS, HEAD)

    def attend(pieces):
        query_block, doc_block = pieces
        scores = low_back(jnp.einsum('qhe,khe->hqk', query_block, key_rows, precision=highest) * HEAD ** (-0.5))
        same_doc = doc_block[None, :, None] == key_docs[None, None, :]
        weights = jax.nn.softmax(jnp.where(same_doc, scores, masked_fill), axis=-1)
        return jnp.einsum('hqk,khe->qhe', low(weights), value_rows, precision=highest)
    mixed = lax.map(jax.checkpoint(attend), (query_rows, doc_rows)).reshape(query_count, HEADS * HEAD)
    mixed = low(low_back(mixed))
    return low_back(matmul(mixed, cross_out))

def feed_forward(normed, ff_in, ff_out):
    hidden = low_back(matmul(normed, ff_in))
    return low_back(matmul(low(jax.nn.gelu(hidden)), ff_out))

def layer(encoder_doc, decoder_doc, onehot, decoder_in, encoder_states, gain_self, gain_cross, gain_ffn, self_query, self_key, self_value, self_out, bias_table, cross_query, cross_key, cross_value, cross_out, ff_in, ff_out):
    results = []
    for group in range(N_DP):
        hidden_in = decoder_in[group]
        after_self = hidden_in + self_branch(low(rms_norm(hidden_in, gain_self)), self_query, self_key, self_value, self_out, bias_table, onehot)
        after_cross = after_self + cross_branch(low(rms_norm(after_self, gain_cross)), encoder_states[group], encoder_doc[group], decoder_doc[group], cross_query, cross_key, cross_value, cross_out)
        results.append(after_cross + feed_forward(low(rms_norm(after_cross, gain_ffn)), ff_in, ff_out))
    return jnp.stack(results)

def reference(decoder_in, encoder_states, encoder_doc, decoder_doc, cotangent, gain_self, gain_cross, gain_ffn, self_query, self_key, self_value, self_out, bias_table, cross_query, cross_key, cross_value, cross_out, ff_in, ff_out):
    onehot = bucket_table(DEC_LEN, BUCKETS, MAX_REACH)
    floats = (decoder_in.astype(jnp.float32), encoder_states.astype(jnp.float32), gain_self.astype(jnp.float32), gain_cross.astype(jnp.float32), gain_ffn.astype(jnp.float32), self_query.astype(jnp.float32), self_key.astype(jnp.float32), self_value.astype(jnp.float32), self_out.astype(jnp.float32), bias_table.astype(jnp.float32), cross_query.astype(jnp.float32), cross_key.astype(jnp.float32), cross_value.astype(jnp.float32), cross_out.astype(jnp.float32), ff_in.astype(jnp.float32), ff_out.astype(jnp.float32))
    output, pullback = jax.vjp(partial(layer, encoder_doc, decoder_doc, onehot), *floats)
    grads = pullback(cotangent.astype(jnp.float32))
    return (output.astype(jnp.bfloat16), grads[0], grads[1], grads[2], grads[3], grads[4], grads[5], grads[6], grads[7], grads[8], grads[9], grads[10], grads[11], grads[12], grads[13], grads[14], grads[15])
```

```python
import functools
import itertools
import math

import jax
import jax.numpy as jnp
import numpy as np
from jax import lax
from jax.experimental import pallas as pl
from jax.experimental.pallas import tpu as pltpu
from jax.sharding import PartitionSpec as P

MAX_REACH = 128
DEC_LEN = 128


epsilon = 1e-06
masked_fill = -1e30
half = jnp.bfloat16
full = jnp.float32


def bucket_map(length, buckets, max_reach):
    exact_span = buckets // 2
    places = np.arange(length)
    distance = places[None, :] - places[:, None]
    passed = np.zeros_like(distance)
    for threshold_index in range(1, buckets - exact_span):
        threshold = int(
            math.ceil(
                exact_span * (max_reach / exact_span) ** (threshold_index / (buckets - exact_span))
            )
        )
        passed = passed + (distance >= threshold)
    bucket_of = np.where(distance < exact_span, distance, exact_span + passed)
    return np.where(distance < 0, -1, bucket_of).astype(np.int32)


def norm_parts(values):
    inverse = lax.rsqrt(jnp.mean(values * values, axis=-1, keepdims=True) + epsilon)
    return values * inverse, inverse


def norm_backward(upstream, normal, inverse, gain_row):
    scaled = upstream * gain_row
    inner = jnp.mean(scaled * normal, axis=-1, keepdims=True)
    return inverse * (scaled - normal * inner), jnp.sum(upstream * normal, axis=0, keepdims=True)


NT = (((1,), (1,)), ((), ()))
NN = (((1,), (0,)), ((), ()))
TN = (((0,), (0,)), ((), ()))
LANES = 128
ONES = 8
MEGA = 2**20
CROSS_ROWS = 2048


def dot(left_side, right_side, dims):
    return lax.dot_general(left_side, right_side, dims, preferred_element_type=full)


def three(value):
    first = value.astype(half).astype(full)
    second = (value - first).astype(half).astype(full)
    return first, second, (value - first - second).astype(half).astype(full)


def placed_three(value, index, rest):
    first, second, third = three(value)
    return jnp.where(
        index == ONES, first, jnp.where(index == ONES + 1, second, jnp.where(index == ONES + 2, third, rest))
    )


def low_lanes(rows):
    return lax.broadcasted_iota(jnp.int32, (rows, LANES), 1) < LANES // 2


def stacked(value, low):
    zero = jnp.zeros_like(value)
    return jnp.concatenate([jnp.where(low, value, zero), jnp.where(low, zero, value)], axis=0)


def loop(count, step, start):
    return lax.fori_loop(0, count, step, start, unroll=count <= 4)


light = pl.CostEstimate(flops=1, bytes_accessed=1, transcendentals=0)


def params(megabytes=56):
    return pltpu.CompilerParams(vmem_limit_bytes=megabytes * MEGA)


def whole(shape):
    return pl.BlockSpec(shape, lambda *_: (0,) * len(shape))


anywhere = pl.BlockSpec(memory_space=pl.ANY)


class Blocks:
    def __init__(self, at):
        self.core, self.ny, self.nx, self.dp, self.seq = at.core, at.ny, at.nx, at.dp, at.seq
        self.high, self.low = at.high, at.low

    def shape(self, rows, columns):
        return (self.ny, self.nx, self.high, self.low, rows, columns)

    def row_place(self, block, place):
        z = lax.div(block, self.nx)
        return (
            lax.rem(lax.rem(block, self.nx) - place[2] + self.nx, self.nx),
            lax.rem(lax.div(z, self.low) - place[3] + self.high, self.high),
            lax.rem(lax.rem(z, self.low) - place[4] + self.low, self.low),
        )

    def column_place(self, y, place):
        return lax.rem(y - place[0] + self.ny, self.ny)

    def paired(self, first, second, place):
        n = first.shape[1] // self.core
        if self.core == 1:
            return jnp.concatenate([first, second], axis=1).astype(half), None
        mine = place[1] == 0
        if n % LANES != LANES // 2:
            cut = [jnp.concatenate([g[:, c * n : (c + 1) * n] for g in (first, second)], axis=1) for c in range(2)]
        else:
            main = n - LANES // 2
            low = lax.broadcasted_iota(jnp.int32, (first.shape[0], LANES), 1) < LANES // 2
            one, two = (g[:, main : main + LANES] for g in (first, second))
            sides = (
                jnp.where(low, one, pltpu.roll(two, LANES // 2, 1)),
                jnp.where(low, pltpu.roll(one, LANES // 2, 1), two),
            )
            cut = [
                jnp.concatenate([first[:, at : at + main], second[:, at : at + main], sides[c]], axis=1)
                for c, at in enumerate((0, main + LANES))
            ]
        return jnp.where(mine, cut[0], cut[1]).astype(half), jnp.where(mine, cut[1], cut[0]).astype(half)

    def put(self, first, second, place, keep, send, offset):
        m, wide = first.shape[0] // self.seq, first.shape[1] // self.ny
        n = 2 * wide // self.core
        for y in range(self.ny):
            at = slice(y * wide, (y + 1) * wide)
            ours, theirs = self.paired(first[:, at], second[:, at], place)
            to_y = self.column_place(jnp.int32(y), place)
            for block in range(self.seq):
                to_x, to_h, to_l = self.row_place(jnp.int32(block), place)
                rows = slice(block * m, (block + 1) * m)
                keep[to_y, to_x, to_h, to_l, :, offset : offset + n] = ours[rows]
                if theirs is not None:
                    send[to_y, to_x, to_h, to_l, :, offset : offset + n] = theirs[rows]


def unpaired(at, piece):
    n = piece.shape[1] // 2
    if at.core == 1 or n % LANES != LANES // 2:
        return piece[:, :n], piece[:, n:]
    main = n - LANES // 2
    side = piece[:, 2 * main :]
    out = []
    for k in range(2):
        big, small = piece[:, k * main : (k + 1) * main], side[:, k * LANES // 2 : (k + 1) * LANES // 2]
        out.append(
            jnp.where(at.c == 0, jnp.concatenate([big, small], axis=1), jnp.concatenate([small, big], axis=1))
        )
    return out


def position_bias(buckets, table, pair):
    out = []
    for head in range(2):
        bias = jnp.full(buckets.shape, masked_fill, full)
        for b in range(table.shape[0]):
            bias = jnp.where(buckets == b, table[b, 2 * pair + head], bias)
        out.append(bias)
    return jnp.concatenate(out, axis=1)


def self_forward_kernel(
    hidden, gain_one, gain_two, weights_q, weights_k, weights_v, weights_o, weights_c, buckets, table,
    query, key, value, mixed, after, normed_two, query_cross, normed, every, *, scale,
):
    step = pl.program_id(0)
    rows = hidden.shape[0]

    @pl.when(step == 0)
    def _():
        normal, _ = norm_parts(hidden[...].astype(full))
        normed[...] = (normal * gain_one[...]).astype(half)

    weights = jnp.concatenate([weights_q[...], weights_k[...], weights_v[...]], axis=1)
    made = dot(normed[...], weights, NN).astype(half)
    query[...] = made[:, :LANES] * scale
    key[...] = made[:, LANES : 2 * LANES]
    value[...] = made[:, 2 * LANES :]
    low = low_lanes(DEC_LEN)
    bias = position_bias(buckets[...], table, step)
    for first in range(0, rows, DEC_LEN):
        at = pl.ds(first, DEC_LEN)
        scores = dot(key[at, :], stacked(query[at, :], low), NT) + bias
        expo = jnp.exp(scores - jnp.max(scores, axis=0, keepdims=True))
        expo = (expo / jnp.sum(expo, axis=0, keepdims=True)).astype(half)
        both = dot(value[at, :], expo, TN).T
        one = jnp.where(low, both[:DEC_LEN], both[DEC_LEN:]).astype(half)
        mixed[at, :] = one
        every[at, pl.ds(pl.multiple_of(step * LANES, LANES), LANES)] = one

    @pl.when(step == pl.num_programs(0) - 1)
    def _():
        total = hidden[...].astype(full) + dot(every[...], weights_o[...], NN)
        after[...] = total
        normal, _ = norm_parts(total)
        again = (normal * gain_two[...]).astype(half)
        normed_two[...] = again
        query_cross[...] = dot(again, weights_c[...], NN).astype(half)


def self_forward(hidden, gain_one, gain_two, weights_q, weights_k, weights_v, weights_o, weights_c, buckets, table, scale):
    rows, width = hidden.shape
    pairs = width // LANES
    column = lambda i: (0, i)
    row_block = pl.BlockSpec((rows, LANES), column)
    weight_block = pl.BlockSpec((width, LANES), column)
    return pl.pallas_call(
        functools.partial(self_forward_kernel, scale=scale),
        name="self_forward",
        grid=(pairs,),
        in_specs=[whole((rows, width)), whole((1, width)), whole((1, width))]
        + [weight_block] * 3
        + [whole((width, width))] * 2
        + [whole((DEC_LEN, DEC_LEN)), pl.BlockSpec(memory_space=pltpu.SMEM)],
        out_specs=[row_block] * 4 + [whole((rows, width))] * 3,
        out_shape=[jax.ShapeDtypeStruct((rows, width), half)] * 4
        + [jax.ShapeDtypeStruct((rows, width), kind) for kind in (full, half, half)],
        scratch_shapes=[pltpu.VMEM((rows, width), half)] * 2,
        compiler_params=params(),
        cost_estimate=light,
    )(hidden, gain_one, gain_two, weights_q, weights_k, weights_v, weights_o, weights_c, buckets, table)


def key_value_kernel(*refs, rows, doc_count):
    shards, (own, weights_k, weights_v, keys, values, mask, states) = refs[:-7], refs[-7:]
    for i, shard in enumerate(shards):
        at = pl.ds(i * rows, rows)
        states[at, :] = shard[:rows, :]
        keys[at, :] = dot(shard[:rows, :], weights_k[...], NN).astype(half)
        values[at, :] = dot(shard[:rows, :], weights_v[...], NN).astype(half)
        docs = shard[rows : rows + 1, :rows].astype(full)
        lane = lax.broadcasted_iota(jnp.int32, (LANES, rows), 0)
        ones = ((lane >= ONES) & (lane < ONES + 3)).astype(full)
        extra = jnp.where(lane < doc_count, jnp.where(docs == own[:, :1], 0.0, masked_fill), ones)
        mask[at, :] = extra.T.astype(half)


def key_value(shards, own, weights_k, weights_v, rows, doc_count):
    width = shards[0].shape[1]
    count = len(shards) * rows
    return pl.pallas_call(
        functools.partial(key_value_kernel, rows=rows, doc_count=doc_count),
        name="key_value",
        out_shape=[jax.ShapeDtypeStruct((count, size), half) for size in (width, width, LANES, width)],
        compiler_params=params(),
        cost_estimate=light,
    )(*shards, own, weights_k, weights_v)


def cross_forward_kernel(*refs, scale, block, opens, closes):
    query, mark, keys, values, mask = refs[:5]
    refs = refs[5:]
    if not opens:
        state_in, refs = refs[:2], refs[2:]
    if closes:
        (mixed, mixed_half, extended), refs = refs[:3], refs[3:]
    else:
        state_out, refs = refs[:2], refs[2:]
    total, wide = refs
    rows = query.shape[0]
    low = low_lanes(rows)
    wide[:, :LANES] = stacked(query[...] * scale, low)
    wide[:rows, LANES:] = mark[...]
    wide[rows:, LANES:] = mark[...]
    if opens:
        total[...] = jnp.zeros_like(total)
        carry = (jnp.full((1, 2 * rows), masked_fill, full), jnp.zeros((1, 2 * rows), full))
    else:
        total[...] = state_in[0][0]
        carry = (state_in[1][0, 0:1], state_in[1][0, 1:2])

    def step(i, carry):
        peak, amount = carry
        at = pl.ds(pl.multiple_of(i * block, block), block)
        scores = dot(jnp.concatenate([keys[at, :], mask[at, :]], axis=1), wide[...], NT)
        fresh = jnp.maximum(peak, jnp.max(scores, axis=0, keepdims=True))
        expo = jnp.exp(scores - fresh)
        fade = jnp.exp(peak - fresh)
        total[...] = total[...] * fade + dot(values[at, :], expo.astype(half), TN)
        return fresh, amount * fade + jnp.sum(expo, axis=0, keepdims=True)

    peak, amount = loop(keys.shape[0] // block, step, carry)
    if not closes:
        state_out[0][0] = total[...]
        state_out[1][0, 0:1] = peak
        state_out[1][0, 1:2] = amount
        return
    both = (total[...] / amount).T
    one = jnp.where(low, both[:rows], both[rows:])
    mixed[...] = one
    mixed_half[...] = one.astype(half)
    index = lax.broadcasted_iota(jnp.int32, (LANES, 2 * rows), 0)
    extra = placed_three(-(peak + jnp.log(amount)), index, 0.0).T
    extended[0, :, :LANES] = wide[:, :LANES]
    extended[0, :, LANES:] = (wide[:, LANES:].astype(full) + extra).astype(half)


def cross_forward(query, mark, source, state, closes, scale):
    rows, pairs = query.shape[0], query.shape[1] // LANES
    count = source[0].shape[0]
    column = lambda i: (0, i)
    plane = lambda i: (i, 0, 0)
    block = min(1024, count)
    state_specs = [pl.BlockSpec((1, LANES, 2 * rows), plane), pl.BlockSpec((1, 2, 2 * rows), plane)]
    state_shape = [
        jax.ShapeDtypeStruct((pairs, LANES, 2 * rows), full),
        jax.ShapeDtypeStruct((pairs, 2, 2 * rows), full),
    ]
    last_specs = [pl.BlockSpec((rows, LANES), column)] * 2 + [pl.BlockSpec((1, 2 * rows, 2 * LANES), plane)]
    last_shape = [
        jax.ShapeDtypeStruct(query.shape, full),
        jax.ShapeDtypeStruct(query.shape, half),
        jax.ShapeDtypeStruct((pairs, 2 * rows, 2 * LANES), half),
    ]
    return pl.pallas_call(
        functools.partial(cross_forward_kernel, scale=scale, block=block, opens=not state, closes=closes),
        name="cross_forward",
        grid=(pairs,),
        in_specs=[pl.BlockSpec((rows, LANES), column), whole((rows, LANES))]
        + [pl.BlockSpec((count, LANES), column), pl.BlockSpec((count, LANES), column), whole((count, LANES))]
        + (state_specs if state else []),
        out_specs=last_specs if closes else state_specs,
        out_shape=last_shape if closes else state_shape,
        scratch_shapes=[
            pltpu.VMEM((LANES, 2 * rows), full),
            pltpu.VMEM((2 * rows, 2 * LANES), half),
        ],
        compiler_params=params(),
        cost_estimate=light,
    )(query, mark, *source, *state)


def cross_backward_kernel(*refs, scale, block, parts):
    extended, upstream, mixed = refs[:3]
    sources = [refs[3 + 3 * i : 6 + 3 * i] for i in range(parts)]
    query_grad = refs[3 + 3 * parts]
    grads = [refs[4 + 3 * parts + 2 * i : 6 + 3 * parts + 2 * i] for i in range(parts)]
    wide, total = refs[-2:]
    rows = upstream.shape[0]
    low = low_lanes(rows)
    lane = lax.broadcasted_iota(jnp.int32, (rows, LANES), 1)
    each = upstream[...].astype(full) * mixed[...]
    wide[:, :LANES] = stacked(upstream[...], low)
    for head in range(2):
        inner = jnp.sum(jnp.where(low == (head == 0), each, 0.0), axis=1, keepdims=True)
        wide[head * rows : (head + 1) * rows, LANES:] = placed_three(-inner, lane, 0.0).astype(half)
    total[...] = jnp.zeros_like(total)
    for (keys, values, mask), (key_grad, value_grad) in zip(sources, grads):

        def step(i, carry):
            at = pl.ds(pl.multiple_of(i * block, block), block)
            extra = mask[at, :]
            expo = jnp.exp(dot(jnp.concatenate([keys[at, :], extra], axis=1), extended[0], NT))
            change = dot(jnp.concatenate([values[at, :], extra], axis=1), wide[...], NT)
            score = (expo * change).astype(half)
            value_grad[at, :] = dot(expo.astype(half), wide[:, :LANES], NN).astype(half)
            key_grad[at, :] = dot(score, extended[0, :, :LANES], NN).astype(half)
            total[...] += dot(keys[at, :], score, TN)
            return carry

        loop(keys.shape[0] // block, step, 0)
    both = total[...].T
    query_grad[...] = (jnp.where(low, both[:rows], both[rows:]) * scale).astype(half)


def cross_backward(mark, extended, upstream, mixed, sources, first, pairs, scale):
    rows, width = upstream.shape[0], pairs * LANES
    count = sources[0][0].shape[0]
    column = lambda i: (0, i)
    later = lambda i: (0, i + first)
    block = min(1024, count)
    every = count * len(sources)
    key_block, later_block = pl.BlockSpec((count, LANES), column), pl.BlockSpec((count, LANES), later)
    return pl.pallas_call(
        marked(functools.partial(cross_backward_kernel, scale=scale, block=block, parts=len(sources))),
        name="cross_backward",
        grid=(pairs,),
        in_specs=[
            anywhere,
            pl.BlockSpec((1, 2 * rows, 2 * LANES), lambda i: (i + first, 0, 0)),
            pl.BlockSpec((rows, LANES), later),
            pl.BlockSpec((rows, LANES), later),
        ]
        + [later_block, later_block, whole((count, LANES))] * len(sources),
        out_specs=[pl.BlockSpec((rows, LANES), column)] + [key_block] * (2 * len(sources)),
        out_shape=[jax.ShapeDtypeStruct((rows, width), half)]
        + [jax.ShapeDtypeStruct((count, width), half)] * (2 * len(sources)),
        scratch_shapes=[
            pltpu.VMEM((2 * rows, 2 * LANES), half),
            pltpu.VMEM((LANES, 2 * rows), full),
        ],
        compiler_params=params(),
        cost_estimate=light,
    )(mark, extended, upstream, mixed, *[array for source in sources for array in source])


def feed_forward_kernel(
    place, after, mixed, weights_o, gain, weights_in, weights_out, cotangent,
    after_cross, activated, resid, branch, mixed_grad, gain_grad, in_keep, in_send, out_keep, out_send,
    normed, total, *, blocks,
):
    step = pl.program_id(0)

    @pl.when(step == 0)
    def _():
        values = after[...] + dot(mixed[...], weights_o[...], NN)
        after_cross[...] = values
        normal, _ = norm_parts(values)
        normed[...] = (normal * gain[...]).astype(half)
        total[...] = jnp.zeros_like(total)

    upstream = cotangent[...]
    pre = dot(normed[...], weights_in[...], NN)
    square = pre * pre
    slope = math.sqrt(2.0 / math.pi)
    bend = jnp.tanh(slope * (pre + 0.044715 * (square * pre)))
    act = (0.5 * pre * (1.0 + bend)).astype(half)
    activated[...] = act
    gelu_grad = 0.5 * (1.0 + bend) + 0.5 * pre * (1.0 - bend * bend) * (slope * (1.0 + 3 * 0.044715 * square))
    pre_grad = (dot(upstream, weights_out[...], NT) * gelu_grad).astype(half)
    total[...] += dot(pre_grad, weights_in[...], NT)

    grad = dot(normed[...], pre_grad, TN).astype(half)
    m = grad.shape[0] // blocks.seq
    to_y = blocks.column_place(lax.div(step, blocks.core), place)
    ours = lax.rem(step, blocks.core) == place[1]

    def fill(target):
        for block in range(blocks.seq):
            to_x, to_h, to_l = blocks.row_place(jnp.int32(block), place)
            target[to_y, to_x, to_h, to_l] = grad[block * m : (block + 1) * m]

    pl.when(ours)(lambda: fill(in_keep))
    pl.when(jnp.logical_not(ours))(lambda: fill(in_send))

    grad = dot(act, upstream, TN)
    wide = grad.shape[1] // blocks.ny
    n = wide // blocks.core
    pieces = out_keep.shape[5] // n
    many = pieces * m
    for y in range(blocks.ny):
        at = slice(y * wide, (y + 1) * wide)
        to_y = blocks.column_place(jnp.int32(y), place)
        for block in range(grad.shape[0] // many):
            to_x, to_h, to_l = blocks.row_place(step * (grad.shape[0] // many) + block, place)
            for piece in range(0, pieces, 2):
                first = block * many + piece * m
                kept, sent = blocks.paired(grad[first : first + m, at], grad[first + m : first + 2 * m, at], place)
                out_keep[to_y, to_x, to_h, to_l, :, piece * n : (piece + 2) * n] = kept
                if sent is not None:
                    out_send[to_y, to_x, to_h, to_l, :, piece * n : (piece + 2) * n] = sent

    @pl.when(step == pl.num_programs(0) - 1)
    def _():
        normal, inverse = norm_parts(after_cross[...])
        change, gain_sum = norm_backward(total[...], normal, inverse, gain[...])
        gain_grad[...] = gain_sum
        change = change + upstream.astype(full)
        resid[...] = change
        rounded = change.astype(half)
        branch[...] = rounded
        mixed_grad[...] = dot(rounded, weights_o[...], NT).astype(half)


def feed_forward(at, after, mixed, weights_o, gain, weights_in, weights_out, cotangent):
    rows, width = after.shape
    depth = weights_in.shape[1]
    blocks = Blocks(at)
    cut = depth // at.dp
    shape = blocks.shape(width // at.seq, cut)
    all_rows = whole((rows, width))
    sized = lambda kind: jax.ShapeDtypeStruct((rows, width), kind)
    return pl.pallas_call(
        functools.partial(feed_forward_kernel, blocks=blocks),
        name="feed_forward",
        grid_spec=pltpu.PrefetchScalarGridSpec(
            num_scalar_prefetch=1,
            grid=(at.dp,),
            in_specs=[
                all_rows,
                all_rows,
                whole((width, width)),
                whole((1, width)),
                pl.BlockSpec((width, cut), lambda i, _: (0, i)),
                pl.BlockSpec((cut, width), lambda i, _: (i, 0)),
                all_rows,
            ],
            out_specs=[all_rows, pl.BlockSpec((rows, cut), lambda i, _: (0, i))]
            + [all_rows] * 3
            + [whole((1, width))]
            + [whole(shape)] * 4,
            scratch_shapes=[pltpu.VMEM((rows, width), half), pltpu.VMEM((rows, width), full)],
        ),
        out_shape=[sized(full), jax.ShapeDtypeStruct((rows, depth), half), sized(full), sized(half), sized(half)]
        + [jax.ShapeDtypeStruct((1, width), full)]
        + [jax.ShapeDtypeStruct(shape, half)] * 4,
        compiler_params=params(),
        cost_estimate=light,
    )(at.place, after, mixed, weights_o, gain, weights_in, weights_out, cotangent)


def encoder_part_kernel(*refs, pieces, early_steps):
    weights_k, weights_v, early, late = refs[2 * pieces :]
    total, first = None, 0
    for i in range(pieces):
        wide = refs[2 * i].shape[1]
        for grad, weights in ((refs[2 * i], weights_k), (refs[2 * i + 1], weights_v)):
            term = dot(grad[...], weights[:, first : first + wide], NT)
            total = term if total is None else total + term
        first += wide
    is_early = pl.program_id(0) < early_steps

    @pl.when(is_early)
    def _():
        early[...] = total.astype(half)

    @pl.when(jnp.logical_not(is_early))
    def _():
        late[...] = total.astype(half)


def encoder_part(mark, at, grads, weights_k, weights_v):
    width = weights_k.shape[0]
    rows = grads[0].shape[0] // at.nz
    early = at.high * (at.low - 1)
    plane = lambda size: jax.ShapeDtypeStruct((size, rows, width), half)
    return pl.pallas_call(
        marked(functools.partial(encoder_part_kernel, pieces=len(grads) // 2, early_steps=early)),
        name="encoder_part",
        grid=(at.nz,),
        in_specs=[anywhere]
        + [
            pl.BlockSpec((rows, grad.shape[1]), lambda i: (i % at.high * at.low + at.low - 1 - i // at.high, 0))
            for grad in grads
        ]
        + [whole((width, width))] * 2,
        out_specs=[
            pl.BlockSpec((None, rows, width), lambda i: (jnp.minimum(i, early - 1), 0, 0)),
            pl.BlockSpec((None, rows, width), lambda i: (jnp.maximum(i - early, 0), 0, 0)),
        ],
        out_shape=[plane(early), plane(at.high)],
        compiler_params=params(),
        cost_estimate=light,
    )(mark, *grads, weights_k, weights_v)


def cross_weights_kernel(place, *refs, blocks, parts, pieces, steps):
    query_grads, refs = refs[:pieces], refs[pieces:]
    normed, mixed, branch = refs[:3]
    states, grads = refs[3 : 3 + parts], refs[3 + parts : -3]
    keep, send, total = refs[-3:]
    n = keep.shape[5] // 4
    step = pl.program_id(0)

    @pl.when(step == 0)
    def _():
        made = [dot(normed[...], grad[...], TN) for grad in query_grads]
        blocks.put(jnp.concatenate(made, axis=1), dot(mixed[...], branch[...], TN), place, keep, send, 0)

    made = []
    for kind in range(2):
        shares = []
        for piece in range(pieces):
            terms = [dot(states[k][...], grads[2 * (piece * parts + k) + kind][...], TN) for k in range(parts)]
            shares.append(sum(terms[1:], terms[0]))
        made.append(jnp.concatenate(shares, axis=1))
    if steps == 1:
        blocks.put(made[0], made[1], place, keep, send, 2 * n)
        return

    @pl.when(step == 0)
    def _():
        total[0], total[1] = made

    @pl.when(step > 0)
    def _():
        total[0] += made[0]
        total[1] += made[1]

    @pl.when(step == steps - 1)
    def _():
        blocks.put(total[0], total[1], place, keep, send, 2 * n)


def cross_weights(mark, at, query_grads, normed, mixed, branch, states, grads):
    rows, width = normed.shape
    blocks = Blocks(at)
    shape = blocks.shape(width // at.seq, 4 * width // at.dp)
    count = states[0].shape[0]
    block = min(count, CROSS_ROWS // len(states))
    plain = [*query_grads, normed, mixed, branch]
    cut = [*states, *grads]
    return pl.pallas_call(
        marked(
            functools.partial(
                cross_weights_kernel, blocks=blocks, parts=len(states), pieces=len(query_grads), steps=count // block
            ),
            1,
        ),
        name="cross_weights",
        grid_spec=pltpu.PrefetchScalarGridSpec(
            num_scalar_prefetch=1,
            grid=(count // block,),
            in_specs=[anywhere]
            + [whole(array.shape) for array in plain]
            + [pl.BlockSpec((block, array.shape[1]), lambda i, _: (i, 0)) for array in cut],
            out_specs=[whole(shape)] * 2,
            scratch_shapes=[pltpu.VMEM((2, width, width), full)],
        ),
        out_shape=[jax.ShapeDtypeStruct(shape, half)] * 2,
        compiler_params=params(),
        cost_estimate=light,
    )(at.place, mark, *plain, *cut)


def self_backward_kernel(
    place, query_grad_one, query_grad_two, weights_c, after, gain_two, resid_in, hidden, gain_one, gain_ffn_grad,
    query, key, value, mixed, weights_ob, weights_q, weights_k, weights_v, buckets, table,
    input_grad, first_keep, first_send, second_keep, second_send,
    resid, branch, grads, bias_rows, gain_two_grad, extra, *, scale, blocks,
):
    step = pl.program_id(0)
    rows, width = hidden.shape

    @pl.when(step == 0)
    def _():
        normal, inverse = norm_parts(after[...])
        cut = query_grad_one.shape[1]
        up = dot(query_grad_one[...], weights_c[:, :cut], NT) + dot(query_grad_two[...], weights_c[:, cut:], NT)
        change, gain_sum = norm_backward(up, normal, inverse, gain_two[...])
        gain_two_grad[...] = gain_sum
        change = change + resid_in[...]
        resid[...] = change
        branch[...] = change.astype(half)

    low = low_lanes(DEC_LEN)
    upstream = dot(branch[...], weights_ob[...], NT).astype(half)
    summed = None
    bias = position_bias(buckets[...], table, step)
    for first in range(0, rows, DEC_LEN):
        at = pl.ds(first, DEC_LEN)
        wide = stacked(query[at, :], low)
        grad = stacked(upstream[first : first + DEC_LEN], low)
        scores = dot(key[at, :], wide, NT) + bias
        expo = jnp.exp(scores - jnp.max(scores, axis=0, keepdims=True))
        expo = expo / jnp.sum(expo, axis=0, keepdims=True)
        change = dot(value[at, :], grad, NT)
        rounded = (expo * (change - jnp.sum(expo * change, axis=0, keepdims=True))).astype(half)
        both = dot(key[at, :], rounded, TN).T
        made = (
            jnp.where(low, both[:DEC_LEN], both[DEC_LEN:]) * scale,
            dot(rounded, wide, NN),
            dot(expo.astype(half), grad, NN),
        )
        for kind in range(3):
            grads[kind, at, pl.ds(pl.multiple_of(step * LANES, LANES), LANES)] = made[kind].astype(half)
        summed = rounded.astype(full) if summed is None else summed + rounded.astype(full)
    count = bias_rows.shape[1]
    of_pair = jnp.concatenate([buckets[...], buckets[...]], axis=1)
    sums = [jnp.sum(jnp.where(of_pair == b, summed, 0.0), axis=0, keepdims=True) for b in range(count)]
    bias_rows[step] = jnp.concatenate(sums, axis=0)

    @pl.when(step == pl.num_programs(0) - 1)
    def _():
        normal, inverse = norm_parts(hidden[...].astype(full))
        normed = (normal * gain_one[...]).astype(half)
        up = (
            dot(grads[0], weights_q[...], NT)
            + dot(grads[1], weights_k[...], NT)
            + dot(grads[2], weights_v[...], NT)
        )
        change, gain_sum = norm_backward(up, normal, inverse, gain_one[...])
        input_grad[...] = resid[...] + change
        n = first_keep.shape[5] // 2
        blocks.put(dot(normed, grads[0], TN), dot(normed, grads[1], TN), place, first_keep, first_send, 0)
        blocks.put(dot(normed, grads[2], TN), dot(mixed[...], branch[...], TN), place, second_keep, second_send, 0)

        index = lax.broadcasted_iota(jnp.int32, (LANES, width), 0)
        gains = jnp.where(
            index == 0,
            gain_sum,
            jnp.where(index == 1, gain_two_grad[...], jnp.where(index == 2, gain_ffn_grad[...], 0.0)),
        )
        extra[...] = gains.T
        lane = lax.broadcasted_iota(jnp.int32, (count, LANES), 1)
        table = jnp.zeros((count, LANES), full)
        for pair in range(bias_rows.shape[0]):
            for head in range(2):
                part = bias_rows[pair, :, head * LANES : (head + 1) * LANES]
                table = jnp.where(lane == 16 + 2 * pair + head, jnp.sum(part, axis=1, keepdims=True), table)
        m = width // blocks.seq
        each = count // blocks.seq
        for block in range(blocks.seq):
            at = slice(block * m, block * m + each)
            extra[at, :] = extra[at, :] + table[block * each : (block + 1) * each]
        for block in range(blocks.seq):
            to_x, to_h, to_l = blocks.row_place(jnp.int32(block), place)
            piece = extra[block * m : (block + 1) * m, :].astype(half)
            for y in range(blocks.ny):
                second_keep[y, to_x, to_h, to_l, :, 2 * n :] = piece
                second_send[y, to_x, to_h, to_l, :, 2 * n :] = piece


def self_backward(
    mark, at, query_grads, weights_c, after, gain_two, resid, hidden, gain_one, gain_ffn_grad,
    query, key, value, mixed, weights_o, weights_q, weights_k, weights_v, buckets, table, scale,
):
    rows, width = hidden.shape
    pairs = width // LANES
    blocks = Blocks(at)
    n, count = width // at.dp, table.shape[0]
    first = blocks.shape(width // at.seq, 2 * n)
    second = blocks.shape(width // at.seq, 2 * n + LANES)
    row_block = pl.BlockSpec((rows, LANES), lambda i, _: (0, i))
    all_rows, square, line = whole((rows, width)), whole((width, width)), whole((1, width))
    return pl.pallas_call(
        marked(functools.partial(self_backward_kernel, scale=scale, blocks=blocks), 1),
        name="self_backward",
        grid_spec=pltpu.PrefetchScalarGridSpec(
            num_scalar_prefetch=1,
            grid=(pairs,),
            in_specs=[anywhere]
            + [whole(grad.shape) for grad in query_grads]
            + [square, all_rows, line, all_rows, all_rows, line, line]
            + [row_block] * 3
            + [all_rows, pl.BlockSpec((LANES, width), lambda i, _: (i, 0))]
            + [square] * 3
            + [whole((DEC_LEN, DEC_LEN)), pl.BlockSpec(memory_space=pltpu.SMEM)],
            out_specs=[all_rows, whole(first), whole(first), whole(second), whole(second)],
            scratch_shapes=[
                pltpu.VMEM((rows, width), full),
                pltpu.VMEM((rows, width), half),
                pltpu.VMEM((3, rows, width), half),
                pltpu.VMEM((pairs, count, 2 * DEC_LEN), full),
                pltpu.VMEM((1, width), full),
                pltpu.VMEM((width, LANES), full),
            ],
        ),
        out_shape=[jax.ShapeDtypeStruct((rows, width), full)]
        + [jax.ShapeDtypeStruct(shape, half) for shape in (first, first, second, second)],
        compiler_params=params(),
        cost_estimate=light,
    )(
        at.place, mark, *query_grads, weights_c, after, gain_two, resid, hidden, gain_one, gain_ffn_grad,
        query, key, value, mixed, weights_o, weights_q, weights_k, weights_v, buckets, table,
    )


class Places:
    def __init__(self, dp_size, seq_size):
        self.dp, self.seq = dp_size, seq_size
        self.core = 2 if dp_size % 2 == 0 else 1
        self.ny = dp_size // self.core
        self.nx = self.ny if seq_size % self.ny == 0 else 1
        self.nz = seq_size // self.nx
        self.low = 2 if self.nz % 2 == 0 else 1
        self.high = self.nz // self.low
        dp_index, seq_index = lax.axis_index("dp"), lax.axis_index("seq")
        self.c, self.y = dp_index % self.core, dp_index // self.core
        self.x, self.z = seq_index % self.nx, seq_index // self.nx
        self.place = jnp.stack([self.y, self.c, self.x, self.z // self.low, self.z % self.low]).astype(jnp.int32)

    def shift(self, value, **steps):
        sizes = {"y": self.ny, "c": self.core, "h": self.high, "l": self.low, "x": self.nx}
        flat = lambda p: ((p["y"] * self.core + p["c"]) * self.seq) + (p["h"] * self.low + p["l"]) * self.nx + p["x"]
        pairs = []
        for numbers in itertools.product(*[range(size) for size in sizes.values()]):
            here = dict(zip(sizes, numbers))
            there = {axis: (here[axis] + steps.get(axis, 0)) % size for axis, size in sizes.items()}
            pairs.append((flat(here), flat(there)))
        return lax.ppermute(value, ("dp", "seq"), pairs)


def gate_kernel(*refs):
    refs[-1][...] = jnp.zeros_like(refs[-1])


def gate(*waits):
    arrays = jax.tree.leaves(waits)
    return pl.pallas_call(
        gate_kernel,
        name="gate",
        in_specs=[pl.BlockSpec(memory_space=pl.ANY)] * len(arrays),
        out_shape=jax.ShapeDtypeStruct((8, LANES), full),
        cost_estimate=pl.CostEstimate(flops=10**13, bytes_accessed=10**10, transcendentals=0),
    )(*arrays)


def marked(kernel, scalars=0):
    return lambda *refs: kernel(*refs[:scalars], *refs[scalars + 1 :])


class Term:
    def __init__(self, array, axes, fixed=(), columns=None):
        self.array, self.axes, self.fixed = array, axes, dict(fixed)
        self.columns = columns or (0, array.shape[-1])

    def at(self, axis, place):
        return Term(self.array, self.axes, {**self.fixed, axis: place}, self.columns)

    def free(self):
        sizes = zip(self.axes, self.array.shape)
        return tuple(size for axis, size in sizes if axis not in self.fixed)

    def spec(self):
        shape = [None if axis in self.fixed else size for axis, size in zip(self.axes, self.array.shape)]
        places = [self.fixed.get(axis, 0) for axis in self.axes]
        return pl.BlockSpec((*shape, *self.array.shape[-2:]), lambda i: (*places, 0, 0))


def totals_kernel(*refs, jobs):
    refs = list(refs)
    sources, outs = refs[: -len(jobs)], refs[-len(jobs) :]
    for groups, out in zip(jobs, outs):
        first = 0
        for columns in groups:
            total = None
            for low, high in columns:
                value = sources.pop(0)[..., low:high].astype(full)
                total = value if total is None else total + value
            out[..., first : first + total.shape[-1]] = total.astype(out.dtype)
            first += total.shape[-1]


def totals(mark, jobs, kind=half):
    terms = [term for groups in jobs for group in groups for term in group]
    shape = lambda groups: (
        *groups[0][0].free(),
        groups[0][0].array.shape[-2],
        sum(group[0].columns[1] - group[0].columns[0] for group in groups),
    )
    return pl.pallas_call(
        marked(
            functools.partial(totals_kernel, jobs=[[[term.columns for term in group] for group in groups] for groups in jobs])
        ),
        name="totals",
        grid=(1,),
        in_specs=[anywhere] + [term.spec() for term in terms],
        out_specs=[whole(shape(groups)) for groups in jobs],
        out_shape=[jax.ShapeDtypeStruct(shape(groups), kind) for groups in jobs],
        compiler_params=params(),
        cost_estimate=light,
    )(mark, *[term.array for term in terms])


class Reduction:
    def __init__(self, at, keep, send, order):
        self.at, self.order = at, order
        self.terms = [Term(keep, "yxhl")]
        if at.core == 2:
            self.terms.append(Term(at.shift(send, c=1), "yxhl"))
        self.left = "yxhl"


def advance(mark, *sums, together=False):
    at = sums[0].at
    axes = [part.order[0] for part in sums]
    size = lambda axis: {"y": at.ny, "x": at.nx, "h": at.high, "l": at.low}[axis]
    group = lambda part, k: [term.at(part.order[0], k) for term in part.terms]
    if together:
        places = [(axes[0], k) for k in range(1, size(axes[0]))]
        jobs = [[group(part, k) for part in sums] for _, k in places]
    else:
        places = [(axis, k) for axis in axes for k in range(1, size(axis))]
        jobs = [[group(part, k)] for part, axis in zip(sums, axes) for k in range(1, size(axis))]
    pieces = list(totals(mark, jobs)) if jobs else []
    got = [at.shift(piece, **{axis: k}) for piece, (axis, k) in zip(pieces, places)]
    first = 0
    for part in sums:
        axis, part.order = part.order[0], part.order[1:]
        part.left = part.left.replace(axis, "")
        part.terms = [term.at(axis, 0) for term in part.terms]
        wide = part.terms[0].columns[1] - part.terms[0].columns[0]
        for _ in range(1, size(axis)):
            if together:
                continue
            part.terms.append(Term(got.pop(0), part.left))
        if together:
            part.terms += [Term(piece, part.left, (), (first, first + wide)) for piece in got]
            first += wide
    return pieces


def finish(mark, *sums):
    return totals(mark, [[part.terms] for part in sums], full)


def shards(
    decoder_in,
    encoder_states,
    encoder_doc,
    decoder_doc,
    cotangent,
    gain_self,
    gain_cross,
    gain_ffn,
    self_query,
    self_key,
    self_value,
    self_out,
    bias_table,
    cross_query,
    cross_key,
    cross_value,
    cross_out,
    ff_in,
    ff_out,
    *,
    dp_size,
    seq_size,
):
    at = Places(dp_size, seq_size)
    width = decoder_in.shape[2]
    head_count = bias_table.shape[1]
    bucket_count = bias_table.shape[0]
    score_scale = (width // head_count) ** (-0.5)
    local_rows = decoder_in.shape[1]
    doc_count = local_rows // DEC_LEN
    position = lax.axis_index("seq")
    own_map = lax.dynamic_slice_in_dim(decoder_doc[0], position * doc_count, doc_count, 0)
    gain_self, gain_cross, gain_ffn = (gain[None, :] for gain in (gain_self, gain_cross, gain_ffn))

    enc_rows = encoder_states.shape[1]
    docs = jnp.pad(encoder_doc.astype(half), ((0, 15), (0, width - enc_rows)))
    shard = jnp.concatenate([encoder_states[0], docs], axis=0)
    column = [[shard] + [at.shift(shard, l=l) for l in range(1, at.low)]]
    for h in range(1, at.high):
        far = at.shift(shard, h=h)
        column.append([far] + [at.shift(far, l=l) for l in range(1, at.low)])
    column = [rows for part in column for rows in part]
    encoded = [column] + [[at.shift(rows, x=x) for rows in column] for x in range(1, at.nx)]
    own = jnp.pad(own_map.astype(full), (0, LANES - doc_count))[:, None]
    lane = jnp.arange(LANES, dtype=jnp.int32)
    mark = (jnp.arange(local_rows, dtype=jnp.int32)[:, None] // DEC_LEN == lane).astype(half)
    buckets = jnp.asarray(bucket_map(DEC_LEN, bucket_count, MAX_REACH))

    query_self, key_self, value_self, out_self, after_self, normed_two, query_cross = self_forward(
        decoder_in[0], gain_self, gain_cross, self_query, self_key, self_value, self_out, cross_query,
        buckets, bias_table, score_scale,
    )
    sources, states, state = [], [], []
    for k, part in enumerate(encoded):
        *source, rows = key_value(part, own, cross_key, cross_value, enc_rows, doc_count)
        sources.append(source)
        states.append(rows)
        state = cross_forward(query_cross, mark, source, state, k == len(encoded) - 1, score_scale)
    mixed_cross, out_cross, extended = state
    (
        after_cross, activated, resid_grad, branch_cross, mixed_grad, gain_ffn_grad,
        in_keep, in_send, out_keep, out_send,
    ) = feed_forward(at, after_self, out_cross, cross_out, gain_ffn, ff_in, ff_out, cotangent[0])
    ff_out_sum = Reduction(at, out_keep, out_send, "yxlh")
    ff_in_sum = Reduction(at, in_keep, in_send, "xylh")

    pairs = width // LANES
    cut = pairs // 3
    mark = gate(out_send, in_send)
    query_grad_one, *grads_one = cross_backward(mark, extended, mixed_grad, mixed_cross, sources, 0, cut, score_scale)
    mark = gate(advance(query_grad_one, ff_out_sum, ff_in_sum))
    query_grad_two, *grads_two = cross_backward(
        mark, extended, mixed_grad, mixed_cross, sources, cut, pairs - cut, score_scale
    )
    mark = gate(advance(query_grad_two, ff_out_sum, ff_in_sum))

    def back_part(mark, x):
        at_part = slice(2 * x, 2 * x + 2)
        return encoder_part(mark, at, [*grads_one[at_part], *grads_two[at_part]], cross_key, cross_value)

    far = [back_part(mark, x) for x in range(1, at.nx)]
    mark = gate(far)
    early = [at.shift(part[0], x=-1 - k) for k, part in enumerate(far)]
    cross_keep, cross_send = cross_weights(
        mark, at, [query_grad_one, query_grad_two], normed_two, out_cross, branch_cross, states, grads_one + grads_two
    )
    cross_sum = Reduction(at, cross_keep, cross_send, "yxlh")
    mark = gate(advance(cross_keep, ff_out_sum, ff_in_sum, together=True), cross_send)
    late = [at.shift(part[1], x=-1 - k) for k, part in enumerate(far)]
    near = back_part(mark, 0)
    ready = advance(near[0], cross_sum)
    mark = gate(ready, early, advance(ready[0], ff_out_sum, ff_in_sum, together=True))

    input_grad, first_keep, first_send, second_keep, second_send = self_backward(
        mark, at, [query_grad_one, query_grad_two], cross_query, after_self, gain_cross, resid_grad, decoder_in[0], gain_self,
        gain_ffn_grad, query_self, key_self, value_self, out_self, self_out, self_query, self_key, self_value,
        buckets, bias_table, score_scale,
    )
    first_sum = Reduction(at, first_keep, first_send, "yxlh")
    second_sum = Reduction(at, second_keep, second_send, "xylh")
    mark = gate(first_send, second_send)
    mark = gate(advance(mark, cross_sum))
    mark = gate(advance(mark, first_sum, second_sum))

    low_terms = [Term(part, "h") for part in (near[0], *early)]
    (ready,) = totals(mark, [[low_terms]])
    high_terms = [Term(part, "h") for part in (near[1], *late, at.shift(ready, l=-1))]
    mark = gate(ready)
    activated, _ = lax.optimization_barrier((activated, mark))
    output = (after_cross + dot(activated, ff_out, NN)).astype(half)
    ff_out_grad, ff_in_grad = finish(mark, ff_out_sum, ff_in_sum)
    mark = gate(ff_in_grad, advance(mark, cross_sum))
    mark = gate(advance(mark, first_sum, second_sum))
    ready = totals(mark, [[[term.at("h", h) for term in high_terms]] for h in range(1, at.high)])
    last_terms = [term.at("h", 0) for term in high_terms] + [
        Term(at.shift(piece, h=-1 - k), "") for k, piece in enumerate(ready)
    ]
    mark = gate(ready, advance(ready[0], cross_sum))
    mark = gate(advance(mark, first_sum, second_sum, together=True))
    (encoder_grad,) = totals(mark, [[last_terms]], full)
    (cross_grads,) = finish(encoder_grad, cross_sum)
    mark = gate(cross_grads, advance(cross_grads, first_sum, second_sum, together=True))
    first_grads, second_grads = finish(mark, first_sum, second_sum)

    n, m = width // at.dp, width // at.seq
    extra = second_grads[:, 2 * n :]
    query_grad, key_grad = unpaired(at, first_grads)
    value_grad, out_grad = unpaired(at, second_grads[:, : 2 * n])
    cross_query_grad, cross_out_grad = unpaired(at, cross_grads[:, : 2 * n])
    cross_key_grad, cross_value_grad = unpaired(at, cross_grads[:, 2 * n :])
    ff_out_pieces = [
        piece
        for first in range(0, ff_out_grad.shape[1], 2 * n)
        for piece in unpaired(at, ff_out_grad[:, first : first + 2 * n])
    ]
    return (
        output[None],
        input_grad[None],
        encoder_grad[None],
        extra[:, 0],
        extra[:, 1],
        extra[:, 2],
        query_grad,
        key_grad,
        value_grad,
        out_grad,
        extra[: bucket_count // at.seq, 16 : 16 + head_count],
        cross_query_grad,
        cross_key_grad,
        cross_value_grad,
        cross_out_grad,
        ff_in_grad,
        jnp.concatenate(ff_out_pieces, axis=0),
    )


def solution(mesh):
    placed = (
        P("dp", "seq", None),
        P("dp", "seq", None),
        P("dp", "seq"),
        P("dp", None),
        P("dp", "seq", None),
    ) + (P(),) * 14
    return jax.shard_map(
        functools.partial(shards, dp_size=mesh.shape["dp"], seq_size=mesh.shape["seq"]),
        mesh=mesh,
        in_specs=placed,
        out_specs=(
            P("dp", "seq", None),
            P("dp", "seq", None),
            P("dp", "seq", None),
            P("seq"),
            P("seq"),
            P("seq"),
            P("seq", "dp"),
            P("seq", "dp"),
            P("seq", "dp"),
            P("seq", "dp"),
            P("seq", None),
            P("seq", "dp"),
            P("seq", "dp"),
            P("seq", "dp"),
            P("seq", "dp"),
            P("seq", "dp"),
            P("seq", "dp"),
        ),
        check_vma=False,
    )
```

```python
import functools
import itertools
import math

import jax
import jax.numpy as jnp
import numpy as np
from jax import lax
from jax.experimental import pallas as pl
from jax.experimental.pallas import tpu as pltpu
from jax.sharding import PartitionSpec as P

MAX_REACH = 128
DEC_LEN = 128


epsilon = 1e-06
masked_fill = -1e30
half = jnp.bfloat16
full = jnp.float32


def bucket_map(length, buckets, max_reach):
    exact_span = buckets // 2
    places = np.arange(length)
    distance = places[None, :] - places[:, None]
    passed = np.zeros_like(distance)
    for threshold_index in range(1, buckets - exact_span):
        threshold = int(
            math.ceil(
                exact_span * (max_reach / exact_span) ** (threshold_index / (buckets - exact_span))
            )
        )
        passed = passed + (distance >= threshold)
    bucket_of = np.where(distance < exact_span, distance, exact_span + passed)
    return np.where(distance < 0, -1, bucket_of).astype(np.int32)


def norm_parts(values):
    inverse = lax.rsqrt(jnp.mean(values * values, axis=-1, keepdims=True) + epsilon)
    return values * inverse, inverse


def norm_backward(upstream, normal, inverse, gain_row):
    scaled = upstream * gain_row
    inner = jnp.mean(scaled * normal, axis=-1, keepdims=True)
    return inverse * (scaled - normal * inner), jnp.sum(upstream * normal, axis=0, keepdims=True)


NT = (((1,), (1,)), ((), ()))
NN = (((1,), (0,)), ((), ()))
TN = (((0,), (0,)), ((), ()))
LANES = 128
ONES = 8
MEGA = 2**20
FUSED_ROWS = 2048
SECOND = "xylh"


def dot(left_side, right_side, dims):
    return lax.dot_general(left_side, right_side, dims, preferred_element_type=full)


def three(value):
    first = value.astype(half).astype(full)
    second = (value - first).astype(half).astype(full)
    return first, second, (value - first - second).astype(half).astype(full)


def placed_three(value, index, rest):
    first, second, third = three(value)
    return jnp.where(
        index == ONES, first, jnp.where(index == ONES + 1, second, jnp.where(index == ONES + 2, third, rest))
    )


def low_lanes(rows):
    return lax.broadcasted_iota(jnp.int32, (rows, LANES), 1) < LANES // 2


def stacked(value, low):
    zero = jnp.zeros_like(value)
    return jnp.concatenate([jnp.where(low, value, zero), jnp.where(low, zero, value)], axis=0)


def loop(count, step, start):
    return lax.fori_loop(0, count, step, start, unroll=count <= 4)


light = pl.CostEstimate(flops=1, bytes_accessed=1, transcendentals=0)


def params(megabytes):
    return pltpu.CompilerParams(vmem_limit_bytes=megabytes * MEGA)


def whole(shape):
    return pl.BlockSpec(shape, lambda *_: (0,) * len(shape))


anywhere = pl.BlockSpec(memory_space=pl.ANY)


class Blocks:
    def __init__(self, at):
        self.core, self.ny, self.nx, self.dp, self.seq = at.core, at.ny, at.nx, at.dp, at.seq
        self.high, self.low = at.high, at.low

    def shape(self, rows, columns):
        return (self.ny, self.nx, self.high, self.low, rows, columns)

    def row_place(self, block, place):
        z = lax.div(block, self.nx)
        return (
            lax.rem(lax.rem(block, self.nx) - place[2] + self.nx, self.nx),
            lax.rem(lax.div(z, self.low) - place[3] + self.high, self.high),
            lax.rem(lax.rem(z, self.low) - place[4] + self.low, self.low),
        )

    def column_place(self, y, place):
        return lax.rem(y - place[0] + self.ny, self.ny)

    def paired(self, first, second, place):
        n = first.shape[1] // self.core
        if self.core == 1:
            return jnp.concatenate([first, second], axis=1).astype(half), None
        mine = place[1] == 0
        if n % LANES != LANES // 2:
            cut = [jnp.concatenate([g[:, c * n : (c + 1) * n] for g in (first, second)], axis=1) for c in range(2)]
        else:
            main = n - LANES // 2
            low = lax.broadcasted_iota(jnp.int32, (first.shape[0], LANES), 1) < LANES // 2
            one, two = (g[:, main : main + LANES] for g in (first, second))
            sides = (
                jnp.where(low, one, pltpu.roll(two, LANES // 2, 1)),
                jnp.where(low, pltpu.roll(one, LANES // 2, 1), two),
            )
            cut = [
                jnp.concatenate([first[:, at : at + main], second[:, at : at + main], sides[c]], axis=1)
                for c, at in enumerate((0, main + LANES))
            ]
        return jnp.where(mine, cut[0], cut[1]).astype(half), jnp.where(mine, cut[1], cut[0]).astype(half)


def unpaired(piece, core):
    n = piece.shape[1] // 2
    if n % LANES != LANES // 2:
        return piece[:, :n], piece[:, n:]
    main = n - LANES // 2
    side = piece[:, 2 * main :]
    turned = pltpu.roll(side, LANES // 2, 1)
    out = []
    for k in range(2):
        big = piece[:, k * main : (k + 1) * main]
        first, second = (side, turned) if k == 0 else (turned, side)
        after = jnp.concatenate([big, first], axis=1)
        ahead = pltpu.roll(jnp.concatenate([big, second], axis=1), LANES // 2, 1)
        out.append(jnp.where(core == 0, after, ahead)[:, :n])
    return out


def position_bias(buckets, table, pair):
    out = []
    for head in range(2):
        bias = jnp.full(buckets.shape, masked_fill, full)
        for b in range(table.shape[0]):
            bias = jnp.where(buckets == b, table[b, 2 * pair + head], bias)
        out.append(bias)
    return jnp.concatenate(out, axis=1)


def self_forward_kernel(
    hidden, gain_one, gain_two, weights_q, weights_k, weights_v, weights_o, weights_c, buckets, table,
    query, key, value, mixed, after, normed_two, query_cross, normed, every, *, scale,
):
    step = pl.program_id(0)
    rows = hidden.shape[0]

    @pl.when(step == 0)
    def _():
        normal, _ = norm_parts(hidden[...].astype(full))
        normed[...] = (normal * gain_one[...]).astype(half)

    weights = jnp.concatenate([weights_q[...], weights_k[...], weights_v[...]], axis=1)
    made = dot(normed[...], weights, NN).astype(half)
    query[...] = made[:, :LANES] * scale
    key[...] = made[:, LANES : 2 * LANES]
    value[...] = made[:, 2 * LANES :]
    low = low_lanes(DEC_LEN)
    bias = position_bias(buckets[...], table, step)
    for first in range(0, rows, DEC_LEN):
        at = pl.ds(first, DEC_LEN)
        scores = dot(key[at, :], stacked(query[at, :], low), NT) + bias
        expo = jnp.exp(scores - jnp.max(scores, axis=0, keepdims=True))
        expo = (expo / jnp.sum(expo, axis=0, keepdims=True)).astype(half)
        both = dot(value[at, :], expo, TN).T
        one = jnp.where(low, both[:DEC_LEN], both[DEC_LEN:]).astype(half)
        mixed[at, :] = one
        every[at, pl.ds(pl.multiple_of(step * LANES, LANES), LANES)] = one

    @pl.when(step == pl.num_programs(0) - 1)
    def _():
        total = hidden[...].astype(full) + dot(every[...], weights_o[...], NN)
        after[...] = total
        normal, _ = norm_parts(total)
        again = (normal * gain_two[...]).astype(half)
        normed_two[...] = again
        query_cross[...] = dot(again, weights_c[...], NN).astype(half)


def self_forward(mark, hidden, gain_one, gain_two, weights_q, weights_k, weights_v, weights_o, weights_c, buckets, table, scale):
    rows, width = hidden.shape
    pairs = width // LANES
    column = lambda i: (0, i)
    row_block = pl.BlockSpec((rows, LANES), column)
    weight_block = pl.BlockSpec((width, LANES), column)
    return pl.pallas_call(
        marked(functools.partial(self_forward_kernel, scale=scale)),
        name="self_forward",
        grid=(pairs,),
        in_specs=[anywhere, whole((rows, width)), whole((1, width)), whole((1, width))]
        + [weight_block] * 3
        + [whole((width, width))] * 2
        + [whole((DEC_LEN, DEC_LEN)), pl.BlockSpec(memory_space=pltpu.SMEM)],
        out_specs=[row_block] * 4 + [whole((rows, width))] * 4,
        out_shape=[jax.ShapeDtypeStruct((rows, width), half)] * 4
        + [jax.ShapeDtypeStruct((rows, width), kind) for kind in (full, half, half, half)],
        scratch_shapes=[pltpu.VMEM((rows, width), half)],
        compiler_params=params(56),
        cost_estimate=light,
    )(mark, hidden, gain_one, gain_two, weights_q, weights_k, weights_v, weights_o, weights_c, buckets, table)


def key_value_kernel(*refs, rows, doc_count):
    shards, (own, weights_k, weights_v, keys, values, mask, states) = refs[:-7], refs[-7:]
    for i, shard in enumerate(shards):
        at = pl.ds(i * rows, rows)
        states[at, :] = shard[:rows, :]
        keys[at, :] = dot(shard[:rows, :], weights_k[...], NN).astype(half)
        values[at, :] = dot(shard[:rows, :], weights_v[...], NN).astype(half)
        docs = shard[rows : rows + 1, :rows].astype(full)
        lane = lax.broadcasted_iota(jnp.int32, (LANES, rows), 0)
        ones = ((lane >= ONES) & (lane < ONES + 3)).astype(full)
        extra = jnp.where(lane < doc_count, jnp.where(docs == own[:, :1], 0.0, masked_fill), ones)
        mask[at, :] = extra.T.astype(half)


def key_value(shards, own, weights_k, weights_v, rows, doc_count):
    width = shards[0].shape[1]
    count = len(shards) * rows
    return pl.pallas_call(
        functools.partial(key_value_kernel, rows=rows, doc_count=doc_count),
        name="key_value",
        out_shape=[jax.ShapeDtypeStruct((count, size), half) for size in (width, width, LANES, width)],
        compiler_params=params(56),
        cost_estimate=light,
    )(*shards, own, weights_k, weights_v)


def cross_forward_kernel(*refs, scale, block, opens, closes):
    query, mark, keys, values, mask = refs[:5]
    refs = refs[5:]
    if not opens:
        state_in, refs = refs[:2], refs[2:]
    if closes:
        (mixed, mixed_half, extended), refs = refs[:3], refs[3:]
    else:
        state_out, refs = refs[:2], refs[2:]
    total, wide = refs
    rows, many = query.shape[0], query.shape[1] // LANES
    low = low_lanes(rows)
    for pair in range(many):
        wide[pair, :, :LANES] = stacked(query[:, pair * LANES : (pair + 1) * LANES] * scale, low)
        wide[pair, :rows, LANES:] = mark[...]
        wide[pair, rows:, LANES:] = mark[...]
    if opens:
        total[...] = jnp.zeros_like(total)
        carry = [(jnp.full((1, 2 * rows), masked_fill, full), jnp.zeros((1, 2 * rows), full)) for _ in range(many)]
    else:
        total[...] = state_in[0][...]
        carry = [(state_in[1][pair, 0:1], state_in[1][pair, 1:2]) for pair in range(many)]

    def step(i, carry):
        at = pl.ds(pl.multiple_of(i * block, block), block)
        scores = [
            dot(jnp.concatenate([keys[at, pair * LANES : (pair + 1) * LANES], mask[at, :]], axis=1), wide[pair], NT)
            for pair in range(many)
        ]
        out = []
        for pair, (peak, amount) in enumerate(carry):
            fresh = jnp.maximum(peak, jnp.max(scores[pair], axis=0, keepdims=True))
            expo = jnp.exp(scores[pair] - fresh)
            fade = jnp.exp(peak - fresh)
            values_here = values[at, pair * LANES : (pair + 1) * LANES]
            total[pair] = total[pair] * fade + dot(values_here, expo.astype(half), TN)
            out.append((fresh, amount * fade + jnp.sum(expo, axis=0, keepdims=True)))
        return out

    carry = loop(keys.shape[0] // block, step, carry)
    if not closes:
        state_out[0][...] = total[...]
        for pair, (peak, amount) in enumerate(carry):
            state_out[1][pair, 0:1] = peak
            state_out[1][pair, 1:2] = amount
        return
    index = lax.broadcasted_iota(jnp.int32, (LANES, 2 * rows), 0)
    for pair, (peak, amount) in enumerate(carry):
        at = slice(pair * LANES, (pair + 1) * LANES)
        both = (total[pair] / amount).T
        one = jnp.where(low, both[:rows], both[rows:])
        mixed[:, at] = one
        mixed_half[:, at] = one.astype(half)
        extra = placed_three(-(peak + jnp.log(amount)), index, 0.0).T
        extended[pair, :, :LANES] = wide[pair, :, :LANES]
        extended[pair, :, LANES:] = (wide[pair, :, LANES:].astype(full) + extra).astype(half)


def cross_forward(query, mark, source, state, closes, scale):
    rows, pairs, many = query.shape[0], query.shape[1] // LANES, 2
    count = source[0].shape[0]
    column = lambda i: (0, i)
    plane = lambda i: (i, 0, 0)
    block = min(1024, count)
    state_specs = [pl.BlockSpec((many, LANES, 2 * rows), plane), pl.BlockSpec((many, 2, 2 * rows), plane)]
    state_shape = [
        jax.ShapeDtypeStruct((pairs, LANES, 2 * rows), full),
        jax.ShapeDtypeStruct((pairs, 2, 2 * rows), full),
    ]
    last_specs = [pl.BlockSpec((rows, many * LANES), column)] * 2 + [pl.BlockSpec((many, 2 * rows, 2 * LANES), plane)]
    last_shape = [
        jax.ShapeDtypeStruct(query.shape, full),
        jax.ShapeDtypeStruct(query.shape, half),
        jax.ShapeDtypeStruct((pairs, 2 * rows, 2 * LANES), half),
    ]
    return pl.pallas_call(
        functools.partial(cross_forward_kernel, scale=scale, block=block, opens=not state, closes=closes),
        name="cross_forward",
        grid=(pairs // many,),
        in_specs=[pl.BlockSpec((rows, many * LANES), column), whole((rows, LANES))]
        + [pl.BlockSpec((count, many * LANES), column), pl.BlockSpec((count, many * LANES), column), whole((count, LANES))]
        + (state_specs if state else []),
        out_specs=last_specs if closes else state_specs,
        out_shape=last_shape if closes else state_shape,
        scratch_shapes=[
            pltpu.VMEM((many, LANES, 2 * rows), full),
            pltpu.VMEM((many, 2 * rows, 2 * LANES), half),
        ],
        compiler_params=params(56),
        cost_estimate=light,
    )(query, mark, *source, *state)


def cross_backward_kernel(*refs, scale, block, parts):
    extended, upstream, mixed = refs[:3]
    sources = [refs[3 + 3 * i : 6 + 3 * i] for i in range(parts)]
    query_grad = refs[3 + 3 * parts]
    grads = [refs[4 + 3 * parts + 2 * i : 6 + 3 * parts + 2 * i] for i in range(parts)]
    wide, total = refs[-2:]
    rows = upstream.shape[0]
    low = low_lanes(rows)
    lane = lax.broadcasted_iota(jnp.int32, (rows, LANES), 1)
    each = upstream[...].astype(full) * mixed[...]
    wide[:, :LANES] = stacked(upstream[...], low)
    for head in range(2):
        inner = jnp.sum(jnp.where(low == (head == 0), each, 0.0), axis=1, keepdims=True)
        wide[head * rows : (head + 1) * rows, LANES:] = placed_three(-inner, lane, 0.0).astype(half)
    total[...] = jnp.zeros_like(total)
    for (keys, values, mask), (key_grad, value_grad) in zip(sources, grads):

        def step(i, carry):
            at = pl.ds(pl.multiple_of(i * block, block), block)
            extra = mask[at, :]
            expo = jnp.exp(dot(jnp.concatenate([keys[at, :], extra], axis=1), extended[0], NT))
            change = dot(jnp.concatenate([values[at, :], extra], axis=1), wide[...], NT)
            score = (expo * change).astype(half)
            value_grad[at, :] = dot(expo.astype(half), wide[:, :LANES], NN).astype(half)
            key_grad[at, :] = dot(score, extended[0, :, :LANES], NN).astype(half)
            total[...] += dot(keys[at, :], score, TN)
            return carry

        loop(keys.shape[0] // block, step, 0)
    both = total[...].T
    query_grad[...] = (jnp.where(low, both[:rows], both[rows:]) * scale).astype(half)


def cross_backward(mark, extended, upstream, mixed, sources, first, pairs, begun, scale):
    rows, width = upstream.shape
    count = sources[0][0].shape[0]
    every = count * len(sources)
    column = lambda i: (0, i + first)
    block = min(1024, count)
    row_block, key_block = pl.BlockSpec((rows, LANES), column), pl.BlockSpec((count, LANES), column)
    operands = [extended, upstream, mixed, *[array for source in sources for array in source]]
    kernel = functools.partial(cross_backward_kernel, scale=scale, block=block, parts=len(sources))
    return pl.pallas_call(
        marked(lambda *refs: kernel(*refs[len(begun) :]), len(begun)),
        name="cross_backward",
        grid=(pairs,),
        in_specs=[anywhere] * (len(begun) + 1)
        + [pl.BlockSpec((1, 2 * rows, 2 * LANES), lambda i: (i + first, 0, 0)), row_block, row_block]
        + [key_block, key_block, whole((count, LANES))] * len(sources),
        out_specs=[row_block] + [key_block] * (2 * len(sources)),
        out_shape=[jax.ShapeDtypeStruct((rows, width), half)]
        + [jax.ShapeDtypeStruct((count, width), half)] * (2 * len(sources)),
        scratch_shapes=[
            pltpu.VMEM((2 * rows, 2 * LANES), half),
            pltpu.VMEM((LANES, 2 * rows), full),
        ],
        input_output_aliases={i: i for i in range(len(begun))},
        compiler_params=params(56),
        cost_estimate=light,
    )(*begun, mark, *operands)


def feed_forward_kernel(
    place, after, mixed, weights_o, gain, weights_in, weights_out, cotangent,
    after_cross, activated, resid, branch, mixed_grad, gain_grad, in_keep, in_send, out_keep, out_send,
    normed, total, *, blocks,
):
    step = pl.program_id(0)

    @pl.when(step == 0)
    def _():
        values = after[...] + dot(mixed[...], weights_o[...], NN)
        after_cross[...] = values
        normal, _ = norm_parts(values)
        normed[...] = (normal * gain[...]).astype(half)
        total[...] = jnp.zeros_like(total)

    upstream = cotangent[...]
    pre = dot(normed[...], weights_in[...], NN)
    square = pre * pre
    slope = math.sqrt(2.0 / math.pi)
    bend = jnp.tanh(slope * (pre + 0.044715 * (square * pre)))
    act = (0.5 * pre * (1.0 + bend)).astype(half)
    activated[...] = act
    gelu_grad = 0.5 * (1.0 + bend) + 0.5 * pre * (1.0 - bend * bend) * (slope * (1.0 + 3 * 0.044715 * square))
    pre_grad = (dot(upstream, weights_out[...], NT) * gelu_grad).astype(half)
    total[...] += dot(pre_grad, weights_in[...], NT)

    grad = dot(normed[...], pre_grad, TN).astype(half)
    m = grad.shape[0] // blocks.seq
    to_y = blocks.column_place(lax.div(step, blocks.core), place)
    ours = lax.rem(step, blocks.core) == place[1]

    def fill(target):
        for block in range(blocks.seq):
            to_x, to_h, to_l = blocks.row_place(jnp.int32(block), place)
            target[to_y, to_x, to_h, to_l] = grad[block * m : (block + 1) * m]

    pl.when(ours)(lambda: fill(in_keep))
    pl.when(jnp.logical_not(ours))(lambda: fill(in_send))

    grad = dot(act, upstream, TN)
    wide = grad.shape[1] // blocks.ny
    n = wide // blocks.core
    pieces = out_keep.shape[5] // n
    many = pieces * m
    for y in range(blocks.ny):
        at = slice(y * wide, (y + 1) * wide)
        to_y = blocks.column_place(jnp.int32(y), place)
        for block in range(grad.shape[0] // many):
            to_x, to_h, to_l = blocks.row_place(step * (grad.shape[0] // many) + block, place)
            for piece in range(0, pieces, 2):
                first = block * many + piece * m
                kept, sent = blocks.paired(grad[first : first + m, at], grad[first + m : first + 2 * m, at], place)
                out_keep[to_y, to_x, to_h, to_l, :, piece * n : (piece + 2) * n] = kept
                if sent is not None:
                    out_send[to_y, to_x, to_h, to_l, :, piece * n : (piece + 2) * n] = sent

    @pl.when(step == pl.num_programs(0) - 1)
    def _():
        normal, inverse = norm_parts(after_cross[...])
        change, gain_sum = norm_backward(total[...], normal, inverse, gain[...])
        gain_grad[...] = gain_sum
        change = change + upstream.astype(full)
        resid[...] = change
        rounded = change.astype(half)
        branch[...] = rounded
        mixed_grad[...] = dot(rounded, weights_o[...], NT).astype(half)


def feed_forward(at, after, mixed, weights_o, gain, weights_in, weights_out, cotangent):
    rows, width = after.shape
    depth = weights_in.shape[1]
    blocks = Blocks(at)
    cut = depth // at.dp
    shape = blocks.shape(width // at.seq, cut)
    all_rows = whole((rows, width))
    sized = lambda kind: jax.ShapeDtypeStruct((rows, width), kind)
    return pl.pallas_call(
        functools.partial(feed_forward_kernel, blocks=blocks),
        name="feed_forward",
        grid_spec=pltpu.PrefetchScalarGridSpec(
            num_scalar_prefetch=1,
            grid=(at.dp,),
            in_specs=[
                all_rows,
                all_rows,
                whole((width, width)),
                whole((1, width)),
                pl.BlockSpec((width, cut), lambda i, _: (0, i)),
                pl.BlockSpec((cut, width), lambda i, _: (i, 0)),
                all_rows,
            ],
            out_specs=[all_rows, pl.BlockSpec((rows, cut), lambda i, _: (0, i))]
            + [all_rows] * 3
            + [whole((1, width))]
            + [whole(shape)] * 4,
            scratch_shapes=[pltpu.VMEM((rows, width), half), pltpu.VMEM((rows, width), full)],
        ),
        out_shape=[sized(full), jax.ShapeDtypeStruct((rows, depth), half), sized(full), sized(half), sized(half)]
        + [jax.ShapeDtypeStruct((1, width), full)]
        + [jax.ShapeDtypeStruct(shape, half)] * 4,
        compiler_params=params(56),
        cost_estimate=light,
    )(at.place, after, mixed, weights_o, gain, weights_in, weights_out, cotangent)


def encoder_part_kernel(key_grad, value_grad, weights_k, weights_v, early, late, *, early_steps):
    total = dot(key_grad[...], weights_k[...], NT) + dot(value_grad[...], weights_v[...], NT)
    is_early = pl.program_id(0) < early_steps

    @pl.when(is_early)
    def _():
        early[...] = total.astype(half)

    @pl.when(jnp.logical_not(is_early))
    def _():
        late[...] = total.astype(half)


def encoder_part(mark, at, grads, weights_k, weights_v):
    width = weights_k.shape[0]
    rows = grads[0].shape[0] // at.nz
    early = at.high * (at.low - 1)
    plane = lambda size: jax.ShapeDtypeStruct((size, rows, width), half)
    block = pl.BlockSpec((rows, width), lambda i: (i % at.high * at.low + at.low - 1 - i // at.high, 0))
    return pl.pallas_call(
        marked(functools.partial(encoder_part_kernel, early_steps=early)),
        name="encoder_part",
        grid=(at.nz,),
        in_specs=[anywhere, block, block, whole((width, width)), whole((width, width))],
        out_specs=[
            pl.BlockSpec((None, rows, width), lambda i: (jnp.minimum(i, early - 1), 0, 0)),
            pl.BlockSpec((None, rows, width), lambda i: (jnp.maximum(i - early, 0), 0, 0)),
        ],
        out_shape=[plane(early), plane(at.high)],
        compiler_params=params(56),
        cost_estimate=light,
    )(mark, *grads, weights_k, weights_v)


def weight_grads_kernel(place, *refs, blocks, counts, chunks, extra, wide):
    refs = list(refs)
    sides = [[(refs.pop(0), refs.pop(0)) for _ in range(count)] for count in counts]
    small = refs.pop(0) if extra else None
    made = [sum((dot(left[...], right[...], TN) for left, right in side[1:]), dot(side[0][0][...], side[0][1][...], TN)) for side in sides]
    m = made[0].shape[0] // blocks.seq
    many = made[0].shape[1] // wide
    for chunk, pairs in enumerate(chunks):
        keep, send = refs[2 * chunk], refs[2 * chunk + 1]
        for y in range(many):
            at = slice(y * wide, (y + 1) * wide)
            columns = [blocks.paired(made[2 * pair][:, at], made[2 * pair + 1][:, at], place) for pair in pairs]
            if extra and chunk == len(chunks) - 1:
                columns.append((small[...], small[...]))
            to_y = blocks.column_place(jnp.int32(y), place) if many > 1 else 0
            for block in range(blocks.seq):
                to_x, to_h, to_l = blocks.row_place(jnp.int32(block), place)
                rows = slice(block * m, (block + 1) * m)
                first = 0
                for ours, theirs in columns:
                    to = slice(first, first + ours.shape[1])
                    keep[to_y, to_x, to_h, to_l, :, to] = ours[rows]
                    send[to_y, to_x, to_h, to_l, :, to] = theirs[rows]
                    first += ours.shape[1]


def weight_grads(mark, at, sides, chunks, extra=None):
    blocks = Blocks(at)
    width = sides[0][0][0].shape[1]
    wide, m = width // at.ny, width // at.seq
    shapes = [blocks.shape(m, len(pairs) * 2 * wide // at.core) for pairs in chunks]
    if extra is not None:
        shapes[-1] = (*shapes[-1][:-1], shapes[-1][-1] + extra.shape[1])
    terms = [term for side in sides for term in side]
    steps = at.ny if wide % LANES == 0 else 1
    from_y = lambda i, place: (0, lax.rem(i + place[0], at.ny) if steps > 1 else 0)
    out_block = lambda shape: pl.BlockSpec((shape[0] // steps, *shape[1:]), lambda i, place: (i, 0, 0, 0, 0, 0))
    return pl.pallas_call(
        marked(
            functools.partial(
                weight_grads_kernel,
                blocks=blocks,
                counts=[len(side) for side in sides],
                chunks=chunks,
                extra=extra is not None,
                wide=wide,
            ),
            1,
        ),
        name="weight_grads",
        grid_spec=pltpu.PrefetchScalarGridSpec(
            num_scalar_prefetch=1,
            grid=(steps,),
            in_specs=[anywhere]
            + [
                spec
                for left, right in terms
                for spec in (whole(left.shape), pl.BlockSpec((right.shape[0], width // steps), from_y))
            ]
            + ([whole(extra.shape)] if extra is not None else []),
            out_specs=[out_block(shape) for shape in shapes for _ in range(2)],
        ),
        out_shape=[jax.ShapeDtypeStruct(shape, half) for shape in shapes for _ in range(2)],
        compiler_params=params(60),
        cost_estimate=light,
    )(at.place, mark, *[array for term in terms for array in term], *([extra] if extra is not None else []))


def laid_out(at, grads):
    out = []
    for grad in grads:
        m, n = grad.shape[0] // at.seq, grad.shape[1] // at.dp
        assert n % LANES != LANES // 2
        blocks = grad.astype(half).reshape(at.high, at.low, at.nx, m, at.ny, at.core, n)
        places = ((0, at.z // at.low, at.high), (1, at.z % at.low, at.low), (2, at.x, at.nx), (4, at.y, at.ny), (5, at.c, at.core))
        for axis, own, size in places:
            blocks = jnp.take(blocks, (own + jnp.arange(size)) % size, axis=axis)
        out.append(blocks.transpose(5, 4, 2, 0, 1, 3, 6))
    both = jnp.concatenate(out, axis=-1)
    return both[0], both[1]


def cross_close_kernel(place, *refs, blocks, parts):
    count = 3 * parts + 6
    arrays, refs = refs[:count], refs[count:]
    shares, (keep, send), refs = refs[: 2 * parts], refs[2 * parts : 2 * parts + 2], refs[2 * parts + 2 :]
    held, refs = refs[:count], refs[count:]
    made, (keep_held, send_held, arrived, gone) = refs[:parts], refs[parts:]
    ins = [pltpu.make_async_copy(array, place_held, arrived.at[i]) for i, (array, place_held) in enumerate(zip(arrays, held))]
    grads, (weights_k, weights_v), states = held[: 2 * parts], held[2 * parts : 2 * parts + 2], held[2 * parts + 2 : -4]
    normed, query_grad, mixed, branch = held[-4:]
    outs = []

    def leave(source, target):
        copy = pltpu.make_async_copy(source, target, gone.at[len(outs)])
        copy.start()
        outs.append(copy)

    order = [*range(1, parts), 0]
    first = [i for x in order[:1] for i in (2 * x, 2 * x + 1)] + [2 * parts, 2 * parts + 1]
    for i in first + [i for i in range(count) if i not in first]:
        ins[i].start()
    ins[2 * parts].wait()
    ins[2 * parts + 1].wait()
    rows = grads[0].shape[0] // (blocks.high * blocks.low)
    early_size = blocks.low - 1
    for x in order:
        ins[2 * x].wait()
        ins[2 * x + 1].wait()
        for block in range(blocks.high * blocks.low):
            at = slice(block * rows, (block + 1) * rows)
            total = dot(grads[2 * x][at, :], weights_k[...], NT) + dot(grads[2 * x + 1][at, :], weights_v[...], NT)
            made[x][at, :] = total.astype(half)
        for block in range(blocks.high * blocks.low):
            h, l = divmod(block, blocks.low)
            source = made[x].at[pl.ds(block * rows, rows), :]
            leave(source, shares[2 * x].at[(blocks.low - 1 - l) * blocks.high + h] if l else shares[2 * x + 1].at[h])

    def place_pair(one, two, offset):
        m, wide = one.shape[0] // blocks.seq, one.shape[1] // blocks.ny
        for y in range(blocks.ny):
            at = slice(y * wide, (y + 1) * wide)
            ours, theirs = blocks.paired(one[:, at], two[:, at], place)
            to_y = blocks.column_place(jnp.int32(y), place)
            to = slice(offset, offset + ours.shape[1])
            for block in range(blocks.seq):
                to_x, to_h, to_l = blocks.row_place(jnp.int32(block), place)
                own = slice(block * m, (block + 1) * m)
                keep_held[to_y, to_x, to_h, to_l, :, to] = ours[own]
                send_held[to_y, to_x, to_h, to_l, :, to] = theirs[own]
        for source, target in ((send_held, send), (keep_held, keep)):
            leave(source.at[:, :, :, :, :, to], target.at[:, :, :, :, :, to])

    n = keep_held.shape[5] // 4
    for copy in ins[2 * parts + 2 : -4]:
        copy.wait()
    total = []
    for kind in range(2):
        terms = [dot(states[x][...], grads[2 * x + kind][...], TN) for x in range(parts)]
        total.append(sum(terms[1:], terms[0]))
    place_pair(total[0], total[1], 2 * n)
    for copy in ins[-4:]:
        copy.wait()
    place_pair(dot(normed[...], query_grad[...], TN), dot(mixed[...], branch[...], TN), 0)
    for copy in outs:
        copy.wait()


def cross_close(mark, at, normed, query_grad, mixed, branch, states, grads, weights_k, weights_v):
    blocks, parts = Blocks(at), len(states)
    count, width = states[0].shape
    shape = blocks.shape(width // at.seq, 4 * width // at.dp)
    arrays = [*grads, weights_k, weights_v, *states, normed, query_grad, mixed, branch]
    plane = lambda size: jax.ShapeDtypeStruct((size, count // at.nz, width), half)
    outs = [plane(at.high * (at.low - 1)), plane(at.high)] * parts + [jax.ShapeDtypeStruct(shape, half)] * 2
    made = pl.pallas_call(
        marked(functools.partial(cross_close_kernel, blocks=blocks, parts=parts), 1),
        name="cross_close",
        in_specs=[pl.BlockSpec(memory_space=pltpu.SMEM)] + [anywhere] * (len(arrays) + 1),
        out_specs=[anywhere] * len(outs),
        out_shape=outs,
        scratch_shapes=[pltpu.VMEM(array.shape, half) for array in arrays]
        + [pltpu.VMEM((count, width), half)] * parts
        + [pltpu.VMEM(shape, half)] * 2
        + [pltpu.SemaphoreType.DMA((len(arrays),)), pltpu.SemaphoreType.DMA((parts * at.nz + 4,))],
        compiler_params=params(56),
        cost_estimate=light,
    )(at.place, mark, *arrays)
    return [made[2 * x : 2 * x + 2] for x in range(parts)], *made[-2:]


def self_backward_kernel(
    query_cross_grad, weights_c, after, gain_two, resid_in, hidden, gain_one, gain_ffn_grad,
    query, key, value, weights_ob, weights_q, weights_k, weights_v, buckets, table,
    input_grad, branch, query_grad, key_grad, value_grad, extra,
    resid, total, bias_rows, gain_two_grad, columns, *, scale, shares,
):
    step = pl.program_id(0)
    rows, width = hidden.shape

    @pl.when(step == 0)
    def _():
        normal, inverse = norm_parts(after[...])
        up = dot(query_cross_grad[...], weights_c[...], NT)
        change, gain_sum = norm_backward(up, normal, inverse, gain_two[...])
        gain_two_grad[...] = gain_sum
        change = change + resid_in[...]
        resid[...] = change
        branch[...] = change.astype(half)
        total[...] = jnp.zeros_like(total)

    low = low_lanes(DEC_LEN)
    upstream = dot(branch[...], weights_ob[...], NT).astype(half)
    summed = None
    bias = position_bias(buckets[...], table, step)
    for first in range(0, rows, DEC_LEN):
        at = pl.ds(first, DEC_LEN)
        wide = stacked(query[at, :], low)
        grad = stacked(upstream[first : first + DEC_LEN], low)
        scores = dot(key[at, :], wide, NT) + bias
        expo = jnp.exp(scores - jnp.max(scores, axis=0, keepdims=True))
        expo = expo / jnp.sum(expo, axis=0, keepdims=True)
        change = dot(value[at, :], grad, NT)
        rounded = (expo * (change - jnp.sum(expo * change, axis=0, keepdims=True))).astype(half)
        both = dot(key[at, :], rounded, TN).T
        query_grad[at, :] = (jnp.where(low, both[:DEC_LEN], both[DEC_LEN:]) * scale).astype(half)
        key_grad[at, :] = dot(rounded, wide, NN).astype(half)
        value_grad[at, :] = dot(expo.astype(half), grad, NN).astype(half)
        summed = rounded.astype(full) if summed is None else summed + rounded.astype(full)
    made = jnp.concatenate([query_grad[...], key_grad[...], value_grad[...]], axis=1)
    total[...] += dot(made, jnp.concatenate([weights_q[...], weights_k[...], weights_v[...]], axis=1), NT)
    count = bias_rows.shape[1]
    of_pair = jnp.concatenate([buckets[...], buckets[...]], axis=1)
    sums = [jnp.sum(jnp.where(of_pair == b, summed, 0.0), axis=0, keepdims=True) for b in range(count)]
    bias_rows[step] = jnp.concatenate(sums, axis=0)

    @pl.when(step == pl.num_programs(0) - 1)
    def _():
        normal, inverse = norm_parts(hidden[...].astype(full))
        change, gain_sum = norm_backward(total[...], normal, inverse, gain_one[...])
        input_grad[...] = resid[...] + change

        index = lax.broadcasted_iota(jnp.int32, (LANES, width), 0)
        gains = jnp.where(
            index == 0,
            gain_sum,
            jnp.where(index == 1, gain_two_grad[...], jnp.where(index == 2, gain_ffn_grad[...], 0.0)),
        )
        columns[...] = gains.T
        lane = lax.broadcasted_iota(jnp.int32, (count, LANES), 1)
        sums = jnp.zeros((count, LANES), full)
        for pair in range(bias_rows.shape[0]):
            for head in range(2):
                part = bias_rows[pair, :, head * LANES : (head + 1) * LANES]
                sums = jnp.where(lane == 16 + 2 * pair + head, jnp.sum(part, axis=1, keepdims=True), sums)
        m, each = width // shares, count // shares
        for block in range(shares):
            at = slice(block * m, block * m + each)
            columns[at, :] = columns[at, :] + sums[block * each : (block + 1) * each]
        extra[...] = columns[...].astype(half)


def self_backward(
    mark, shares, query_cross_grad, weights_c, after, gain_two, resid, hidden, gain_one, gain_ffn_grad,
    query, key, value, weights_o, weights_q, weights_k, weights_v, buckets, table, scale,
):
    rows, width = hidden.shape
    pairs, count = width // LANES, table.shape[0]
    row_block = pl.BlockSpec((rows, LANES), lambda i: (0, i))
    weight_block = pl.BlockSpec((width, LANES), lambda i: (0, i))
    all_rows, line = whole((rows, width)), whole((1, width))
    sized = lambda kind: jax.ShapeDtypeStruct((rows, width), kind)
    return pl.pallas_call(
        marked(functools.partial(self_backward_kernel, scale=scale, shares=shares)),
        name="self_backward",
        grid=(pairs,),
        in_specs=[anywhere, all_rows, whole((width, width)), all_rows, line, all_rows, all_rows, line, line]
        + [row_block] * 3
        + [pl.BlockSpec((LANES, width), lambda i: (i, 0))]
        + [weight_block] * 3
        + [whole((DEC_LEN, DEC_LEN)), pl.BlockSpec(memory_space=pltpu.SMEM)],
        out_specs=[all_rows, all_rows] + [row_block] * 3 + [whole((width, LANES))],
        out_shape=[sized(full)] + [sized(half)] * 4 + [jax.ShapeDtypeStruct((width, LANES), half)],
        scratch_shapes=[
            pltpu.VMEM((rows, width), full),
            pltpu.VMEM((rows, width), full),
            pltpu.VMEM((pairs, count, 2 * DEC_LEN), full),
            pltpu.VMEM((1, width), full),
            pltpu.VMEM((width, LANES), full),
        ],
        compiler_params=params(56),
        cost_estimate=light,
    )(
        mark, query_cross_grad, weights_c, after, gain_two, resid, hidden, gain_one, gain_ffn_grad,
        query, key, value, weights_o, weights_q, weights_k, weights_v, buckets, table,
    )


class Places:
    def __init__(self, dp_size, seq_size):
        self.dp, self.seq = dp_size, seq_size
        self.core = 2 if dp_size % 2 == 0 else 1
        self.ny = dp_size // self.core
        self.nx = self.ny if seq_size % self.ny == 0 else 1
        self.nz = seq_size // self.nx
        self.low = 2 if self.nz % 2 == 0 else 1
        self.high = self.nz // self.low
        dp_index, seq_index = lax.axis_index("dp"), lax.axis_index("seq")
        self.c, self.y = dp_index % self.core, dp_index // self.core
        self.x, self.z = seq_index % self.nx, seq_index // self.nx
        self.place = jnp.stack([self.y, self.c, self.x, self.z // self.low, self.z % self.low]).astype(jnp.int32)

    def shift(self, value, **steps):
        sizes = {"y": self.ny, "c": self.core, "h": self.high, "l": self.low, "x": self.nx}
        flat = lambda p: ((p["y"] * self.core + p["c"]) * self.seq) + (p["h"] * self.low + p["l"]) * self.nx + p["x"]
        pairs = []
        for numbers in itertools.product(*[range(size) for size in sizes.values()]):
            here = dict(zip(sizes, numbers))
            there = {axis: (here[axis] + steps.get(axis, 0)) % size for axis, size in sizes.items()}
            pairs.append((flat(here), flat(there)))
        return lax.ppermute(value, ("dp", "seq"), pairs)


def gate_kernel(*refs):
    refs[-1][...] = jnp.zeros_like(refs[-1])


def gate(*waits):
    arrays = jax.tree.leaves(waits)
    return pl.pallas_call(
        gate_kernel,
        name="gate",
        in_specs=[pl.BlockSpec(memory_space=pl.ANY)] * len(arrays),
        out_shape=jax.ShapeDtypeStruct((8, LANES), full),
        cost_estimate=pl.CostEstimate(flops=10**13, bytes_accessed=10**10, transcendentals=0),
    )(*arrays)


def marked(kernel, scalars=0):
    return lambda *refs: kernel(*refs[:scalars], *refs[scalars + 1 :])


class Term:
    def __init__(self, array, axes, fixed=(), columns=None):
        self.array, self.axes, self.fixed = array, axes, dict(fixed)
        self.columns = columns or (0, array.shape[-1])

    def at(self, axis, place):
        return Term(self.array, self.axes, {**self.fixed, axis: place}, self.columns)

    def free(self):
        sizes = zip(self.axes, self.array.shape)
        return tuple(size for axis, size in sizes if axis not in self.fixed)

    def spec(self):
        shape = [None if axis in self.fixed else size for axis, size in zip(self.axes, self.array.shape)]
        places = [self.fixed.get(axis, 0) for axis in self.axes]
        return pl.BlockSpec((*shape, *self.array.shape[-2:]), lambda i: (*places, 0, 0))


def totals_kernel(*refs, jobs):
    refs = list(refs)
    sources, outs = refs[: -len(jobs)], refs[-len(jobs) :]
    for groups, out in zip(jobs, outs):
        first = 0
        for columns in groups:
            total = None
            for low, high in columns:
                value = sources.pop(0)[..., low:high].astype(full)
                total = value if total is None else total + value
            out[..., first : first + total.shape[-1]] = total.astype(out.dtype)
            first += total.shape[-1]


def totals(mark, jobs, kind=half):
    terms = [term for groups in jobs for group in groups for term in group]
    shape = lambda groups: (
        *groups[0][0].free(),
        groups[0][0].array.shape[-2],
        sum(group[0].columns[1] - group[0].columns[0] for group in groups),
    )
    return pl.pallas_call(
        marked(
            functools.partial(totals_kernel, jobs=[[[term.columns for term in group] for group in groups] for groups in jobs])
        ),
        name="totals",
        grid=(1,),
        in_specs=[anywhere] + [term.spec() for term in terms],
        out_specs=[whole(shape(groups)) for groups in jobs],
        out_shape=[jax.ShapeDtypeStruct(shape(groups), kind) for groups in jobs],
        compiler_params=params(56),
        cost_estimate=light,
    )(mark, *[term.array for term in terms])


def final_kernel(place, *refs, terms, shapes, head_count):
    refs = list(refs)
    sources, outs = refs[: sum(len(columns) for columns in terms)], refs[sum(len(columns) for columns in terms) :]
    for columns, holds in zip(terms, shapes):
        total = None
        for low, high in columns:
            value = sources.pop(0)[..., low:high].astype(full)
            total = value if total is None else total + value
        first = 0
        for hold in holds:
            if hold == "plain":
                outs.pop(0)[...] = total
            elif hold == "pair":
                wide = outs[0].shape[1] * 2
                for out, value in zip(outs[:2], unpaired(total[:, first : first + wide], place[1])):
                    out[...] = value
                outs, first = outs[2:], first + wide
            elif hold == "rows":
                out, m = outs.pop(0), total.shape[0]
                wide = out.shape[1]
                for piece in range(0, out.shape[0] // m, 2):
                    two = unpaired(total[:, piece * wide : (piece + 2) * wide], place[1])
                    out[piece * m : (piece + 1) * m, :] = two[0]
                    out[(piece + 1) * m : (piece + 2) * m, :] = two[1]
            else:
                turned = total[:, first:].T
                for k in range(3):
                    outs.pop(0)[...] = turned[k : k + 1, :]
                bias = outs.pop(0)
                bias[...] = pltpu.roll(total[:, first:], LANES - 16, 1)[: bias.shape[0], :head_count]


def final(mark, at, sums, holds, shapes, head_count):
    terms = [part.terms for part in sums]
    arrays = [term for group in terms for term in group]
    as_prefetch = lambda spec: pl.BlockSpec(spec.block_shape, lambda i, _, index=spec.index_map: index(i))
    return pl.pallas_call(
        marked(
            functools.partial(
                final_kernel,
                terms=[[term.columns for term in group] for group in terms],
                shapes=holds,
                head_count=head_count,
            ),
            1,
        ),
        name="final",
        grid_spec=pltpu.PrefetchScalarGridSpec(
            num_scalar_prefetch=1,
            grid=(1,),
            in_specs=[anywhere] + [as_prefetch(term.spec()) for term in arrays],
            out_specs=[whole(shape) for shape in shapes],
        ),
        out_shape=[jax.ShapeDtypeStruct(shape, full) for shape in shapes],
        compiler_params=params(56),
        cost_estimate=light,
    )(at.place, mark, *[term.array for term in arrays])


class Reduction:
    def __init__(self, at, keep, send, order):
        self.at, self.order = at, order
        self.terms = [Term(keep, "yxhl")]
        if at.core == 2:
            self.terms.append(Term(at.shift(send, c=1), "yxhl"))
        self.left = "yxhl"


def advance(mark, *sums, together=False):
    at = sums[0].at
    axes = [part.order[0] for part in sums]
    size = lambda axis: {"y": at.ny, "x": at.nx, "h": at.high, "l": at.low}[axis]
    group = lambda part, k: [term.at(part.order[0], k) for term in part.terms]
    if together:
        places = [(axes[0], k) for k in range(1, size(axes[0]))]
        jobs = [[group(part, k) for part in sums] for _, k in places]
    else:
        places = [(axis, k) for axis in axes for k in range(1, size(axis))]
        jobs = [[group(part, k)] for part, axis in zip(sums, axes) for k in range(1, size(axis))]
    pieces = list(totals(mark, jobs)) if jobs else []
    got = [at.shift(piece, **{axis: k}) for piece, (axis, k) in zip(pieces, places)]
    first = 0
    for part in sums:
        axis, part.order = part.order[0], part.order[1:]
        part.left = part.left.replace(axis, "")
        part.terms = [term.at(axis, 0) for term in part.terms]
        wide = part.terms[0].columns[1] - part.terms[0].columns[0]
        for _ in range(1, size(axis)):
            if together:
                continue
            part.terms.append(Term(got.pop(0), part.left))
        if together:
            part.terms += [Term(piece, part.left, (), (first, first + wide)) for piece in got]
            first += wide
    return pieces


def shards(
    decoder_in,
    encoder_states,
    encoder_doc,
    decoder_doc,
    cotangent,
    gain_self,
    gain_cross,
    gain_ffn,
    self_query,
    self_key,
    self_value,
    self_out,
    bias_table,
    cross_query,
    cross_key,
    cross_value,
    cross_out,
    ff_in,
    ff_out,
    *,
    dp_size,
    seq_size,
):
    at = Places(dp_size, seq_size)
    width = decoder_in.shape[2]
    head_count = bias_table.shape[1]
    bucket_count = bias_table.shape[0]
    score_scale = (width // head_count) ** (-0.5)
    local_rows = decoder_in.shape[1]
    doc_count = local_rows // DEC_LEN
    position = lax.axis_index("seq")
    own_map = lax.dynamic_slice_in_dim(decoder_doc[0], position * doc_count, doc_count, 0)
    gain_self, gain_cross, gain_ffn = (gain[None, :] for gain in (gain_self, gain_cross, gain_ffn))

    enc_rows = encoder_states.shape[1]
    docs = jnp.pad(encoder_doc.astype(half), ((0, 15), (0, width - enc_rows)))
    shard = jnp.concatenate([encoder_states[0], docs], axis=0)
    near = [at.shift(shard, l=l) for l in range(1, at.low)]
    over = [at.shift(shard, x=x) for x in range(1, at.nx)]
    far = [at.shift(shard, h=h) for h in range(1, at.high)]
    mark = gate(shard)
    own = jnp.pad(own_map.astype(full), (0, LANES - doc_count))[:, None]
    lane = jnp.arange(LANES, dtype=jnp.int32)
    mark = (jnp.arange(local_rows, dtype=jnp.int32)[:, None] // DEC_LEN == lane).astype(half)
    buckets = jnp.asarray(bucket_map(DEC_LEN, bucket_count, MAX_REACH))

    query_self, key_self, value_self, out_self, after_self, normed_two, query_cross, normed_one = self_forward(
        mark, decoder_in[0], gain_self, gain_cross, self_query, self_key, self_value, self_out, cross_query,
        buckets, bias_table, score_scale,
    )
    near, over, far, query_cross = lax.optimization_barrier((near, over, far, query_cross))
    column = [shard, *near]
    for rows in far:
        column += [rows] + [at.shift(rows, l=l) for l in range(1, at.low)]
    encoded = [column] + [[first] + [at.shift(rows, x=x + 1) for rows in column[1:]] for x, first in enumerate(over)]
    sources, states, state = [], [], []
    for k, part in enumerate(encoded):
        *source, rows = key_value(part, own, cross_key, cross_value, enc_rows, doc_count)
        sources.append(source)
        states.append(rows)
        state = cross_forward(query_cross, mark, source, state, k == len(encoded) - 1, score_scale)
    mixed_cross, out_cross, extended = state
    (
        after_cross, activated, resid_grad, branch_cross, mixed_grad, gain_ffn_grad,
        in_keep, in_send, out_keep, out_send,
    ) = feed_forward(at, after_self, out_cross, cross_out, gain_ffn, ff_in, ff_out, cotangent[0])
    ff_out_sum = Reduction(at, out_keep, out_send, "yxlh")
    ff_in_sum = Reduction(at, in_keep, in_send, "xylh")

    pairs = width // LANES
    cut = pairs // 3
    mark = gate(out_send, in_send)
    begun = cross_backward(mark, extended, mixed_grad, mixed_cross, sources, 0, cut, [], score_scale)
    mark = gate(advance(begun[0], ff_out_sum, ff_in_sum))
    query_grad, *grads = cross_backward(
        mark, extended, mixed_grad, mixed_cross, sources, cut, pairs - cut, begun, score_scale
    )
    mark = gate(advance(query_grad, ff_out_sum, ff_in_sum))

    if len(states) * states[0].shape[0] <= FUSED_ROWS:
        shares, cross_keep, cross_send = cross_close(
            mark, at, normed_two, query_grad, out_cross, branch_cross, states, grads, cross_key, cross_value
        )
    else:
        shares = [encoder_part(mark, at, grads[2 * x : 2 * x + 2], cross_key, cross_value) for x in range(at.nx)]
        summed = lambda side: sum(dot(rows, grads[2 * x + side], TN) for x, rows in enumerate(states))
        cross_keep, cross_send = laid_out(
            at, [dot(normed_two, query_grad, TN), dot(out_cross, branch_cross, TN), summed(0), summed(1)]
        )
    early = [at.shift(part[0], x=-1 - k) for k, part in enumerate(shares[1:])]
    late = [at.shift(part[1], x=-1 - k) for k, part in enumerate(shares[1:])]
    cross_sum = Reduction(at, cross_keep, cross_send, "yxlh")
    mark = gate(advance(cross_keep, ff_out_sum, ff_in_sum, together=True))
    mark = gate(shares[1:], cross_send, advance(mark, cross_sum))

    input_grad, branch_self, *self_grads, extra = self_backward(
        mark, at.seq, query_grad, cross_query, after_self, gain_cross, resid_grad, decoder_in[0], gain_self,
        gain_ffn_grad, query_self, key_self, value_self, self_out, self_query, self_key, self_value,
        buckets, bias_table, score_scale,
    )
    cross_ready = advance(input_grad, cross_sum)
    (ready,) = totals(cross_ready[0], [[[Term(part, "h") for part in (shares[0][0], *early)]]])
    high_terms = [Term(part, "h") for part in (shares[0][1], *late, at.shift(ready, l=-1))]
    mark = gate(cross_ready, ready, advance(ready, ff_out_sum, ff_in_sum, together=True))
    first_keep, first_send, second_keep, second_send = weight_grads(
        mark,
        at,
        [[(normed_one, grad)] for grad in self_grads] + [[(out_self, branch_self)]],
        [[0], [1]],
        extra,
    )
    first_sum = Reduction(at, first_keep, first_send, "yxlh")
    second_sum = Reduction(at, second_keep, second_send, SECOND)
    mark = gate(first_send, second_send)

    n, m = width // at.dp, width // at.seq
    ready = advance(mark, first_sum, second_sum)
    cross_ready = advance(ready[0], cross_sum)
    high_ready = totals(cross_ready[0], [[[term.at("h", h) for term in high_terms]] for h in range(1, at.high)])
    last_terms = [term.at("h", 0) for term in high_terms] + [
        Term(at.shift(piece, h=-1 - k), "") for k, piece in enumerate(high_ready)
    ]
    mark = gate(ready, cross_ready, high_ready)
    ff_out_grad, ff_in_grad = final(
        mark, at, [ff_out_sum, ff_in_sum], [["rows"], ["plain"]],
        [(ff_out.shape[0] // at.seq, n), (m, ff_in.shape[1] // at.dp)], head_count,
    )
    activated, mark = lax.optimization_barrier((activated, mark))
    output = (after_cross + dot(activated, ff_out, NN)).astype(half)
    cross_ready = advance(ff_in_grad, cross_sum)
    mark = gate(output, cross_ready, advance(cross_ready[0], first_sum, second_sum))
    small = (m, n)
    cross_query_grad, cross_out_grad, cross_key_grad, cross_value_grad = final(
        mark, at, [cross_sum], [["pair", "pair"]], [small] * 4, head_count
    )
    (encoder_grad,) = totals(cross_value_grad, [[last_terms]], full)
    mark = gate(encoder_grad, advance(encoder_grad, first_sum, second_sum, together=True))
    mark = gate(advance(mark, first_sum, second_sum, together=True))
    query_grad, key_grad, value_grad, out_grad, *gains, bias_grad = final(
        mark, at, [first_sum, second_sum], [["pair"], ["pair", "extra"]],
        [small] * 4 + [(1, m)] * 3 + [(bucket_count // at.seq, head_count)], head_count,
    )
    return (
        output[None],
        input_grad[None],
        encoder_grad[None],
        *(gain.reshape(-1) for gain in gains),
        query_grad,
        key_grad,
        value_grad,
        out_grad,
        bias_grad,
        cross_query_grad,
        cross_key_grad,
        cross_value_grad,
        cross_out_grad,
        ff_in_grad,
        ff_out_grad,
    )


def solution(mesh):
    placed = (
        P("dp", "seq", None),
        P("dp", "seq", None),
        P("dp", "seq"),
        P("dp", None),
        P("dp", "seq", None),
    ) + (P(),) * 14
    return jax.shard_map(
        functools.partial(shards, dp_size=mesh.shape["dp"], seq_size=mesh.shape["seq"]),
        mesh=mesh,
        in_specs=placed,
        out_specs=(
            P("dp", "seq", None),
            P("dp", "seq", None),
            P("dp", "seq", None),
            P("seq"),
            P("seq"),
            P("seq"),
            P("seq", "dp"),
            P("seq", "dp"),
            P("seq", "dp"),
            P("seq", "dp"),
            P("seq", None),
            P("seq", "dp"),
            P("seq", "dp"),
            P("seq", "dp"),
            P("seq", "dp"),
            P("seq", "dp"),
            P("seq", "dp"),
        ),
        check_vma=False,
    )
```

```python
import functools
import itertools
import math

import jax
import jax.numpy as jnp
import numpy as np
from jax import lax
from jax.experimental import pallas as pl
from jax.experimental.pallas import tpu as pltpu
from jax.sharding import PartitionSpec as P

MAX_REACH = 128
DEC_LEN = 128


epsilon = 1e-06
masked_fill = -1e30
half = jnp.bfloat16
full = jnp.float32


def bucket_map(length, buckets, max_reach):
    exact_span = buckets // 2
    places = np.arange(length)
    distance = places[None, :] - places[:, None]
    passed = np.zeros_like(distance)
    for threshold_index in range(1, buckets - exact_span):
        threshold = int(
            math.ceil(
                exact_span * (max_reach / exact_span) ** (threshold_index / (buckets - exact_span))
            )
        )
        passed = passed + (distance >= threshold)
    bucket_of = np.where(distance < exact_span, distance, exact_span + passed)
    return np.where(distance < 0, -1, bucket_of).astype(np.int32)


def norm_parts(values):
    inverse = lax.rsqrt(jnp.mean(values * values, axis=-1, keepdims=True) + epsilon)
    return values * inverse, inverse


def norm_backward(upstream, normal, inverse, gain_row):
    scaled = upstream * gain_row
    inner = jnp.mean(scaled * normal, axis=-1, keepdims=True)
    return inverse * (scaled - normal * inner), jnp.sum(upstream * normal, axis=0, keepdims=True)


NT = (((1,), (1,)), ((), ()))
NN = (((1,), (0,)), ((), ()))
TN = (((0,), (0,)), ((), ()))
LANES = 128
ONES = 8
MEGA = 2**20
PAIRS = 2
FUSED_ROWS = 2048
SECOND = "xylh"


def dot(left_side, right_side, dims):
    return lax.dot_general(left_side, right_side, dims, preferred_element_type=full)


def three(value):
    first = value.astype(half).astype(full)
    second = (value - first).astype(half).astype(full)
    return first, second, (value - first - second).astype(half).astype(full)


def placed_three(value, index, rest):
    first, second, third = three(value)
    return jnp.where(
        index == ONES, first, jnp.where(index == ONES + 1, second, jnp.where(index == ONES + 2, third, rest))
    )


def low_lanes(rows):
    return lax.broadcasted_iota(jnp.int32, (rows, LANES), 1) < LANES // 2


def stacked(value, low):
    zero = jnp.zeros_like(value)
    return jnp.concatenate([jnp.where(low, value, zero), jnp.where(low, zero, value)], axis=0)


def loop(count, step, start):
    return lax.fori_loop(0, count, step, start, unroll=count <= 4)


light = pl.CostEstimate(flops=1, bytes_accessed=1, transcendentals=0)


def params(megabytes):
    return pltpu.CompilerParams(vmem_limit_bytes=megabytes * MEGA)


def whole(shape):
    return pl.BlockSpec(shape, lambda *_: (0,) * len(shape))


anywhere = pl.BlockSpec(memory_space=pl.ANY)


class Blocks:
    def __init__(self, at):
        self.core, self.ny, self.nx, self.dp, self.seq = at.core, at.ny, at.nx, at.dp, at.seq
        self.high, self.low = at.high, at.low

    def shape(self, rows, columns):
        return (self.ny, self.nx, self.high, self.low, rows, columns)

    def row_place(self, block, place):
        z = lax.div(block, self.nx)
        return (
            lax.rem(lax.rem(block, self.nx) - place[2] + self.nx, self.nx),
            lax.rem(lax.div(z, self.low) - place[3] + self.high, self.high),
            lax.rem(lax.rem(z, self.low) - place[4] + self.low, self.low),
        )

    def column_place(self, y, place):
        return lax.rem(y - place[0] + self.ny, self.ny)

    def paired(self, first, second, place):
        n = first.shape[1] // self.core
        if self.core == 1:
            return jnp.concatenate([first, second], axis=1).astype(half), None
        mine = place[1] == 0
        if n % LANES != LANES // 2:
            cut = [jnp.concatenate([g[:, c * n : (c + 1) * n] for g in (first, second)], axis=1) for c in range(2)]
        else:
            main = n - LANES // 2
            low = lax.broadcasted_iota(jnp.int32, (first.shape[0], LANES), 1) < LANES // 2
            one, two = (g[:, main : main + LANES] for g in (first, second))
            sides = (
                jnp.where(low, one, pltpu.roll(two, LANES // 2, 1)),
                jnp.where(low, pltpu.roll(one, LANES // 2, 1), two),
            )
            cut = [
                jnp.concatenate([first[:, at : at + main], second[:, at : at + main], sides[c]], axis=1)
                for c, at in enumerate((0, main + LANES))
            ]
        return jnp.where(mine, cut[0], cut[1]).astype(half), jnp.where(mine, cut[1], cut[0]).astype(half)


def unpaired(piece, core):
    n = piece.shape[1] // 2
    if n % LANES != LANES // 2:
        return piece[:, :n], piece[:, n:]
    main = n - LANES // 2
    side = piece[:, 2 * main :]
    turned = pltpu.roll(side, LANES // 2, 1)
    out = []
    for k in range(2):
        big = piece[:, k * main : (k + 1) * main]
        first, second = (side, turned) if k == 0 else (turned, side)
        after = jnp.concatenate([big, first], axis=1)
        ahead = pltpu.roll(jnp.concatenate([big, second], axis=1), LANES // 2, 1)
        out.append(jnp.where(core == 0, after, ahead)[:, :n])
    return out


def position_bias(buckets, table, pair):
    out = []
    for head in range(2):
        bias = jnp.full(buckets.shape, masked_fill, full)
        for b in range(table.shape[0]):
            bias = jnp.where(buckets == b, table[b, 2 * pair + head], bias)
        out.append(bias)
    return jnp.concatenate(out, axis=1)


def self_forward_kernel(
    hidden, gain_one, gain_two, weights_q, weights_k, weights_v, weights_o, weights_c, buckets, table,
    query, key, value, mixed, after, normed_two, query_cross, normed, every, *, scale,
):
    step = pl.program_id(0)
    rows = hidden.shape[0]

    @pl.when(step == 0)
    def _():
        normal, _ = norm_parts(hidden[...].astype(full))
        normed[...] = (normal * gain_one[...]).astype(half)

    many = query.shape[1] // LANES
    wide = many * LANES
    weights = jnp.concatenate([weights_q[...], weights_k[...], weights_v[...]], axis=1)
    made = dot(normed[...], weights, NN).astype(half)
    query[...] = made[:, :wide] * scale
    key[...] = made[:, wide : 2 * wide]
    value[...] = made[:, 2 * wide :]
    low = low_lanes(DEC_LEN)
    bias = [position_bias(buckets[...], table, step * many + pair) for pair in range(many)]
    work = [
        (pair, slice(pair * LANES, (pair + 1) * LANES), pl.ds(first, DEC_LEN))
        for pair in range(many)
        for first in range(0, rows, DEC_LEN)
    ]
    scores = [dot(key[at, own], stacked(query[at, own], low), NT) + bias[pair] for pair, own, at in work]
    expos = []
    for score in scores:
        expo = jnp.exp(score - jnp.max(score, axis=0, keepdims=True))
        expos.append((expo / jnp.sum(expo, axis=0, keepdims=True)).astype(half))
    for (pair, own, at), expo in zip(work, expos):
        both = dot(value[at, own], expo, TN).T
        one = jnp.where(low, both[:DEC_LEN], both[DEC_LEN:]).astype(half)
        mixed[at, own] = one
        every[at, pl.ds(pl.multiple_of(step * wide + pair * LANES, LANES), LANES)] = one

    @pl.when(step == pl.num_programs(0) - 1)
    def _():
        total = hidden[...].astype(full) + dot(every[...], weights_o[...], NN)
        after[...] = total
        normal, _ = norm_parts(total)
        again = (normal * gain_two[...]).astype(half)
        normed_two[...] = again
        query_cross[...] = dot(again, weights_c[...], NN).astype(half)


def self_forward(mark, hidden, gain_one, gain_two, weights_q, weights_k, weights_v, weights_o, weights_c, buckets, table, scale):
    rows, width = hidden.shape
    pairs = width // LANES
    many = PAIRS
    column = lambda i: (0, i)
    row_block = pl.BlockSpec((rows, many * LANES), column)
    weight_block = pl.BlockSpec((width, many * LANES), column)
    return pl.pallas_call(
        marked(functools.partial(self_forward_kernel, scale=scale)),
        name="self_forward",
        grid=(pairs // many,),
        in_specs=[anywhere, whole((rows, width)), whole((1, width)), whole((1, width))]
        + [weight_block] * 3
        + [whole((width, width))] * 2
        + [whole((DEC_LEN, DEC_LEN)), pl.BlockSpec(memory_space=pltpu.SMEM)],
        out_specs=[row_block] * 4 + [whole((rows, width))] * 4,
        out_shape=[jax.ShapeDtypeStruct((rows, width), half)] * 4
        + [jax.ShapeDtypeStruct((rows, width), kind) for kind in (full, half, half, half)],
        scratch_shapes=[pltpu.VMEM((rows, width), half)],
        compiler_params=params(56),
        cost_estimate=light,
    )(mark, hidden, gain_one, gain_two, weights_q, weights_k, weights_v, weights_o, weights_c, buckets, table)


def key_value_kernel(*refs, rows, doc_count):
    shards, (own, weights_k, weights_v, keys, values, mask, states) = refs[:-7], refs[-7:]
    for i, shard in enumerate(shards):
        at = pl.ds(i * rows, rows)
        states[at, :] = shard[:rows, :]
        keys[at, :] = dot(shard[:rows, :], weights_k[...], NN).astype(half)
        values[at, :] = dot(shard[:rows, :], weights_v[...], NN).astype(half)
        docs = shard[rows : rows + 1, :rows].astype(full)
        lane = lax.broadcasted_iota(jnp.int32, (LANES, rows), 0)
        ones = ((lane >= ONES) & (lane < ONES + 3)).astype(full)
        extra = jnp.where(lane < doc_count, jnp.where(docs == own[:, :1], 0.0, masked_fill), ones)
        mask[at, :] = extra.T.astype(half)


def key_value(shards, own, weights_k, weights_v, rows, doc_count):
    width = shards[0].shape[1]
    count = len(shards) * rows
    return pl.pallas_call(
        functools.partial(key_value_kernel, rows=rows, doc_count=doc_count),
        name="key_value",
        out_shape=[jax.ShapeDtypeStruct((count, size), half) for size in (width, width, LANES, width)],
        compiler_params=params(56),
        cost_estimate=light,
    )(*shards, own, weights_k, weights_v)


def cross_forward_kernel(*refs, scale, block, opens, closes):
    query, mark, keys, values, mask = refs[:5]
    refs = refs[5:]
    if not opens:
        state_in, refs = refs[:2], refs[2:]
    if closes:
        (mixed, mixed_half, extended), refs = refs[:3], refs[3:]
    else:
        state_out, refs = refs[:2], refs[2:]
    total, wide = refs
    rows, many = query.shape[0], query.shape[1] // LANES
    low = low_lanes(rows)
    for pair in range(many):
        wide[pair, :, :LANES] = stacked(query[:, pair * LANES : (pair + 1) * LANES] * scale, low)
        wide[pair, :rows, LANES:] = mark[...]
        wide[pair, rows:, LANES:] = mark[...]
    if opens:
        total[...] = jnp.zeros_like(total)
        carry = [(jnp.full((1, 2 * rows), masked_fill, full), jnp.zeros((1, 2 * rows), full)) for _ in range(many)]
    else:
        total[...] = state_in[0][...]
        carry = [(state_in[1][pair, 0:1], state_in[1][pair, 1:2]) for pair in range(many)]

    def step(i, carry):
        at = pl.ds(pl.multiple_of(i * block, block), block)
        scores = [
            dot(jnp.concatenate([keys[at, pair * LANES : (pair + 1) * LANES], mask[at, :]], axis=1), wide[pair], NT)
            for pair in range(many)
        ]
        out = []
        for pair, (peak, amount) in enumerate(carry):
            fresh = jnp.maximum(peak, jnp.max(scores[pair], axis=0, keepdims=True))
            expo = jnp.exp(scores[pair] - fresh)
            fade = jnp.exp(peak - fresh)
            values_here = values[at, pair * LANES : (pair + 1) * LANES]
            total[pair] = total[pair] * fade + dot(values_here, expo.astype(half), TN)
            out.append((fresh, amount * fade + jnp.sum(expo, axis=0, keepdims=True)))
        return out

    carry = loop(keys.shape[0] // block, step, carry)
    if not closes:
        state_out[0][...] = total[...]
        for pair, (peak, amount) in enumerate(carry):
            state_out[1][pair, 0:1] = peak
            state_out[1][pair, 1:2] = amount
        return
    index = lax.broadcasted_iota(jnp.int32, (LANES, 2 * rows), 0)
    for pair, (peak, amount) in enumerate(carry):
        at = slice(pair * LANES, (pair + 1) * LANES)
        both = (total[pair] / amount).T
        one = jnp.where(low, both[:rows], both[rows:])
        mixed[:, at] = one
        mixed_half[:, at] = one.astype(half)
        extra = placed_three(-(peak + jnp.log(amount)), index, 0.0).T
        extended[pair, :, :LANES] = wide[pair, :, :LANES]
        extended[pair, :, LANES:] = (wide[pair, :, LANES:].astype(full) + extra).astype(half)


def cross_forward(query, mark, source, state, closes, scale):
    rows, pairs, many = query.shape[0], query.shape[1] // LANES, PAIRS
    count = source[0].shape[0]
    column = lambda i: (0, i)
    plane = lambda i: (i, 0, 0)
    block = min(1024, count)
    state_specs = [pl.BlockSpec((many, LANES, 2 * rows), plane), pl.BlockSpec((many, 2, 2 * rows), plane)]
    state_shape = [
        jax.ShapeDtypeStruct((pairs, LANES, 2 * rows), full),
        jax.ShapeDtypeStruct((pairs, 2, 2 * rows), full),
    ]
    last_specs = [pl.BlockSpec((rows, many * LANES), column)] * 2 + [pl.BlockSpec((many, 2 * rows, 2 * LANES), plane)]
    last_shape = [
        jax.ShapeDtypeStruct(query.shape, full),
        jax.ShapeDtypeStruct(query.shape, half),
        jax.ShapeDtypeStruct((pairs, 2 * rows, 2 * LANES), half),
    ]
    return pl.pallas_call(
        functools.partial(cross_forward_kernel, scale=scale, block=block, opens=not state, closes=closes),
        name="cross_forward",
        grid=(pairs // many,),
        in_specs=[pl.BlockSpec((rows, many * LANES), column), whole((rows, LANES))]
        + [pl.BlockSpec((count, many * LANES), column), pl.BlockSpec((count, many * LANES), column), whole((count, LANES))]
        + (state_specs if state else []),
        out_specs=last_specs if closes else state_specs,
        out_shape=last_shape if closes else state_shape,
        scratch_shapes=[
            pltpu.VMEM((many, LANES, 2 * rows), full),
            pltpu.VMEM((many, 2 * rows, 2 * LANES), half),
        ],
        compiler_params=params(56),
        cost_estimate=light,
    )(query, mark, *source, *state)


def cross_backward_kernel(*refs, scale, block, parts):
    extended, upstream, mixed = refs[:3]
    sources = [refs[3 + 3 * i : 6 + 3 * i] for i in range(parts)]
    query_grad = refs[3 + 3 * parts]
    grads = [refs[4 + 3 * parts + 2 * i : 6 + 3 * parts + 2 * i] for i in range(parts)]
    wide, total = refs[-2:]
    rows = upstream.shape[0]
    low = low_lanes(rows)
    lane = lax.broadcasted_iota(jnp.int32, (rows, LANES), 1)
    each = upstream[...].astype(full) * mixed[...]
    wide[:, :LANES] = stacked(upstream[...], low)
    for head in range(2):
        inner = jnp.sum(jnp.where(low == (head == 0), each, 0.0), axis=1, keepdims=True)
        wide[head * rows : (head + 1) * rows, LANES:] = placed_three(-inner, lane, 0.0).astype(half)
    total[...] = jnp.zeros_like(total)
    for (keys, values, mask), (key_grad, value_grad) in zip(sources, grads):

        def step(i, carry):
            at = pl.ds(pl.multiple_of(i * block, block), block)
            extra = mask[at, :]
            expo = jnp.exp(dot(jnp.concatenate([keys[at, :], extra], axis=1), extended[0], NT))
            change = dot(jnp.concatenate([values[at, :], extra], axis=1), wide[...], NT)
            score = (expo * change).astype(half)
            value_grad[at, :] = dot(expo.astype(half), wide[:, :LANES], NN).astype(half)
            key_grad[at, :] = dot(score, extended[0, :, :LANES], NN).astype(half)
            total[...] += dot(keys[at, :], score, TN)
            return carry

        loop(keys.shape[0] // block, step, 0)
    both = total[...].T
    query_grad[...] = (jnp.where(low, both[:rows], both[rows:]) * scale).astype(half)


def cross_backward(mark, extended, upstream, mixed, sources, first, pairs, begun, scale):
    rows, width = upstream.shape
    count = sources[0][0].shape[0]
    every = count * len(sources)
    column = lambda i: (0, i + first)
    block = min(1024, count)
    row_block, key_block = pl.BlockSpec((rows, LANES), column), pl.BlockSpec((count, LANES), column)
    operands = [extended, upstream, mixed, *[array for source in sources for array in source]]
    kernel = functools.partial(cross_backward_kernel, scale=scale, block=block, parts=len(sources))
    return pl.pallas_call(
        marked(lambda *refs: kernel(*refs[len(begun) :]), len(begun)),
        name="cross_backward",
        grid=(pairs,),
        in_specs=[anywhere] * (len(begun) + 1)
        + [pl.BlockSpec((1, 2 * rows, 2 * LANES), lambda i: (i + first, 0, 0)), row_block, row_block]
        + [key_block, key_block, whole((count, LANES))] * len(sources),
        out_specs=[row_block] + [key_block] * (2 * len(sources)),
        out_shape=[jax.ShapeDtypeStruct((rows, width), half)]
        + [jax.ShapeDtypeStruct((count, width), half)] * (2 * len(sources)),
        scratch_shapes=[
            pltpu.VMEM((2 * rows, 2 * LANES), half),
            pltpu.VMEM((LANES, 2 * rows), full),
        ],
        input_output_aliases={i: i for i in range(len(begun))},
        compiler_params=params(56),
        cost_estimate=light,
    )(*begun, mark, *operands)


def feed_forward_kernel(
    place, after, mixed, weights_o, gain, weights_in, weights_out, cotangent,
    after_cross, activated, resid, branch, mixed_grad, gain_grad, in_keep, in_send, out_keep, out_send,
    normed, total, *, blocks,
):
    step = pl.program_id(0)

    @pl.when(step == 0)
    def _():
        values = after[...] + dot(mixed[...], weights_o[...], NN)
        after_cross[...] = values
        normal, _ = norm_parts(values)
        normed[...] = (normal * gain[...]).astype(half)
        total[...] = jnp.zeros_like(total)

    upstream = cotangent[...]
    pre = dot(normed[...], weights_in[...], NN)
    square = pre * pre
    slope = math.sqrt(2.0 / math.pi)
    bend = jnp.tanh(slope * (pre + 0.044715 * (square * pre)))
    act = (0.5 * pre * (1.0 + bend)).astype(half)
    activated[...] = act
    gelu_grad = 0.5 * (1.0 + bend) + 0.5 * pre * (1.0 - bend * bend) * (slope * (1.0 + 3 * 0.044715 * square))
    pre_grad = (dot(upstream, weights_out[...], NT) * gelu_grad).astype(half)
    total[...] += dot(pre_grad, weights_in[...], NT)

    grad = dot(normed[...], pre_grad, TN).astype(half)
    m = grad.shape[0] // blocks.seq
    to_y = blocks.column_place(lax.div(step, blocks.core), place)
    ours = lax.rem(step, blocks.core) == place[1]

    def fill(target):
        for block in range(blocks.seq):
            to_x, to_h, to_l = blocks.row_place(jnp.int32(block), place)
            target[to_y, to_x, to_h, to_l] = grad[block * m : (block + 1) * m]

    pl.when(ours)(lambda: fill(in_keep))
    pl.when(jnp.logical_not(ours))(lambda: fill(in_send))

    grad = dot(act, upstream, TN)
    wide = grad.shape[1] // blocks.ny
    n = wide // blocks.core
    pieces = out_keep.shape[5] // n
    many = pieces * m
    for y in range(blocks.ny):
        at = slice(y * wide, (y + 1) * wide)
        to_y = blocks.column_place(jnp.int32(y), place)
        for block in range(grad.shape[0] // many):
            to_x, to_h, to_l = blocks.row_place(step * (grad.shape[0] // many) + block, place)
            for piece in range(0, pieces, 2):
                first = block * many + piece * m
                kept, sent = blocks.paired(grad[first : first + m, at], grad[first + m : first + 2 * m, at], place)
                out_keep[to_y, to_x, to_h, to_l, :, piece * n : (piece + 2) * n] = kept
                if sent is not None:
                    out_send[to_y, to_x, to_h, to_l, :, piece * n : (piece + 2) * n] = sent

    @pl.when(step == pl.num_programs(0) - 1)
    def _():
        normal, inverse = norm_parts(after_cross[...])
        change, gain_sum = norm_backward(total[...], normal, inverse, gain[...])
        gain_grad[...] = gain_sum
        change = change + upstream.astype(full)
        resid[...] = change
        rounded = change.astype(half)
        branch[...] = rounded
        mixed_grad[...] = dot(rounded, weights_o[...], NT).astype(half)


def feed_forward(at, after, mixed, weights_o, gain, weights_in, weights_out, cotangent):
    rows, width = after.shape
    depth = weights_in.shape[1]
    blocks = Blocks(at)
    cut = depth // at.dp
    shape = blocks.shape(width // at.seq, cut)
    all_rows = whole((rows, width))
    sized = lambda kind: jax.ShapeDtypeStruct((rows, width), kind)
    return pl.pallas_call(
        functools.partial(feed_forward_kernel, blocks=blocks),
        name="feed_forward",
        grid_spec=pltpu.PrefetchScalarGridSpec(
            num_scalar_prefetch=1,
            grid=(at.dp,),
            in_specs=[
                all_rows,
                all_rows,
                whole((width, width)),
                whole((1, width)),
                pl.BlockSpec((width, cut), lambda i, _: (0, i)),
                pl.BlockSpec((cut, width), lambda i, _: (i, 0)),
                all_rows,
            ],
            out_specs=[all_rows, pl.BlockSpec((rows, cut), lambda i, _: (0, i))]
            + [all_rows] * 3
            + [whole((1, width))]
            + [whole(shape)] * 4,
            scratch_shapes=[pltpu.VMEM((rows, width), half), pltpu.VMEM((rows, width), full)],
        ),
        out_shape=[sized(full), jax.ShapeDtypeStruct((rows, depth), half), sized(full), sized(half), sized(half)]
        + [jax.ShapeDtypeStruct((1, width), full)]
        + [jax.ShapeDtypeStruct(shape, half)] * 4,
        compiler_params=params(56),
        cost_estimate=light,
    )(at.place, after, mixed, weights_o, gain, weights_in, weights_out, cotangent)


def encoder_part_kernel(key_grad, value_grad, weights_k, weights_v, early, late, *, early_steps):
    total = dot(key_grad[...], weights_k[...], NT) + dot(value_grad[...], weights_v[...], NT)
    is_early = pl.program_id(0) < early_steps

    @pl.when(is_early)
    def _():
        early[...] = total.astype(half)

    @pl.when(jnp.logical_not(is_early))
    def _():
        late[...] = total.astype(half)


def encoder_part(mark, at, grads, weights_k, weights_v):
    width = weights_k.shape[0]
    rows = grads[0].shape[0] // at.nz
    early = at.high * (at.low - 1)
    plane = lambda size: jax.ShapeDtypeStruct((size, rows, width), half)
    block = pl.BlockSpec((rows, width), lambda i: (i % at.high * at.low + at.low - 1 - i // at.high, 0))
    return pl.pallas_call(
        marked(functools.partial(encoder_part_kernel, early_steps=early)),
        name="encoder_part",
        grid=(at.nz,),
        in_specs=[anywhere, block, block, whole((width, width)), whole((width, width))],
        out_specs=[
            pl.BlockSpec((None, rows, width), lambda i: (jnp.minimum(i, early - 1), 0, 0)),
            pl.BlockSpec((None, rows, width), lambda i: (jnp.maximum(i - early, 0), 0, 0)),
        ],
        out_shape=[plane(early), plane(at.high)],
        compiler_params=params(56),
        cost_estimate=light,
    )(mark, *grads, weights_k, weights_v)


def weight_grads_kernel(place, *refs, blocks, counts, chunks, extra, wide):
    refs = list(refs)
    sides = [[(refs.pop(0), refs.pop(0)) for _ in range(count)] for count in counts]
    small = refs.pop(0) if extra else None
    made = [sum((dot(left[...], right[...], TN) for left, right in side[1:]), dot(side[0][0][...], side[0][1][...], TN)) for side in sides]
    m = made[0].shape[0] // blocks.seq
    many = made[0].shape[1] // wide
    for chunk, pairs in enumerate(chunks):
        keep, send = refs[2 * chunk], refs[2 * chunk + 1]
        for y in range(many):
            at = slice(y * wide, (y + 1) * wide)
            columns = [blocks.paired(made[2 * pair][:, at], made[2 * pair + 1][:, at], place) for pair in pairs]
            if extra and chunk == len(chunks) - 1:
                columns.append((small[...], small[...]))
            to_y = blocks.column_place(jnp.int32(y), place) if many > 1 else 0
            for block in range(blocks.seq):
                to_x, to_h, to_l = blocks.row_place(jnp.int32(block), place)
                rows = slice(block * m, (block + 1) * m)
                first = 0
                for ours, theirs in columns:
                    to = slice(first, first + ours.shape[1])
                    keep[to_y, to_x, to_h, to_l, :, to] = ours[rows]
                    send[to_y, to_x, to_h, to_l, :, to] = theirs[rows]
                    first += ours.shape[1]


def weight_grads(mark, at, sides, chunks, extra=None):
    blocks = Blocks(at)
    width = sides[0][0][0].shape[1]
    wide, m = width // at.ny, width // at.seq
    shapes = [blocks.shape(m, len(pairs) * 2 * wide // at.core) for pairs in chunks]
    if extra is not None:
        shapes[-1] = (*shapes[-1][:-1], shapes[-1][-1] + extra.shape[1])
    terms = [term for side in sides for term in side]
    steps = at.ny if wide % LANES == 0 else 1
    from_y = lambda i, place: (0, lax.rem(i + place[0], at.ny) if steps > 1 else 0)
    out_block = lambda shape: pl.BlockSpec((shape[0] // steps, *shape[1:]), lambda i, place: (i, 0, 0, 0, 0, 0))
    return pl.pallas_call(
        marked(
            functools.partial(
                weight_grads_kernel,
                blocks=blocks,
                counts=[len(side) for side in sides],
                chunks=chunks,
                extra=extra is not None,
                wide=wide,
            ),
            1,
        ),
        name="weight_grads",
        grid_spec=pltpu.PrefetchScalarGridSpec(
            num_scalar_prefetch=1,
            grid=(steps,),
            in_specs=[anywhere]
            + [
                spec
                for left, right in terms
                for spec in (whole(left.shape), pl.BlockSpec((right.shape[0], width // steps), from_y))
            ]
            + ([whole(extra.shape)] if extra is not None else []),
            out_specs=[out_block(shape) for shape in shapes for _ in range(2)],
        ),
        out_shape=[jax.ShapeDtypeStruct(shape, half) for shape in shapes for _ in range(2)],
        compiler_params=params(60),
        cost_estimate=light,
    )(at.place, mark, *[array for term in terms for array in term], *([extra] if extra is not None else []))


def laid_out(at, grads):
    out = []
    for grad in grads:
        m, n = grad.shape[0] // at.seq, grad.shape[1] // at.dp
        assert n % LANES != LANES // 2
        blocks = grad.astype(half).reshape(at.high, at.low, at.nx, m, at.ny, at.core, n)
        places = ((0, at.z // at.low, at.high), (1, at.z % at.low, at.low), (2, at.x, at.nx), (4, at.y, at.ny), (5, at.c, at.core))
        for axis, own, size in places:
            blocks = jnp.take(blocks, (own + jnp.arange(size)) % size, axis=axis)
        out.append(blocks.transpose(5, 4, 2, 0, 1, 3, 6))
    both = jnp.concatenate(out, axis=-1)
    return both[0], both[1]


def cross_close_kernel(place, *refs, blocks, parts):
    count = 3 * parts + 6
    arrays, refs = refs[:count], refs[count:]
    shares, (keep, send), refs = refs[: 2 * parts], refs[2 * parts : 2 * parts + 2], refs[2 * parts + 2 :]
    held, refs = refs[:count], refs[count:]
    made, (keep_held, send_held, arrived, gone) = refs[:parts], refs[parts:]
    ins = [pltpu.make_async_copy(array, place_held, arrived.at[i]) for i, (array, place_held) in enumerate(zip(arrays, held))]
    grads, (weights_k, weights_v), states = held[: 2 * parts], held[2 * parts : 2 * parts + 2], held[2 * parts + 2 : -4]
    normed, query_grad, mixed, branch = held[-4:]
    outs = []

    def leave(source, target):
        copy = pltpu.make_async_copy(source, target, gone.at[len(outs)])
        copy.start()
        outs.append(copy)

    order = [*range(1, parts), 0]
    first = [i for x in order[:1] for i in (2 * x, 2 * x + 1)] + [2 * parts, 2 * parts + 1]
    for i in first + [i for i in range(count) if i not in first]:
        ins[i].start()
    ins[2 * parts].wait()
    ins[2 * parts + 1].wait()
    rows = grads[0].shape[0] // (blocks.high * blocks.low)
    early_size = blocks.low - 1
    for x in order:
        ins[2 * x].wait()
        ins[2 * x + 1].wait()
        for block in range(blocks.high * blocks.low):
            at = slice(block * rows, (block + 1) * rows)
            total = dot(grads[2 * x][at, :], weights_k[...], NT) + dot(grads[2 * x + 1][at, :], weights_v[...], NT)
            made[x][at, :] = total.astype(half)
        for block in range(blocks.high * blocks.low):
            h, l = divmod(block, blocks.low)
            source = made[x].at[pl.ds(block * rows, rows), :]
            leave(source, shares[2 * x].at[(blocks.low - 1 - l) * blocks.high + h] if l else shares[2 * x + 1].at[h])

    def place_pair(one, two, offset):
        m, wide = one.shape[0] // blocks.seq, one.shape[1] // blocks.ny
        for y in range(blocks.ny):
            at = slice(y * wide, (y + 1) * wide)
            ours, theirs = blocks.paired(one[:, at], two[:, at], place)
            to_y = blocks.column_place(jnp.int32(y), place)
            to = slice(offset, offset + ours.shape[1])
            for block in range(blocks.seq):
                to_x, to_h, to_l = blocks.row_place(jnp.int32(block), place)
                own = slice(block * m, (block + 1) * m)
                keep_held[to_y, to_x, to_h, to_l, :, to] = ours[own]
                send_held[to_y, to_x, to_h, to_l, :, to] = theirs[own]
        for source, target in ((send_held, send), (keep_held, keep)):
            leave(source.at[:, :, :, :, :, to], target.at[:, :, :, :, :, to])

    n = keep_held.shape[5] // 4
    for copy in ins[2 * parts + 2 : -4]:
        copy.wait()
    total = []
    for kind in range(2):
        terms = [dot(states[x][...], grads[2 * x + kind][...], TN) for x in range(parts)]
        total.append(sum(terms[1:], terms[0]))
    place_pair(total[0], total[1], 2 * n)
    for copy in ins[-4:]:
        copy.wait()
    place_pair(dot(normed[...], query_grad[...], TN), dot(mixed[...], branch[...], TN), 0)
    for copy in outs:
        copy.wait()


def cross_close(mark, at, normed, query_grad, mixed, branch, states, grads, weights_k, weights_v):
    blocks, parts = Blocks(at), len(states)
    count, width = states[0].shape
    shape = blocks.shape(width // at.seq, 4 * width // at.dp)
    arrays = [*grads, weights_k, weights_v, *states, normed, query_grad, mixed, branch]
    plane = lambda size: jax.ShapeDtypeStruct((size, count // at.nz, width), half)
    outs = [plane(at.high * (at.low - 1)), plane(at.high)] * parts + [jax.ShapeDtypeStruct(shape, half)] * 2
    made = pl.pallas_call(
        marked(functools.partial(cross_close_kernel, blocks=blocks, parts=parts), 1),
        name="cross_close",
        in_specs=[pl.BlockSpec(memory_space=pltpu.SMEM)] + [anywhere] * (len(arrays) + 1),
        out_specs=[anywhere] * len(outs),
        out_shape=outs,
        scratch_shapes=[pltpu.VMEM(array.shape, half) for array in arrays]
        + [pltpu.VMEM((count, width), half)] * parts
        + [pltpu.VMEM(shape, half)] * 2
        + [pltpu.SemaphoreType.DMA((len(arrays),)), pltpu.SemaphoreType.DMA((parts * at.nz + 4,))],
        compiler_params=params(56),
        cost_estimate=light,
    )(at.place, mark, *arrays)
    return [made[2 * x : 2 * x + 2] for x in range(parts)], *made[-2:]


def self_backward_kernel(
    query_cross_grad, weights_c, after, gain_two, resid_in, hidden, gain_one, gain_ffn_grad,
    query, key, value, weights_ob, weights_q, weights_k, weights_v, buckets, table,
    input_grad, branch, query_grad, key_grad, value_grad, extra,
    resid, total, bias_rows, gain_two_grad, columns, *, scale, shares,
):
    step = pl.program_id(0)
    rows, width = hidden.shape

    @pl.when(step == 0)
    def _():
        normal, inverse = norm_parts(after[...])
        up = dot(query_cross_grad[...], weights_c[...], NT)
        change, gain_sum = norm_backward(up, normal, inverse, gain_two[...])
        gain_two_grad[...] = gain_sum
        change = change + resid_in[...]
        resid[...] = change
        branch[...] = change.astype(half)
        total[...] = jnp.zeros_like(total)

    low = low_lanes(DEC_LEN)
    many = query.shape[1] // LANES
    upstream = dot(branch[...], weights_ob[...], NT).astype(half)
    count = bias_rows.shape[1]
    of_pair = jnp.concatenate([buckets[...], buckets[...]], axis=1)
    work = [(pair, pl.ds(first, DEC_LEN)) for pair in range(many) for first in range(0, rows, DEC_LEN)]
    spans = [slice(pair * LANES, (pair + 1) * LANES) for pair in range(many)]
    bias = [position_bias(buckets[...], table, step * many + pair) for pair in range(many)]
    wides = [stacked(query[at, spans[pair]], low) for pair, at in work]
    up = [stacked(upstream[at.start : at.start + DEC_LEN, spans[pair]], low) for pair, at in work]
    scores = [dot(key[at, spans[pair]], wide, NT) + bias[pair] for (pair, at), wide in zip(work, wides)]
    changes = [dot(value[at, spans[pair]], grad, NT) for (pair, at), grad in zip(work, up)]
    summed = [None] * many
    for (pair, at), wide, grad, score, change in zip(work, wides, up, scores, changes):
        own = spans[pair]
        expo = jnp.exp(score - jnp.max(score, axis=0, keepdims=True))
        expo = expo / jnp.sum(expo, axis=0, keepdims=True)
        rounded = (expo * (change - jnp.sum(expo * change, axis=0, keepdims=True))).astype(half)
        both = dot(key[at, own], rounded, TN).T
        query_grad[at, own] = (jnp.where(low, both[:DEC_LEN], both[DEC_LEN:]) * scale).astype(half)
        key_grad[at, own] = dot(rounded, wide, NN).astype(half)
        value_grad[at, own] = dot(expo.astype(half), grad, NN).astype(half)
        summed[pair] = rounded.astype(full) if summed[pair] is None else summed[pair] + rounded.astype(full)
    made = jnp.concatenate([query_grad[...], key_grad[...], value_grad[...]], axis=1)
    total[...] += dot(made, jnp.concatenate([weights_q[...], weights_k[...], weights_v[...]], axis=1), NT)
    for pair in range(many):
        sums = [jnp.sum(jnp.where(of_pair == b, summed[pair], 0.0), axis=0, keepdims=True) for b in range(count)]
        bias_rows[step * many + pair] = jnp.concatenate(sums, axis=0)

    @pl.when(step == pl.num_programs(0) - 1)
    def _():
        normal, inverse = norm_parts(hidden[...].astype(full))
        change, gain_sum = norm_backward(total[...], normal, inverse, gain_one[...])
        input_grad[...] = resid[...] + change

        index = lax.broadcasted_iota(jnp.int32, (LANES, width), 0)
        gains = jnp.where(
            index == 0,
            gain_sum,
            jnp.where(index == 1, gain_two_grad[...], jnp.where(index == 2, gain_ffn_grad[...], 0.0)),
        )
        columns[...] = gains.T
        lane = lax.broadcasted_iota(jnp.int32, (count, LANES), 1)
        sums = jnp.zeros((count, LANES), full)
        for pair in range(bias_rows.shape[0]):
            for head in range(2):
                part = bias_rows[pair, :, head * LANES : (head + 1) * LANES]
                sums = jnp.where(lane == 16 + 2 * pair + head, jnp.sum(part, axis=1, keepdims=True), sums)
        m, each = width // shares, count // shares
        for block in range(shares):
            at = slice(block * m, block * m + each)
            columns[at, :] = columns[at, :] + sums[block * each : (block + 1) * each]
        extra[...] = columns[...].astype(half)


def self_backward(
    mark, shares, query_cross_grad, weights_c, after, gain_two, resid, hidden, gain_one, gain_ffn_grad,
    query, key, value, weights_o, weights_q, weights_k, weights_v, buckets, table, scale,
):
    rows, width = hidden.shape
    pairs, count = width // LANES, table.shape[0]
    many = PAIRS
    row_block = pl.BlockSpec((rows, many * LANES), lambda i: (0, i))
    weight_block = pl.BlockSpec((width, many * LANES), lambda i: (0, i))
    all_rows, line = whole((rows, width)), whole((1, width))
    sized = lambda kind: jax.ShapeDtypeStruct((rows, width), kind)
    return pl.pallas_call(
        marked(functools.partial(self_backward_kernel, scale=scale, shares=shares)),
        name="self_backward",
        grid=(pairs // many,),
        in_specs=[anywhere, all_rows, whole((width, width)), all_rows, line, all_rows, all_rows, line, line]
        + [row_block] * 3
        + [pl.BlockSpec((many * LANES, width), lambda i: (i, 0))]
        + [weight_block] * 3
        + [whole((DEC_LEN, DEC_LEN)), pl.BlockSpec(memory_space=pltpu.SMEM)],
        out_specs=[all_rows, all_rows] + [row_block] * 3 + [whole((width, LANES))],
        out_shape=[sized(full)] + [sized(half)] * 4 + [jax.ShapeDtypeStruct((width, LANES), half)],
        scratch_shapes=[
            pltpu.VMEM((rows, width), full),
            pltpu.VMEM((rows, width), full),
            pltpu.VMEM((pairs, count, 2 * DEC_LEN), full),
            pltpu.VMEM((1, width), full),
            pltpu.VMEM((width, LANES), full),
        ],
        compiler_params=params(56),
        cost_estimate=light,
    )(
        mark, query_cross_grad, weights_c, after, gain_two, resid, hidden, gain_one, gain_ffn_grad,
        query, key, value, weights_o, weights_q, weights_k, weights_v, buckets, table,
    )


class Places:
    def __init__(self, dp_size, seq_size):
        self.dp, self.seq = dp_size, seq_size
        self.core = 2 if dp_size % 2 == 0 else 1
        self.ny = dp_size // self.core
        self.nx = self.ny if seq_size % self.ny == 0 else 1
        self.nz = seq_size // self.nx
        self.low = 2 if self.nz % 2 == 0 else 1
        self.high = self.nz // self.low
        dp_index, seq_index = lax.axis_index("dp"), lax.axis_index("seq")
        self.c, self.y = dp_index % self.core, dp_index // self.core
        self.x, self.z = seq_index % self.nx, seq_index // self.nx
        self.place = jnp.stack([self.y, self.c, self.x, self.z // self.low, self.z % self.low]).astype(jnp.int32)

    def shift(self, value, **steps):
        sizes = {"y": self.ny, "c": self.core, "h": self.high, "l": self.low, "x": self.nx}
        flat = lambda p: ((p["y"] * self.core + p["c"]) * self.seq) + (p["h"] * self.low + p["l"]) * self.nx + p["x"]
        pairs = []
        for numbers in itertools.product(*[range(size) for size in sizes.values()]):
            here = dict(zip(sizes, numbers))
            there = {axis: (here[axis] + steps.get(axis, 0)) % size for axis, size in sizes.items()}
            pairs.append((flat(here), flat(there)))
        return lax.ppermute(value, ("dp", "seq"), pairs)


def gate_kernel(*refs):
    refs[-1][...] = jnp.zeros_like(refs[-1])


def gate(*waits):
    arrays = jax.tree.leaves(waits)
    return pl.pallas_call(
        gate_kernel,
        name="gate",
        in_specs=[pl.BlockSpec(memory_space=pl.ANY)] * len(arrays),
        out_shape=jax.ShapeDtypeStruct((8, LANES), full),
        cost_estimate=pl.CostEstimate(flops=10**13, bytes_accessed=10**10, transcendentals=0),
    )(*arrays)


def marked(kernel, scalars=0):
    return lambda *refs: kernel(*refs[:scalars], *refs[scalars + 1 :])


class Term:
    def __init__(self, array, axes, fixed=(), columns=None):
        self.array, self.axes, self.fixed = array, axes, dict(fixed)
        self.columns = columns or (0, array.shape[-1])

    def at(self, axis, place):
        return Term(self.array, self.axes, {**self.fixed, axis: place}, self.columns)

    def free(self):
        sizes = zip(self.axes, self.array.shape)
        return tuple(size for axis, size in sizes if axis not in self.fixed)

    def spec(self):
        shape = [None if axis in self.fixed else size for axis, size in zip(self.axes, self.array.shape)]
        places = [self.fixed.get(axis, 0) for axis in self.axes]
        return pl.BlockSpec((*shape, *self.array.shape[-2:]), lambda i: (*places, 0, 0))


def totals_kernel(*refs, jobs):
    refs = list(refs)
    sources, outs = refs[: -len(jobs)], refs[-len(jobs) :]
    for groups, out in zip(jobs, outs):
        first = 0
        for columns in groups:
            total = None
            for low, high in columns:
                value = sources.pop(0)[..., low:high].astype(full)
                total = value if total is None else total + value
            out[..., first : first + total.shape[-1]] = total.astype(out.dtype)
            first += total.shape[-1]


def totals(mark, jobs, kind=half):
    terms = [term for groups in jobs for group in groups for term in group]
    shape = lambda groups: (
        *groups[0][0].free(),
        groups[0][0].array.shape[-2],
        sum(group[0].columns[1] - group[0].columns[0] for group in groups),
    )
    return pl.pallas_call(
        marked(
            functools.partial(totals_kernel, jobs=[[[term.columns for term in group] for group in groups] for groups in jobs])
        ),
        name="totals",
        grid=(1,),
        in_specs=[anywhere] + [term.spec() for term in terms],
        out_specs=[whole(shape(groups)) for groups in jobs],
        out_shape=[jax.ShapeDtypeStruct(shape(groups), kind) for groups in jobs],
        compiler_params=params(56),
        cost_estimate=light,
    )(mark, *[term.array for term in terms])


def final_kernel(place, *refs, terms, shapes, head_count):
    refs = list(refs)
    sources, outs = refs[: sum(len(columns) for columns in terms)], refs[sum(len(columns) for columns in terms) :]
    for columns, holds in zip(terms, shapes):
        total = None
        for low, high in columns:
            value = sources.pop(0)[..., low:high].astype(full)
            total = value if total is None else total + value
        first = 0
        for hold in holds:
            if hold == "plain":
                outs.pop(0)[...] = total
            elif hold == "pair":
                wide = outs[0].shape[1] * 2
                for out, value in zip(outs[:2], unpaired(total[:, first : first + wide], place[1])):
                    out[...] = value
                outs, first = outs[2:], first + wide
            elif hold == "rows":
                out, m = outs.pop(0), total.shape[0]
                wide = out.shape[1]
                for piece in range(0, out.shape[0] // m, 2):
                    two = unpaired(total[:, piece * wide : (piece + 2) * wide], place[1])
                    out[piece * m : (piece + 1) * m, :] = two[0]
                    out[(piece + 1) * m : (piece + 2) * m, :] = two[1]
            else:
                turned = total[:, first:].T
                for k in range(3):
                    outs.pop(0)[...] = turned[k : k + 1, :]
                bias = outs.pop(0)
                bias[...] = pltpu.roll(total[:, first:], LANES - 16, 1)[: bias.shape[0], :head_count]


def final(mark, at, sums, holds, shapes, head_count):
    terms = [part.terms for part in sums]
    arrays = [term for group in terms for term in group]
    as_prefetch = lambda spec: pl.BlockSpec(spec.block_shape, lambda i, _, index=spec.index_map: index(i))
    return pl.pallas_call(
        marked(
            functools.partial(
                final_kernel,
                terms=[[term.columns for term in group] for group in terms],
                shapes=holds,
                head_count=head_count,
            ),
            1,
        ),
        name="final",
        grid_spec=pltpu.PrefetchScalarGridSpec(
            num_scalar_prefetch=1,
            grid=(1,),
            in_specs=[anywhere] + [as_prefetch(term.spec()) for term in arrays],
            out_specs=[whole(shape) for shape in shapes],
        ),
        out_shape=[jax.ShapeDtypeStruct(shape, full) for shape in shapes],
        compiler_params=params(56),
        cost_estimate=light,
    )(at.place, mark, *[term.array for term in arrays])


class Reduction:
    def __init__(self, at, keep, send, order):
        self.at, self.order = at, order
        self.terms = [Term(keep, "yxhl")]
        if at.core == 2:
            self.terms.append(Term(at.shift(send, c=1), "yxhl"))
        self.left = "yxhl"


def advance(mark, *sums, together=False):
    at = sums[0].at
    axes = [part.order[0] for part in sums]
    size = lambda axis: {"y": at.ny, "x": at.nx, "h": at.high, "l": at.low}[axis]
    group = lambda part, k: [term.at(part.order[0], k) for term in part.terms]
    if together:
        places = [(axes[0], k) for k in range(1, size(axes[0]))]
        jobs = [[group(part, k) for part in sums] for _, k in places]
    else:
        places = [(axis, k) for axis in axes for k in range(1, size(axis))]
        jobs = [[group(part, k)] for part, axis in zip(sums, axes) for k in range(1, size(axis))]
    pieces = list(totals(mark, jobs)) if jobs else []
    got = [at.shift(piece, **{axis: k}) for piece, (axis, k) in zip(pieces, places)]
    first = 0
    for part in sums:
        axis, part.order = part.order[0], part.order[1:]
        part.left = part.left.replace(axis, "")
        part.terms = [term.at(axis, 0) for term in part.terms]
        wide = part.terms[0].columns[1] - part.terms[0].columns[0]
        for _ in range(1, size(axis)):
            if together:
                continue
            part.terms.append(Term(got.pop(0), part.left))
        if together:
            part.terms += [Term(piece, part.left, (), (first, first + wide)) for piece in got]
            first += wide
    return pieces


def shards(
    decoder_in,
    encoder_states,
    encoder_doc,
    decoder_doc,
    cotangent,
    gain_self,
    gain_cross,
    gain_ffn,
    self_query,
    self_key,
    self_value,
    self_out,
    bias_table,
    cross_query,
    cross_key,
    cross_value,
    cross_out,
    ff_in,
    ff_out,
    *,
    dp_size,
    seq_size,
):
    at = Places(dp_size, seq_size)
    width = decoder_in.shape[2]
    head_count = bias_table.shape[1]
    bucket_count = bias_table.shape[0]
    score_scale = (width // head_count) ** (-0.5)
    local_rows = decoder_in.shape[1]
    doc_count = local_rows // DEC_LEN
    position = lax.axis_index("seq")
    own_map = lax.dynamic_slice_in_dim(decoder_doc[0], position * doc_count, doc_count, 0)
    gain_self, gain_cross, gain_ffn = (gain[None, :] for gain in (gain_self, gain_cross, gain_ffn))

    enc_rows = encoder_states.shape[1]
    docs = jnp.pad(encoder_doc.astype(half), ((0, 15), (0, width - enc_rows)))
    shard = jnp.concatenate([encoder_states[0], docs], axis=0)
    near = [at.shift(shard, l=l) for l in range(1, at.low)]
    over = [at.shift(shard, x=x) for x in range(1, at.nx)]
    far = [at.shift(shard, h=h) for h in range(1, at.high)]
    mark = gate(shard)
    own = jnp.pad(own_map.astype(full), (0, LANES - doc_count))[:, None]
    lane = jnp.arange(LANES, dtype=jnp.int32)
    mark = (jnp.arange(local_rows, dtype=jnp.int32)[:, None] // DEC_LEN == lane).astype(half)
    buckets = jnp.asarray(bucket_map(DEC_LEN, bucket_count, MAX_REACH))

    query_self, key_self, value_self, out_self, after_self, normed_two, query_cross, normed_one = self_forward(
        mark, decoder_in[0], gain_self, gain_cross, self_query, self_key, self_value, self_out, cross_query,
        buckets, bias_table, score_scale,
    )
    near, over, far, query_cross = lax.optimization_barrier((near, over, far, query_cross))
    column = [shard, *near]
    for rows in far:
        column += [rows] + [at.shift(rows, l=l) for l in range(1, at.low)]
    encoded = [column] + [[first] + [at.shift(rows, x=x + 1) for rows in column[1:]] for x, first in enumerate(over)]
    sources, states, state = [], [], []
    for k, part in enumerate(encoded):
        *source, rows = key_value(part, own, cross_key, cross_value, enc_rows, doc_count)
        sources.append(source)
        states.append(rows)
        state = cross_forward(query_cross, mark, source, state, k == len(encoded) - 1, score_scale)
    mixed_cross, out_cross, extended = state
    (
        after_cross, activated, resid_grad, branch_cross, mixed_grad, gain_ffn_grad,
        in_keep, in_send, out_keep, out_send,
    ) = feed_forward(at, after_self, out_cross, cross_out, gain_ffn, ff_in, ff_out, cotangent[0])
    ff_out_sum = Reduction(at, out_keep, out_send, "yxlh")
    ff_in_sum = Reduction(at, in_keep, in_send, "xylh")

    pairs = width // LANES
    cut = 1
    mark = gate(out_send, in_send)
    begun = cross_backward(mark, extended, mixed_grad, mixed_cross, sources, 0, cut, [], score_scale)
    mark = gate(advance(begun[0], ff_out_sum, ff_in_sum))
    query_grad, *grads = cross_backward(
        mark, extended, mixed_grad, mixed_cross, sources, cut, pairs - cut, begun, score_scale
    )
    mark = gate(advance(query_grad, ff_out_sum, ff_in_sum))

    if len(states) * states[0].shape[0] <= FUSED_ROWS:
        shares, cross_keep, cross_send = cross_close(
            mark, at, normed_two, query_grad, out_cross, branch_cross, states, grads, cross_key, cross_value
        )
    else:
        shares = [encoder_part(mark, at, grads[2 * x : 2 * x + 2], cross_key, cross_value) for x in range(at.nx)]
        summed = lambda side: sum(dot(rows, grads[2 * x + side], TN) for x, rows in enumerate(states))
        cross_keep, cross_send = laid_out(
            at, [dot(normed_two, query_grad, TN), dot(out_cross, branch_cross, TN), summed(0), summed(1)]
        )
    early = [at.shift(part[0], x=-1 - k) for k, part in enumerate(shares[1:])]
    late = [at.shift(part[1], x=-1 - k) for k, part in enumerate(shares[1:])]
    cross_sum = Reduction(at, cross_keep, cross_send, "yxlh")
    mark = gate(advance(cross_keep, ff_out_sum, ff_in_sum, together=True))
    mark = gate(shares[1:], cross_send, advance(mark, cross_sum))

    input_grad, branch_self, *self_grads, extra = self_backward(
        mark, at.seq, query_grad, cross_query, after_self, gain_cross, resid_grad, decoder_in[0], gain_self,
        gain_ffn_grad, query_self, key_self, value_self, self_out, self_query, self_key, self_value,
        buckets, bias_table, score_scale,
    )
    (low_ready,) = totals(input_grad, [[[Term(part, "h") for part in (shares[0][0], *early)]]])
    high_terms = [Term(part, "h") for part in (shares[0][1], *late, at.shift(low_ready, l=-1))]
    ready = advance(low_ready, ff_out_sum, ff_in_sum, together=True)
    mark = gate(low_ready, late, ready, advance(ready[0], cross_sum))
    first_keep, first_send, second_keep, second_send = weight_grads(
        mark,
        at,
        [[(normed_one, grad)] for grad in self_grads] + [[(out_self, branch_self)]],
        [[0], [1]],
        extra,
    )
    first_sum = Reduction(at, first_keep, first_send, "yxlh")
    second_sum = Reduction(at, second_keep, second_send, SECOND)
    mark = gate(first_send, second_send)

    n, m = width // at.dp, width // at.seq
    ready = advance(mark, first_sum, second_sum)
    cross_ready = advance(ready[0], cross_sum)
    high_ready = totals(cross_ready[0], [[[term.at("h", h) for term in high_terms]] for h in range(1, at.high)])
    last_terms = [term.at("h", 0) for term in high_terms] + [
        Term(at.shift(piece, h=-1 - k), "") for k, piece in enumerate(high_ready)
    ]
    mark = gate(ready, cross_ready, high_ready)
    ff_out_grad, ff_in_grad = final(
        mark, at, [ff_out_sum, ff_in_sum], [["rows"], ["plain"]],
        [(ff_out.shape[0] // at.seq, n), (m, ff_in.shape[1] // at.dp)], head_count,
    )
    activated, mark = lax.optimization_barrier((activated, mark))
    output = (after_cross + dot(activated, ff_out, NN)).astype(half)
    cross_ready = advance(ff_in_grad, cross_sum)
    mark = gate(output, cross_ready, advance(cross_ready[0], first_sum, second_sum))
    mark = gate(advance(mark, first_sum, second_sum, together=True))
    small = (m, n)
    cross_query_grad, cross_out_grad, cross_key_grad, cross_value_grad = final(
        mark, at, [cross_sum], [["pair", "pair"]], [small] * 4, head_count
    )
    ready = advance(cross_value_grad, first_sum, second_sum, together=True)
    mark = gate(ready)
    (encoder_grad,) = totals(mark, [[last_terms]], full)
    mark = encoder_grad
    query_grad, key_grad, value_grad, out_grad, *gains, bias_grad = final(
        mark, at, [first_sum, second_sum], [["pair"], ["pair", "extra"]],
        [small] * 4 + [(1, m)] * 3 + [(bucket_count // at.seq, head_count)], head_count,
    )
    return (
        output[None],
        input_grad[None],
        encoder_grad[None],
        *(gain.reshape(-1) for gain in gains),
        query_grad,
        key_grad,
        value_grad,
        out_grad,
        bias_grad,
        cross_query_grad,
        cross_key_grad,
        cross_value_grad,
        cross_out_grad,
        ff_in_grad,
        ff_out_grad,
    )


def solution(mesh):
    placed = (
        P("dp", "seq", None),
        P("dp", "seq", None),
        P("dp", "seq"),
        P("dp", None),
        P("dp", "seq", None),
    ) + (P(),) * 14
    return jax.shard_map(
        functools.partial(shards, dp_size=mesh.shape["dp"], seq_size=mesh.shape["seq"]),
        mesh=mesh,
        in_specs=placed,
        out_specs=(
            P("dp", "seq", None),
            P("dp", "seq", None),
            P("dp", "seq", None),
            P("seq"),
            P("seq"),
            P("seq"),
            P("seq", "dp"),
            P("seq", "dp"),
            P("seq", "dp"),
            P("seq", "dp"),
            P("seq", None),
            P("seq", "dp"),
            P("seq", "dp"),
            P("seq", "dp"),
            P("seq", "dp"),
            P("seq", "dp"),
            P("seq", "dp"),
        ),
        check_vma=False,
    )
```

```python
import functools
import itertools
import math

import jax
import jax.numpy as jnp
import numpy as np
from jax import lax
from jax.experimental import pallas as pl
from jax.experimental.pallas import tpu as pltpu
from jax.sharding import PartitionSpec as P

MAX_REACH = 128
DEC_LEN = 128


epsilon = 1e-06
masked_fill = -1e30
half = jnp.bfloat16
full = jnp.float32


def bucket_map(length, buckets, max_reach):
    exact_span = buckets // 2
    places = np.arange(length)
    distance = places[None, :] - places[:, None]
    passed = np.zeros_like(distance)
    for threshold_index in range(1, buckets - exact_span):
        threshold = int(
            math.ceil(
                exact_span * (max_reach / exact_span) ** (threshold_index / (buckets - exact_span))
            )
        )
        passed = passed + (distance >= threshold)
    bucket_of = np.where(distance < exact_span, distance, exact_span + passed)
    return np.where(distance < 0, -1, bucket_of).astype(np.int32)


def norm_parts(values):
    inverse = lax.rsqrt(jnp.mean(values * values, axis=-1, keepdims=True) + epsilon)
    return values * inverse, inverse


def norm_backward(upstream, normal, inverse, gain_row):
    scaled = upstream * gain_row
    inner = jnp.mean(scaled * normal, axis=-1, keepdims=True)
    return inverse * (scaled - normal * inner), jnp.sum(upstream * normal, axis=0, keepdims=True)


NT = (((1,), (1,)), ((), ()))
NN = (((1,), (0,)), ((), ()))
TN = (((0,), (0,)), ((), ()))
LANES = 128
ONES = 8
MEGA = 2**20
PAIRS = 2
FUSED_ROWS = 2048
SECOND = "xylh"


def dot(left_side, right_side, dims):
    return lax.dot_general(left_side, right_side, dims, preferred_element_type=full)


def three(value):
    first = value.astype(half).astype(full)
    second = (value - first).astype(half).astype(full)
    return first, second, (value - first - second).astype(half).astype(full)


def placed_three(value, index, rest):
    first, second, third = three(value)
    return jnp.where(
        index == ONES, first, jnp.where(index == ONES + 1, second, jnp.where(index == ONES + 2, third, rest))
    )


def low_lanes(rows):
    return lax.broadcasted_iota(jnp.int32, (rows, LANES), 1) < LANES // 2


def stacked(value, low):
    zero = jnp.zeros_like(value)
    return jnp.concatenate([jnp.where(low, value, zero), jnp.where(low, zero, value)], axis=0)


def loop(count, step, start):
    return lax.fori_loop(0, count, step, start, unroll=count <= 4)


light = pl.CostEstimate(flops=1, bytes_accessed=1, transcendentals=0)


def params(megabytes):
    return pltpu.CompilerParams(vmem_limit_bytes=megabytes * MEGA)


def whole(shape):
    return pl.BlockSpec(shape, lambda *_: (0,) * len(shape))


anywhere = pl.BlockSpec(memory_space=pl.ANY)


class Blocks:
    def __init__(self, at):
        self.core, self.ny, self.nx, self.dp, self.seq = at.core, at.ny, at.nx, at.dp, at.seq
        self.high, self.low = at.high, at.low

    def shape(self, rows, columns):
        return (self.ny, self.nx, self.high, self.low, rows, columns)

    def row_place(self, block, place):
        z = lax.div(block, self.nx)
        return (
            lax.rem(lax.rem(block, self.nx) - place[2] + self.nx, self.nx),
            lax.rem(lax.div(z, self.low) - place[3] + self.high, self.high),
            lax.rem(lax.rem(z, self.low) - place[4] + self.low, self.low),
        )

    def column_place(self, y, place):
        return lax.rem(y - place[0] + self.ny, self.ny)

    def paired(self, first, second, place):
        n = first.shape[1] // self.core
        if self.core == 1:
            return jnp.concatenate([first, second], axis=1).astype(half), None
        mine = place[1] == 0
        if n % LANES != LANES // 2:
            cut = [jnp.concatenate([g[:, c * n : (c + 1) * n] for g in (first, second)], axis=1) for c in range(2)]
        else:
            main = n - LANES // 2
            low = lax.broadcasted_iota(jnp.int32, (first.shape[0], LANES), 1) < LANES // 2
            one, two = (g[:, main : main + LANES] for g in (first, second))
            sides = (
                jnp.where(low, one, pltpu.roll(two, LANES // 2, 1)),
                jnp.where(low, pltpu.roll(one, LANES // 2, 1), two),
            )
            cut = [
                jnp.concatenate([first[:, at : at + main], second[:, at : at + main], sides[c]], axis=1)
                for c, at in enumerate((0, main + LANES))
            ]
        return jnp.where(mine, cut[0], cut[1]).astype(half), jnp.where(mine, cut[1], cut[0]).astype(half)


def unpaired(piece, core):
    n = piece.shape[1] // 2
    if n % LANES != LANES // 2:
        return piece[:, :n], piece[:, n:]
    main = n - LANES // 2
    side = piece[:, 2 * main :]
    turned = pltpu.roll(side, LANES // 2, 1)
    out = []
    for k in range(2):
        big = piece[:, k * main : (k + 1) * main]
        first, second = (side, turned) if k == 0 else (turned, side)
        after = jnp.concatenate([big, first], axis=1)
        ahead = pltpu.roll(jnp.concatenate([big, second], axis=1), LANES // 2, 1)
        out.append(jnp.where(core == 0, after, ahead)[:, :n])
    return out


def position_bias(buckets, table, pair):
    out = []
    for head in range(2):
        bias = jnp.full(buckets.shape, masked_fill, full)
        for b in range(table.shape[0]):
            bias = jnp.where(buckets == b, table[b, 2 * pair + head], bias)
        out.append(bias)
    return jnp.concatenate(out, axis=1)


def self_forward_kernel(
    hidden, gain_one, gain_two, weights_q, weights_k, weights_v, weights_o, weights_c, buckets, table,
    query, key, value, mixed, after, normed_two, query_cross, normed, every, *, scale,
):
    step = pl.program_id(0)
    rows = hidden.shape[0]

    @pl.when(step == 0)
    def _():
        normal, _ = norm_parts(hidden[...].astype(full))
        normed[...] = (normal * gain_one[...]).astype(half)

    many = query.shape[1] // LANES
    wide = many * LANES
    weights = jnp.concatenate([weights_q[...], weights_k[...], weights_v[...]], axis=1)
    made = dot(normed[...], weights, NN).astype(half)
    query[...] = made[:, :wide] * scale
    key[...] = made[:, wide : 2 * wide]
    value[...] = made[:, 2 * wide :]
    low = low_lanes(DEC_LEN)
    bias = [position_bias(buckets[...], table, step * many + pair) for pair in range(many)]
    work = [
        (pair, slice(pair * LANES, (pair + 1) * LANES), pl.ds(first, DEC_LEN))
        for pair in range(many)
        for first in range(0, rows, DEC_LEN)
    ]
    scores = [dot(key[at, own], stacked(query[at, own], low), NT) + bias[pair] for pair, own, at in work]
    expos = []
    for score in scores:
        expo = jnp.exp(score - jnp.max(score, axis=0, keepdims=True))
        expos.append((expo / jnp.sum(expo, axis=0, keepdims=True)).astype(half))
    for (pair, own, at), expo in zip(work, expos):
        both = dot(value[at, own], expo, TN).T
        one = jnp.where(low, both[:DEC_LEN], both[DEC_LEN:]).astype(half)
        mixed[at, own] = one
        every[at, pl.ds(pl.multiple_of(step * wide + pair * LANES, LANES), LANES)] = one

    @pl.when(step == pl.num_programs(0) - 1)
    def _():
        total = hidden[...].astype(full) + dot(every[...], weights_o[...], NN)
        after[...] = total
        normal, _ = norm_parts(total)
        again = (normal * gain_two[...]).astype(half)
        normed_two[...] = again
        query_cross[...] = dot(again, weights_c[...], NN).astype(half)


def self_forward(mark, hidden, gain_one, gain_two, weights_q, weights_k, weights_v, weights_o, weights_c, buckets, table, scale):
    rows, width = hidden.shape
    pairs = width // LANES
    many = PAIRS
    column = lambda i: (0, i)
    row_block = pl.BlockSpec((rows, many * LANES), column)
    weight_block = pl.BlockSpec((width, many * LANES), column)
    return pl.pallas_call(
        marked(functools.partial(self_forward_kernel, scale=scale)),
        name="self_forward",
        grid=(pairs // many,),
        in_specs=[anywhere, whole((rows, width)), whole((1, width)), whole((1, width))]
        + [weight_block] * 3
        + [whole((width, width))] * 2
        + [whole((DEC_LEN, DEC_LEN)), pl.BlockSpec(memory_space=pltpu.SMEM)],
        out_specs=[row_block] * 4 + [whole((rows, width))] * 4,
        out_shape=[jax.ShapeDtypeStruct((rows, width), half)] * 4
        + [jax.ShapeDtypeStruct((rows, width), kind) for kind in (full, half, half, half)],
        scratch_shapes=[pltpu.VMEM((rows, width), half)],
        compiler_params=params(56),
        cost_estimate=light,
    )(mark, hidden, gain_one, gain_two, weights_q, weights_k, weights_v, weights_o, weights_c, buckets, table)


def key_value_kernel(*refs, rows, doc_count):
    shards, (own, weights_k, weights_v, keys, values, mask, states) = refs[:-7], refs[-7:]
    for i, shard in enumerate(shards):
        at = pl.ds(i * rows, rows)
        states[at, :] = shard[:rows, :]
        keys[at, :] = dot(shard[:rows, :], weights_k[...], NN).astype(half)
        values[at, :] = dot(shard[:rows, :], weights_v[...], NN).astype(half)
        docs = shard[rows : rows + 1, :rows].astype(full)
        lane = lax.broadcasted_iota(jnp.int32, (LANES, rows), 0)
        ones = ((lane >= ONES) & (lane < ONES + 3)).astype(full)
        extra = jnp.where(lane < doc_count, jnp.where(docs == own[:, :1], 0.0, masked_fill), ones)
        mask[at, :] = extra.T.astype(half)


def key_value(shards, own, weights_k, weights_v, rows, doc_count, begun=(), place=0, places=1):
    width = shards[0].shape[1]
    count = len(shards) * rows
    sizes = (width, width, LANES, width)
    kernel = functools.partial(key_value_kernel, rows=rows, doc_count=doc_count)
    return pl.pallas_call(
        lambda *refs: kernel(*refs[len(begun) :]),
        name="key_value",
        grid=(1,),
        in_specs=[anywhere] * len(begun) + [whole(array.shape) for array in (*shards, own, weights_k, weights_v)],
        out_specs=[pl.BlockSpec((count, size), lambda i: (place, 0)) for size in sizes],
        out_shape=[jax.ShapeDtypeStruct((places * count, size), half) for size in sizes],
        input_output_aliases={i: i for i in range(len(begun))},
        compiler_params=params(56),
        cost_estimate=light,
    )(*begun, *shards, own, weights_k, weights_v)


def cross_forward_kernel(*refs, scale, block, opens, closes):
    query, mark, keys, values, mask = refs[:5]
    refs = refs[5:]
    if not opens:
        state_in, refs = refs[:2], refs[2:]
    if closes:
        (mixed, mixed_half, extended), refs = refs[:3], refs[3:]
    else:
        state_out, refs = refs[:2], refs[2:]
    total, wide = refs
    rows, many = query.shape[0], query.shape[1] // LANES
    low = low_lanes(rows)
    for pair in range(many):
        wide[pair, :, :LANES] = stacked(query[:, pair * LANES : (pair + 1) * LANES] * scale, low)
        wide[pair, :rows, LANES:] = mark[...]
        wide[pair, rows:, LANES:] = mark[...]
    if opens:
        total[...] = jnp.zeros_like(total)
        carry = [(jnp.full((1, 2 * rows), masked_fill, full), jnp.zeros((1, 2 * rows), full)) for _ in range(many)]
    else:
        total[...] = state_in[0][...]
        carry = [(state_in[1][pair, 0:1], state_in[1][pair, 1:2]) for pair in range(many)]

    def step(i, carry):
        at = pl.ds(pl.multiple_of(i * block, block), block)
        scores = [
            dot(jnp.concatenate([keys[at, pair * LANES : (pair + 1) * LANES], mask[at, :]], axis=1), wide[pair], NT)
            for pair in range(many)
        ]
        out = []
        for pair, (peak, amount) in enumerate(carry):
            fresh = jnp.maximum(peak, jnp.max(scores[pair], axis=0, keepdims=True))
            expo = jnp.exp(scores[pair] - fresh)
            fade = jnp.exp(peak - fresh)
            values_here = values[at, pair * LANES : (pair + 1) * LANES]
            total[pair] = total[pair] * fade + dot(values_here, expo.astype(half), TN)
            out.append((fresh, amount * fade + jnp.sum(expo, axis=0, keepdims=True)))
        return out

    carry = loop(keys.shape[0] // block, step, carry)
    if not closes:
        state_out[0][...] = total[...]
        for pair, (peak, amount) in enumerate(carry):
            state_out[1][pair, 0:1] = peak
            state_out[1][pair, 1:2] = amount
        return
    index = lax.broadcasted_iota(jnp.int32, (LANES, 2 * rows), 0)
    for pair, (peak, amount) in enumerate(carry):
        at = slice(pair * LANES, (pair + 1) * LANES)
        both = (total[pair] / amount).T
        one = jnp.where(low, both[:rows], both[rows:])
        mixed[:, at] = one
        mixed_half[:, at] = one.astype(half)
        extra = placed_three(-(peak + jnp.log(amount)), index, 0.0).T
        extended[pair, :, :LANES] = wide[pair, :, :LANES]
        extended[pair, :, LANES:] = (wide[pair, :, LANES:].astype(full) + extra).astype(half)


def cross_forward(query, mark, source, state, closes, scale):
    rows, pairs, many = query.shape[0], query.shape[1] // LANES, PAIRS
    count = source[0].shape[0]
    column = lambda i: (0, i)
    plane = lambda i: (i, 0, 0)
    block = min(1024, count)
    state_specs = [pl.BlockSpec((many, LANES, 2 * rows), plane), pl.BlockSpec((many, 2, 2 * rows), plane)]
    state_shape = [
        jax.ShapeDtypeStruct((pairs, LANES, 2 * rows), full),
        jax.ShapeDtypeStruct((pairs, 2, 2 * rows), full),
    ]
    last_specs = [pl.BlockSpec((rows, many * LANES), column)] * 2 + [pl.BlockSpec((many, 2 * rows, 2 * LANES), plane)]
    last_shape = [
        jax.ShapeDtypeStruct(query.shape, full),
        jax.ShapeDtypeStruct(query.shape, half),
        jax.ShapeDtypeStruct((pairs, 2 * rows, 2 * LANES), half),
    ]
    return pl.pallas_call(
        functools.partial(cross_forward_kernel, scale=scale, block=block, opens=not state, closes=closes),
        name="cross_forward",
        grid=(pairs // many,),
        in_specs=[pl.BlockSpec((rows, many * LANES), column), whole((rows, LANES))]
        + [pl.BlockSpec((count, many * LANES), column), pl.BlockSpec((count, many * LANES), column), whole((count, LANES))]
        + (state_specs if state else []),
        out_specs=last_specs if closes else state_specs,
        out_shape=last_shape if closes else state_shape,
        scratch_shapes=[
            pltpu.VMEM((many, LANES, 2 * rows), full),
            pltpu.VMEM((many, 2 * rows, 2 * LANES), half),
        ],
        compiler_params=params(56),
        cost_estimate=light,
    )(query, mark, *source, *state)


def cross_backward_kernel(*refs, scale, block, parts):
    extended, upstream, mixed = refs[:3]
    sources = [refs[3 + 3 * i : 6 + 3 * i] for i in range(parts)]
    query_grad = refs[3 + 3 * parts]
    grads = [refs[4 + 3 * parts + 2 * i : 6 + 3 * parts + 2 * i] for i in range(parts)]
    wide, total = refs[-2:]
    rows = upstream.shape[0]
    low = low_lanes(rows)
    lane = lax.broadcasted_iota(jnp.int32, (rows, LANES), 1)
    each = upstream[...].astype(full) * mixed[...]
    wide[:, :LANES] = stacked(upstream[...], low)
    for head in range(2):
        inner = jnp.sum(jnp.where(low == (head == 0), each, 0.0), axis=1, keepdims=True)
        wide[head * rows : (head + 1) * rows, LANES:] = placed_three(-inner, lane, 0.0).astype(half)
    total[...] = jnp.zeros_like(total)
    for (keys, values, mask), (key_grad, value_grad) in zip(sources, grads):

        def step(i, carry):
            at = pl.ds(pl.multiple_of(i * block, block), block)
            extra = mask[at, :]
            expo = jnp.exp(dot(jnp.concatenate([keys[at, :], extra], axis=1), extended[0], NT))
            change = dot(jnp.concatenate([values[at, :], extra], axis=1), wide[...], NT)
            score = (expo * change).astype(half)
            value_grad[at, :] = dot(expo.astype(half), wide[:, :LANES], NN).astype(half)
            key_grad[at, :] = dot(score, extended[0, :, :LANES], NN).astype(half)
            total[...] += dot(keys[at, :], score, TN)
            return carry

        loop(keys.shape[0] // block, step, 0)
    both = total[...].T
    query_grad[...] = (jnp.where(low, both[:rows], both[rows:]) * scale).astype(half)


def cross_backward(mark, extended, upstream, mixed, sources, first, pairs, begun, scale):
    rows, width = upstream.shape
    count = sources[0][0].shape[0]
    every = count * len(sources)
    column = lambda i: (0, i + first)
    block = min(1024, count)
    row_block, key_block = pl.BlockSpec((rows, LANES), column), pl.BlockSpec((count, LANES), column)
    operands = [extended, upstream, mixed, *[array for source in sources for array in source]]
    kernel = functools.partial(cross_backward_kernel, scale=scale, block=block, parts=len(sources))
    return pl.pallas_call(
        marked(lambda *refs: kernel(*refs[len(begun) :]), len(begun)),
        name="cross_backward",
        grid=(pairs,),
        in_specs=[anywhere] * (len(begun) + 1)
        + [pl.BlockSpec((1, 2 * rows, 2 * LANES), lambda i: (i + first, 0, 0)), row_block, row_block]
        + [key_block, key_block, whole((count, LANES))] * len(sources),
        out_specs=[row_block] + [key_block] * (2 * len(sources)),
        out_shape=[jax.ShapeDtypeStruct((rows, width), half)]
        + [jax.ShapeDtypeStruct((count, width), half)] * (2 * len(sources)),
        scratch_shapes=[
            pltpu.VMEM((2 * rows, 2 * LANES), half),
            pltpu.VMEM((LANES, 2 * rows), full),
        ],
        input_output_aliases={i: i for i in range(len(begun))},
        compiler_params=params(56),
        cost_estimate=light,
    )(*begun, mark, *operands)


def feed_forward_kernel(
    place, after, mixed, weights_o, gain, weights_in, weights_out, cotangent,
    after_cross, activated, resid, branch, mixed_grad, gain_grad, in_keep, in_send, out_keep, out_send,
    normed, total, *, blocks,
):
    step = pl.program_id(0)

    @pl.when(step == 0)
    def _():
        values = after[...] + dot(mixed[...], weights_o[...], NN)
        after_cross[...] = values
        normal, _ = norm_parts(values)
        normed[...] = (normal * gain[...]).astype(half)
        total[...] = jnp.zeros_like(total)

    upstream = cotangent[...]
    pre = dot(normed[...], weights_in[...], NN)
    square = pre * pre
    slope = math.sqrt(2.0 / math.pi)
    bend = jnp.tanh(slope * (pre + 0.044715 * (square * pre)))
    act = (0.5 * pre * (1.0 + bend)).astype(half)
    activated[...] = act
    gelu_grad = 0.5 * (1.0 + bend) + 0.5 * pre * (1.0 - bend * bend) * (slope * (1.0 + 3 * 0.044715 * square))
    pre_grad = (dot(upstream, weights_out[...], NT) * gelu_grad).astype(half)
    total[...] += dot(pre_grad, weights_in[...], NT)

    grad = dot(normed[...], pre_grad, TN).astype(half)
    m = grad.shape[0] // blocks.seq
    to_y = blocks.column_place(lax.div(step, blocks.core), place)
    ours = lax.rem(step, blocks.core) == place[1]

    def fill(target):
        for block in range(blocks.seq):
            to_x, to_h, to_l = blocks.row_place(jnp.int32(block), place)
            target[to_y, to_x, to_h, to_l] = grad[block * m : (block + 1) * m]

    pl.when(ours)(lambda: fill(in_keep))
    pl.when(jnp.logical_not(ours))(lambda: fill(in_send))

    grad = dot(act, upstream, TN)
    wide = grad.shape[1] // blocks.ny
    n = wide // blocks.core
    pieces = out_keep.shape[5] // n
    many = pieces * m
    for y in range(blocks.ny):
        at = slice(y * wide, (y + 1) * wide)
        to_y = blocks.column_place(jnp.int32(y), place)
        for block in range(grad.shape[0] // many):
            to_x, to_h, to_l = blocks.row_place(step * (grad.shape[0] // many) + block, place)
            for piece in range(0, pieces, 2):
                first = block * many + piece * m
                kept, sent = blocks.paired(grad[first : first + m, at], grad[first + m : first + 2 * m, at], place)
                out_keep[to_y, to_x, to_h, to_l, :, piece * n : (piece + 2) * n] = kept
                if sent is not None:
                    out_send[to_y, to_x, to_h, to_l, :, piece * n : (piece + 2) * n] = sent

    @pl.when(step == pl.num_programs(0) - 1)
    def _():
        normal, inverse = norm_parts(after_cross[...])
        change, gain_sum = norm_backward(total[...], normal, inverse, gain[...])
        gain_grad[...] = gain_sum
        change = change + upstream.astype(full)
        resid[...] = change
        rounded = change.astype(half)
        branch[...] = rounded
        mixed_grad[...] = dot(rounded, weights_o[...], NT).astype(half)


def feed_forward(at, after, mixed, weights_o, gain, weights_in, weights_out, cotangent):
    rows, width = after.shape
    depth = weights_in.shape[1]
    blocks = Blocks(at)
    cut = depth // at.dp
    shape = blocks.shape(width // at.seq, cut)
    all_rows = whole((rows, width))
    sized = lambda kind: jax.ShapeDtypeStruct((rows, width), kind)
    return pl.pallas_call(
        functools.partial(feed_forward_kernel, blocks=blocks),
        name="feed_forward",
        grid_spec=pltpu.PrefetchScalarGridSpec(
            num_scalar_prefetch=1,
            grid=(at.dp,),
            in_specs=[
                all_rows,
                all_rows,
                whole((width, width)),
                whole((1, width)),
                pl.BlockSpec((width, cut), lambda i, _: (0, i)),
                pl.BlockSpec((cut, width), lambda i, _: (i, 0)),
                all_rows,
            ],
            out_specs=[all_rows, pl.BlockSpec((rows, cut), lambda i, _: (0, i))]
            + [all_rows] * 3
            + [whole((1, width))]
            + [whole(shape)] * 4,
            scratch_shapes=[pltpu.VMEM((rows, width), half), pltpu.VMEM((rows, width), full)],
        ),
        out_shape=[sized(full), jax.ShapeDtypeStruct((rows, depth), half), sized(full), sized(half), sized(half)]
        + [jax.ShapeDtypeStruct((1, width), full)]
        + [jax.ShapeDtypeStruct(shape, half)] * 4,
        compiler_params=params(56),
        cost_estimate=light,
    )(at.place, after, mixed, weights_o, gain, weights_in, weights_out, cotangent)


def encoder_part_kernel(key_grad, value_grad, weights_k, weights_v, early, late, *, early_steps):
    total = dot(key_grad[...], weights_k[...], NT) + dot(value_grad[...], weights_v[...], NT)
    is_early = pl.program_id(0) < early_steps

    @pl.when(is_early)
    def _():
        early[...] = total.astype(half)

    @pl.when(jnp.logical_not(is_early))
    def _():
        late[...] = total.astype(half)


def encoder_part(mark, at, grads, weights_k, weights_v):
    width = weights_k.shape[0]
    rows = grads[0].shape[0] // at.nz
    early = at.high * (at.low - 1)
    plane = lambda size: jax.ShapeDtypeStruct((size, rows, width), half)
    block = pl.BlockSpec((rows, width), lambda i: (i % at.high * at.low + at.low - 1 - i // at.high, 0))
    return pl.pallas_call(
        marked(functools.partial(encoder_part_kernel, early_steps=early)),
        name="encoder_part",
        grid=(at.nz,),
        in_specs=[anywhere, block, block, whole((width, width)), whole((width, width))],
        out_specs=[
            pl.BlockSpec((None, rows, width), lambda i: (jnp.minimum(i, early - 1), 0, 0)),
            pl.BlockSpec((None, rows, width), lambda i: (jnp.maximum(i - early, 0), 0, 0)),
        ],
        out_shape=[plane(early), plane(at.high)],
        compiler_params=params(56),
        cost_estimate=light,
    )(mark, *grads, weights_k, weights_v)


def weight_grads_kernel(place, *refs, blocks, counts, chunks, extra, wide):
    refs = list(refs)
    sides = [[(refs.pop(0), refs.pop(0)) for _ in range(count)] for count in counts]
    small = refs.pop(0) if extra else None
    made = [sum((dot(left[...], right[...], TN) for left, right in side[1:]), dot(side[0][0][...], side[0][1][...], TN)) for side in sides]
    m = made[0].shape[0] // blocks.seq
    many = made[0].shape[1] // wide
    for chunk, pairs in enumerate(chunks):
        keep, send = refs[2 * chunk], refs[2 * chunk + 1]
        for y in range(many):
            at = slice(y * wide, (y + 1) * wide)
            columns = [blocks.paired(made[2 * pair][:, at], made[2 * pair + 1][:, at], place) for pair in pairs]
            if extra and chunk == len(chunks) - 1:
                columns.append((small[...], small[...]))
            to_y = blocks.column_place(jnp.int32(y), place) if many > 1 else 0
            for block in range(blocks.seq):
                to_x, to_h, to_l = blocks.row_place(jnp.int32(block), place)
                rows = slice(block * m, (block + 1) * m)
                first = 0
                for ours, theirs in columns:
                    to = slice(first, first + ours.shape[1])
                    keep[to_y, to_x, to_h, to_l, :, to] = ours[rows]
                    send[to_y, to_x, to_h, to_l, :, to] = theirs[rows]
                    first += ours.shape[1]


def weight_grads(mark, at, sides, chunks, extra=None):
    blocks = Blocks(at)
    width = sides[0][0][0].shape[1]
    wide, m = width // at.ny, width // at.seq
    shapes = [blocks.shape(m, len(pairs) * 2 * wide // at.core) for pairs in chunks]
    if extra is not None:
        shapes[-1] = (*shapes[-1][:-1], shapes[-1][-1] + extra.shape[1])
    terms = [term for side in sides for term in side]
    steps = at.ny if wide % LANES == 0 else 1
    from_y = lambda i, place: (0, lax.rem(i + place[0], at.ny) if steps > 1 else 0)
    out_block = lambda shape: pl.BlockSpec((shape[0] // steps, *shape[1:]), lambda i, place: (i, 0, 0, 0, 0, 0))
    return pl.pallas_call(
        marked(
            functools.partial(
                weight_grads_kernel,
                blocks=blocks,
                counts=[len(side) for side in sides],
                chunks=chunks,
                extra=extra is not None,
                wide=wide,
            ),
            1,
        ),
        name="weight_grads",
        grid_spec=pltpu.PrefetchScalarGridSpec(
            num_scalar_prefetch=1,
            grid=(steps,),
            in_specs=[anywhere]
            + [
                spec
                for left, right in terms
                for spec in (whole(left.shape), pl.BlockSpec((right.shape[0], width // steps), from_y))
            ]
            + ([whole(extra.shape)] if extra is not None else []),
            out_specs=[out_block(shape) for shape in shapes for _ in range(2)],
        ),
        out_shape=[jax.ShapeDtypeStruct(shape, half) for shape in shapes for _ in range(2)],
        compiler_params=params(60),
        cost_estimate=light,
    )(at.place, mark, *[array for term in terms for array in term], *([extra] if extra is not None else []))


def laid_out(at, grads):
    out = []
    for grad in grads:
        m, n = grad.shape[0] // at.seq, grad.shape[1] // at.dp
        assert n % LANES != LANES // 2
        blocks = grad.astype(half).reshape(at.high, at.low, at.nx, m, at.ny, at.core, n)
        places = ((0, at.z // at.low, at.high), (1, at.z % at.low, at.low), (2, at.x, at.nx), (4, at.y, at.ny), (5, at.c, at.core))
        for axis, own, size in places:
            blocks = jnp.take(blocks, (own + jnp.arange(size)) % size, axis=axis)
        out.append(blocks.transpose(5, 4, 2, 0, 1, 3, 6))
    both = jnp.concatenate(out, axis=-1)
    return both[0], both[1]


def cross_close_kernel(place, *refs, blocks, parts):
    count = 3 * parts + 6
    arrays, refs = refs[:count], refs[count:]
    shares, (keep, send), refs = refs[: 2 * parts], refs[2 * parts : 2 * parts + 2], refs[2 * parts + 2 :]
    held, refs = refs[:count], refs[count:]
    made, (keep_held, send_held, arrived, gone) = refs[:parts], refs[parts:]
    ins = [pltpu.make_async_copy(array, place_held, arrived.at[i]) for i, (array, place_held) in enumerate(zip(arrays, held))]
    grads, (weights_k, weights_v), states = held[: 2 * parts], held[2 * parts : 2 * parts + 2], held[2 * parts + 2 : -4]
    normed, query_grad, mixed, branch = held[-4:]
    outs = []

    def leave(source, target):
        copy = pltpu.make_async_copy(source, target, gone.at[len(outs)])
        copy.start()
        outs.append(copy)

    order = [*range(1, parts), 0]
    first = [i for x in order[:1] for i in (2 * x, 2 * x + 1)] + [2 * parts, 2 * parts + 1]
    for i in first + [i for i in range(count) if i not in first]:
        ins[i].start()
    ins[2 * parts].wait()
    ins[2 * parts + 1].wait()
    rows = grads[0].shape[0] // (blocks.high * blocks.low)
    early_size = blocks.low - 1
    for x in order:
        ins[2 * x].wait()
        ins[2 * x + 1].wait()
        for block in range(blocks.high * blocks.low):
            at = slice(block * rows, (block + 1) * rows)
            total = dot(grads[2 * x][at, :], weights_k[...], NT) + dot(grads[2 * x + 1][at, :], weights_v[...], NT)
            made[x][at, :] = total.astype(half)
        for block in range(blocks.high * blocks.low):
            h, l = divmod(block, blocks.low)
            source = made[x].at[pl.ds(block * rows, rows), :]
            leave(source, shares[2 * x].at[(blocks.low - 1 - l) * blocks.high + h] if l else shares[2 * x + 1].at[h])

    def place_pair(one, two, offset):
        m, wide = one.shape[0] // blocks.seq, one.shape[1] // blocks.ny
        for y in range(blocks.ny):
            at = slice(y * wide, (y + 1) * wide)
            ours, theirs = blocks.paired(one[:, at], two[:, at], place)
            to_y = blocks.column_place(jnp.int32(y), place)
            to = slice(offset, offset + ours.shape[1])
            for block in range(blocks.seq):
                to_x, to_h, to_l = blocks.row_place(jnp.int32(block), place)
                own = slice(block * m, (block + 1) * m)
                keep_held[to_y, to_x, to_h, to_l, :, to] = ours[own]
                send_held[to_y, to_x, to_h, to_l, :, to] = theirs[own]
        for source, target in ((send_held, send), (keep_held, keep)):
            leave(source.at[:, :, :, :, :, to], target.at[:, :, :, :, :, to])

    n = keep_held.shape[5] // 4
    for copy in ins[2 * parts + 2 : -4]:
        copy.wait()
    total = []
    for kind in range(2):
        terms = [dot(states[x][...], grads[2 * x + kind][...], TN) for x in range(parts)]
        total.append(sum(terms[1:], terms[0]))
    place_pair(total[0], total[1], 2 * n)
    for copy in ins[-4:]:
        copy.wait()
    place_pair(dot(normed[...], query_grad[...], TN), dot(mixed[...], branch[...], TN), 0)
    for copy in outs:
        copy.wait()


def cross_close(mark, at, normed, query_grad, mixed, branch, states, grads, weights_k, weights_v):
    blocks, parts = Blocks(at), len(states)
    count, width = states[0].shape
    shape = blocks.shape(width // at.seq, 4 * width // at.dp)
    arrays = [*grads, weights_k, weights_v, *states, normed, query_grad, mixed, branch]
    plane = lambda size: jax.ShapeDtypeStruct((size, count // at.nz, width), half)
    outs = [plane(at.high * (at.low - 1)), plane(at.high)] * parts + [jax.ShapeDtypeStruct(shape, half)] * 2
    made = pl.pallas_call(
        marked(functools.partial(cross_close_kernel, blocks=blocks, parts=parts), 1),
        name="cross_close",
        in_specs=[pl.BlockSpec(memory_space=pltpu.SMEM)] + [anywhere] * (len(arrays) + 1),
        out_specs=[anywhere] * len(outs),
        out_shape=outs,
        scratch_shapes=[pltpu.VMEM(array.shape, half) for array in arrays]
        + [pltpu.VMEM((count, width), half)] * parts
        + [pltpu.VMEM(shape, half)] * 2
        + [pltpu.SemaphoreType.DMA((len(arrays),)), pltpu.SemaphoreType.DMA((parts * at.nz + 4,))],
        compiler_params=params(56),
        cost_estimate=light,
    )(at.place, mark, *arrays)
    return [made[2 * x : 2 * x + 2] for x in range(parts)], *made[-2:]


def self_backward_kernel(
    query_cross_grad, weights_c, after, gain_two, resid_in, hidden, gain_one, gain_ffn_grad,
    query, key, value, weights_ob, weights_q, weights_k, weights_v, buckets, table,
    input_grad, branch, query_grad, key_grad, value_grad, extra,
    resid, total, bias_rows, gain_two_grad, columns, *, scale, shares,
):
    step = pl.program_id(0)
    rows, width = hidden.shape

    @pl.when(step == 0)
    def _():
        normal, inverse = norm_parts(after[...])
        up = dot(query_cross_grad[...], weights_c[...], NT)
        change, gain_sum = norm_backward(up, normal, inverse, gain_two[...])
        gain_two_grad[...] = gain_sum
        change = change + resid_in[...]
        resid[...] = change
        branch[...] = change.astype(half)
        total[...] = jnp.zeros_like(total)

    low = low_lanes(DEC_LEN)
    many = query.shape[1] // LANES
    upstream = dot(branch[...], weights_ob[...], NT).astype(half)
    count = bias_rows.shape[1]
    of_pair = jnp.concatenate([buckets[...], buckets[...]], axis=1)
    work = [(pair, pl.ds(first, DEC_LEN)) for pair in range(many) for first in range(0, rows, DEC_LEN)]
    spans = [slice(pair * LANES, (pair + 1) * LANES) for pair in range(many)]
    bias = [position_bias(buckets[...], table, step * many + pair) for pair in range(many)]
    wides = [stacked(query[at, spans[pair]], low) for pair, at in work]
    up = [stacked(upstream[at.start : at.start + DEC_LEN, spans[pair]], low) for pair, at in work]
    scores = [dot(key[at, spans[pair]], wide, NT) + bias[pair] for (pair, at), wide in zip(work, wides)]
    changes = [dot(value[at, spans[pair]], grad, NT) for (pair, at), grad in zip(work, up)]
    summed = [None] * many
    for (pair, at), wide, grad, score, change in zip(work, wides, up, scores, changes):
        own = spans[pair]
        expo = jnp.exp(score - jnp.max(score, axis=0, keepdims=True))
        expo = expo / jnp.sum(expo, axis=0, keepdims=True)
        rounded = (expo * (change - jnp.sum(expo * change, axis=0, keepdims=True))).astype(half)
        both = dot(key[at, own], rounded, TN).T
        query_grad[at, own] = (jnp.where(low, both[:DEC_LEN], both[DEC_LEN:]) * scale).astype(half)
        key_grad[at, own] = dot(rounded, wide, NN).astype(half)
        value_grad[at, own] = dot(expo.astype(half), grad, NN).astype(half)
        summed[pair] = rounded.astype(full) if summed[pair] is None else summed[pair] + rounded.astype(full)
    made = jnp.concatenate([query_grad[...], key_grad[...], value_grad[...]], axis=1)
    total[...] += dot(made, jnp.concatenate([weights_q[...], weights_k[...], weights_v[...]], axis=1), NT)
    for pair in range(many):
        sums = [jnp.sum(jnp.where(of_pair == b, summed[pair], 0.0), axis=0, keepdims=True) for b in range(count)]
        bias_rows[step * many + pair] = jnp.concatenate(sums, axis=0)

    @pl.when(step == pl.num_programs(0) - 1)
    def _():
        normal, inverse = norm_parts(hidden[...].astype(full))
        change, gain_sum = norm_backward(total[...], normal, inverse, gain_one[...])
        input_grad[...] = resid[...] + change

        index = lax.broadcasted_iota(jnp.int32, (LANES, width), 0)
        gains = jnp.where(
            index == 0,
            gain_sum,
            jnp.where(index == 1, gain_two_grad[...], jnp.where(index == 2, gain_ffn_grad[...], 0.0)),
        )
        columns[...] = gains.T
        lane = lax.broadcasted_iota(jnp.int32, (count, LANES), 1)
        sums = jnp.zeros((count, LANES), full)
        for pair in range(bias_rows.shape[0]):
            for head in range(2):
                part = bias_rows[pair, :, head * LANES : (head + 1) * LANES]
                sums = jnp.where(lane == 16 + 2 * pair + head, jnp.sum(part, axis=1, keepdims=True), sums)
        m, each = width // shares, count // shares
        for block in range(shares):
            at = slice(block * m, block * m + each)
            columns[at, :] = columns[at, :] + sums[block * each : (block + 1) * each]
        extra[...] = columns[...].astype(half)


def self_backward(
    mark, shares, query_cross_grad, weights_c, after, gain_two, resid, hidden, gain_one, gain_ffn_grad,
    query, key, value, weights_o, weights_q, weights_k, weights_v, buckets, table, scale,
):
    rows, width = hidden.shape
    pairs, count = width // LANES, table.shape[0]
    many = PAIRS
    row_block = pl.BlockSpec((rows, many * LANES), lambda i: (0, i))
    weight_block = pl.BlockSpec((width, many * LANES), lambda i: (0, i))
    all_rows, line = whole((rows, width)), whole((1, width))
    sized = lambda kind: jax.ShapeDtypeStruct((rows, width), kind)
    return pl.pallas_call(
        marked(functools.partial(self_backward_kernel, scale=scale, shares=shares)),
        name="self_backward",
        grid=(pairs // many,),
        in_specs=[anywhere, all_rows, whole((width, width)), all_rows, line, all_rows, all_rows, line, line]
        + [row_block] * 3
        + [pl.BlockSpec((many * LANES, width), lambda i: (i, 0))]
        + [weight_block] * 3
        + [whole((DEC_LEN, DEC_LEN)), pl.BlockSpec(memory_space=pltpu.SMEM)],
        out_specs=[all_rows, all_rows] + [row_block] * 3 + [whole((width, LANES))],
        out_shape=[sized(full)] + [sized(half)] * 4 + [jax.ShapeDtypeStruct((width, LANES), half)],
        scratch_shapes=[
            pltpu.VMEM((rows, width), full),
            pltpu.VMEM((rows, width), full),
            pltpu.VMEM((pairs, count, 2 * DEC_LEN), full),
            pltpu.VMEM((1, width), full),
            pltpu.VMEM((width, LANES), full),
        ],
        compiler_params=params(56),
        cost_estimate=light,
    )(
        mark, query_cross_grad, weights_c, after, gain_two, resid, hidden, gain_one, gain_ffn_grad,
        query, key, value, weights_o, weights_q, weights_k, weights_v, buckets, table,
    )


class Places:
    def __init__(self, dp_size, seq_size):
        self.dp, self.seq = dp_size, seq_size
        self.core = 2 if dp_size % 2 == 0 else 1
        self.ny = dp_size // self.core
        self.nx = self.ny if seq_size % self.ny == 0 else 1
        self.nz = seq_size // self.nx
        self.low = 2 if self.nz % 2 == 0 else 1
        self.high = self.nz // self.low
        dp_index, seq_index = lax.axis_index("dp"), lax.axis_index("seq")
        self.c, self.y = dp_index % self.core, dp_index // self.core
        self.x, self.z = seq_index % self.nx, seq_index // self.nx
        self.place = jnp.stack([self.y, self.c, self.x, self.z // self.low, self.z % self.low]).astype(jnp.int32)

    def shift(self, value, **steps):
        sizes = {"y": self.ny, "c": self.core, "h": self.high, "l": self.low, "x": self.nx}
        flat = lambda p: ((p["y"] * self.core + p["c"]) * self.seq) + (p["h"] * self.low + p["l"]) * self.nx + p["x"]
        pairs = []
        for numbers in itertools.product(*[range(size) for size in sizes.values()]):
            here = dict(zip(sizes, numbers))
            there = {axis: (here[axis] + steps.get(axis, 0)) % size for axis, size in sizes.items()}
            pairs.append((flat(here), flat(there)))
        return lax.ppermute(value, ("dp", "seq"), pairs)


def gate_kernel(*refs):
    refs[-1][...] = jnp.zeros_like(refs[-1])


def gate(*waits):
    arrays = jax.tree.leaves(waits)
    return pl.pallas_call(
        gate_kernel,
        name="gate",
        in_specs=[pl.BlockSpec(memory_space=pl.ANY)] * len(arrays),
        out_shape=jax.ShapeDtypeStruct((8, LANES), full),
        cost_estimate=pl.CostEstimate(flops=10**13, bytes_accessed=10**10, transcendentals=0),
    )(*arrays)


def marked(kernel, scalars=0):
    return lambda *refs: kernel(*refs[:scalars], *refs[scalars + 1 :])


class Term:
    def __init__(self, array, axes, fixed=(), columns=None):
        self.array, self.axes, self.fixed = array, axes, dict(fixed)
        self.columns = columns or (0, array.shape[-1])

    def at(self, axis, place):
        return Term(self.array, self.axes, {**self.fixed, axis: place}, self.columns)

    def free(self):
        sizes = zip(self.axes, self.array.shape)
        return tuple(size for axis, size in sizes if axis not in self.fixed)

    def spec(self):
        shape = [None if axis in self.fixed else size for axis, size in zip(self.axes, self.array.shape)]
        places = [self.fixed.get(axis, 0) for axis in self.axes]
        return pl.BlockSpec((*shape, *self.array.shape[-2:]), lambda i: (*places, 0, 0))


def totals_kernel(*refs, jobs):
    refs = list(refs)
    sources, outs = refs[: -len(jobs)], refs[-len(jobs) :]
    for groups, out in zip(jobs, outs):
        first = 0
        for columns in groups:
            total = None
            for low, high in columns:
                value = sources.pop(0)[..., low:high].astype(full)
                total = value if total is None else total + value
            out[..., first : first + total.shape[-1]] = total.astype(out.dtype)
            first += total.shape[-1]


def totals(mark, jobs, kind=half):
    terms = [term for groups in jobs for group in groups for term in group]
    shape = lambda groups: (
        *groups[0][0].free(),
        groups[0][0].array.shape[-2],
        sum(group[0].columns[1] - group[0].columns[0] for group in groups),
    )
    return pl.pallas_call(
        marked(
            functools.partial(totals_kernel, jobs=[[[term.columns for term in group] for group in groups] for groups in jobs])
        ),
        name="totals",
        grid=(1,),
        in_specs=[anywhere] + [term.spec() for term in terms],
        out_specs=[whole(shape(groups)) for groups in jobs],
        out_shape=[jax.ShapeDtypeStruct(shape(groups), kind) for groups in jobs],
        compiler_params=params(56),
        cost_estimate=light,
    )(mark, *[term.array for term in terms])


def final_kernel(place, *refs, terms, shapes, head_count):
    refs = list(refs)
    sources, outs = refs[: sum(len(columns) for columns in terms)], refs[sum(len(columns) for columns in terms) :]
    for columns, holds in zip(terms, shapes):
        total = None
        for low, high in columns:
            value = sources.pop(0)[..., low:high].astype(full)
            total = value if total is None else total + value
        first = 0
        for hold in holds:
            if hold == "plain":
                outs.pop(0)[...] = total
            elif hold == "pair":
                wide = outs[0].shape[1] * 2
                for out, value in zip(outs[:2], unpaired(total[:, first : first + wide], place[1])):
                    out[...] = value
                outs, first = outs[2:], first + wide
            elif hold == "rows":
                out, m = outs.pop(0), total.shape[0]
                wide = out.shape[1]
                for piece in range(0, out.shape[0] // m, 2):
                    two = unpaired(total[:, piece * wide : (piece + 2) * wide], place[1])
                    out[piece * m : (piece + 1) * m, :] = two[0]
                    out[(piece + 1) * m : (piece + 2) * m, :] = two[1]
            else:
                turned = total[:, first:].T
                for k in range(3):
                    outs.pop(0)[...] = turned[k : k + 1, :]
                bias = outs.pop(0)
                bias[...] = pltpu.roll(total[:, first:], LANES - 16, 1)[: bias.shape[0], :head_count]


def final(mark, at, sums, holds, shapes, head_count):
    terms = [part.terms for part in sums]
    arrays = [term for group in terms for term in group]
    as_prefetch = lambda spec: pl.BlockSpec(spec.block_shape, lambda i, _, index=spec.index_map: index(i))
    return pl.pallas_call(
        marked(
            functools.partial(
                final_kernel,
                terms=[[term.columns for term in group] for group in terms],
                shapes=holds,
                head_count=head_count,
            ),
            1,
        ),
        name="final",
        grid_spec=pltpu.PrefetchScalarGridSpec(
            num_scalar_prefetch=1,
            grid=(1,),
            in_specs=[anywhere] + [as_prefetch(term.spec()) for term in arrays],
            out_specs=[whole(shape) for shape in shapes],
        ),
        out_shape=[jax.ShapeDtypeStruct(shape, full) for shape in shapes],
        compiler_params=params(56),
        cost_estimate=light,
    )(at.place, mark, *[term.array for term in arrays])


class Reduction:
    def __init__(self, at, keep, send, order):
        self.at, self.order = at, order
        self.terms = [Term(keep, "yxhl")]
        if at.core == 2:
            self.terms.append(Term(at.shift(send, c=1), "yxhl"))
        self.left = "yxhl"


def advance(mark, *sums, together=False):
    at = sums[0].at
    axes = [part.order[0] for part in sums]
    size = lambda axis: {"y": at.ny, "x": at.nx, "h": at.high, "l": at.low}[axis]
    group = lambda part, k: [term.at(part.order[0], k) for term in part.terms]
    if together:
        places = [(axes[0], k) for k in range(1, size(axes[0]))]
        jobs = [[group(part, k) for part in sums] for _, k in places]
    else:
        places = [(axis, k) for axis in axes for k in range(1, size(axis))]
        jobs = [[group(part, k)] for part, axis in zip(sums, axes) for k in range(1, size(axis))]
    pieces = list(totals(mark, jobs)) if jobs else []
    got = [at.shift(piece, **{axis: k}) for piece, (axis, k) in zip(pieces, places)]
    first = 0
    for part in sums:
        axis, part.order = part.order[0], part.order[1:]
        part.left = part.left.replace(axis, "")
        part.terms = [term.at(axis, 0) for term in part.terms]
        wide = part.terms[0].columns[1] - part.terms[0].columns[0]
        for _ in range(1, size(axis)):
            if together:
                continue
            part.terms.append(Term(got.pop(0), part.left))
        if together:
            part.terms += [Term(piece, part.left, (), (first, first + wide)) for piece in got]
            first += wide
    return pieces


def shards(
    decoder_in,
    encoder_states,
    encoder_doc,
    decoder_doc,
    cotangent,
    gain_self,
    gain_cross,
    gain_ffn,
    self_query,
    self_key,
    self_value,
    self_out,
    bias_table,
    cross_query,
    cross_key,
    cross_value,
    cross_out,
    ff_in,
    ff_out,
    *,
    dp_size,
    seq_size,
):
    at = Places(dp_size, seq_size)
    width = decoder_in.shape[2]
    head_count = bias_table.shape[1]
    bucket_count = bias_table.shape[0]
    score_scale = (width // head_count) ** (-0.5)
    local_rows = decoder_in.shape[1]
    doc_count = local_rows // DEC_LEN
    position = lax.axis_index("seq")
    own_map = lax.dynamic_slice_in_dim(decoder_doc[0], position * doc_count, doc_count, 0)
    gain_self, gain_cross, gain_ffn = (gain[None, :] for gain in (gain_self, gain_cross, gain_ffn))

    enc_rows = encoder_states.shape[1]
    docs = jnp.pad(encoder_doc.astype(half), ((0, 15), (0, width - enc_rows)))
    shard = jnp.concatenate([encoder_states[0], docs], axis=0)
    near = [at.shift(shard, l=l) for l in range(1, at.low)]
    over = [at.shift(shard, x=x) for x in range(1, at.nx)]
    far = [at.shift(shard, h=h) for h in range(1, at.high)]
    mark = gate(shard)
    own = jnp.pad(own_map.astype(full), (0, LANES - doc_count))[:, None]
    lane = jnp.arange(LANES, dtype=jnp.int32)
    mark = (jnp.arange(local_rows, dtype=jnp.int32)[:, None] // DEC_LEN == lane).astype(half)
    buckets = jnp.asarray(bucket_map(DEC_LEN, bucket_count, MAX_REACH))

    query_self, key_self, value_self, out_self, after_self, normed_two, query_cross, normed_one = self_forward(
        mark, decoder_in[0], gain_self, gain_cross, self_query, self_key, self_value, self_out, cross_query,
        buckets, bias_table, score_scale,
    )
    near, over, far, query_cross = lax.optimization_barrier((near, over, far, query_cross))
    ahead = [at.shift(rows, l=l) for rows in far for l in range(1, at.low)]
    far_over = [[at.shift(rows, x=x) for rows in far] for x in range(1, at.nx)]
    near_over = [[at.shift(rows, x=x) for rows in near] for x in range(1, at.nx)]
    make = functools.partial(
        key_value, own=own, weights_k=cross_key, weights_v=cross_value, rows=enc_rows, doc_count=doc_count
    )
    column = [shard, *near]
    if at.high == 2 and at.low == 2:
        made = make(column, place=0, places=2)
        ahead, far_over, made = lax.optimization_barrier((ahead, far_over, made))
        column += [far[0], *ahead]
        made = make(column[2:], begun=made, place=1, places=2)
    else:
        step = at.low - 1
        for h, rows in enumerate(far):
            column += [rows, *ahead[h * step : (h + 1) * step]]
        made = make(column)
    sources, states, state = [], [], []
    for x in range(at.nx):
        if x:
            part = [over[x - 1], *near_over[x - 1]]
            for rows in far_over[x - 1]:
                part += [rows, *[at.shift(rows, l=l) for l in range(1, at.low)]]
            made = make(part)
        *source, rows = made
        sources.append(source)
        states.append(rows)
        state = cross_forward(query_cross, mark, source, state, x == at.nx - 1, score_scale)
    mixed_cross, out_cross, extended = state
    (
        after_cross, activated, resid_grad, branch_cross, mixed_grad, gain_ffn_grad,
        in_keep, in_send, out_keep, out_send,
    ) = feed_forward(at, after_self, out_cross, cross_out, gain_ffn, ff_in, ff_out, cotangent[0])
    ff_out_sum = Reduction(at, out_keep, out_send, "yxlh")
    ff_in_sum = Reduction(at, in_keep, in_send, "xylh")

    pairs = width // LANES
    cut = 1
    mark = gate(out_send, in_send)
    begun = cross_backward(mark, extended, mixed_grad, mixed_cross, sources, 0, cut, [], score_scale)
    mark = gate(advance(begun[0], ff_out_sum, ff_in_sum))
    query_grad, *grads = cross_backward(
        mark, extended, mixed_grad, mixed_cross, sources, cut, pairs - cut, begun, score_scale
    )
    mark = gate(advance(query_grad, ff_out_sum, ff_in_sum))

    if len(states) * states[0].shape[0] <= FUSED_ROWS:
        shares, cross_keep, cross_send = cross_close(
            mark, at, normed_two, query_grad, out_cross, branch_cross, states, grads, cross_key, cross_value
        )
    else:
        shares = [encoder_part(mark, at, grads[2 * x : 2 * x + 2], cross_key, cross_value) for x in range(at.nx)]
        summed = lambda side: sum(dot(rows, grads[2 * x + side], TN) for x, rows in enumerate(states))
        cross_keep, cross_send = laid_out(
            at, [dot(normed_two, query_grad, TN), dot(out_cross, branch_cross, TN), summed(0), summed(1)]
        )
    early = [at.shift(part[0], x=-1 - k) for k, part in enumerate(shares[1:])]
    late = [at.shift(part[1], x=-1 - k) for k, part in enumerate(shares[1:])]
    cross_sum = Reduction(at, cross_keep, cross_send, "yxlh")
    mark = gate(advance(cross_keep, ff_out_sum, ff_in_sum, together=True))
    mark = gate(shares[1:], cross_send, advance(mark, cross_sum))

    input_grad, branch_self, *self_grads, extra = self_backward(
        mark, at.seq, query_grad, cross_query, after_self, gain_cross, resid_grad, decoder_in[0], gain_self,
        gain_ffn_grad, query_self, key_self, value_self, self_out, self_query, self_key, self_value,
        buckets, bias_table, score_scale,
    )
    (low_ready,) = totals(input_grad, [[[Term(part, "h") for part in (shares[0][0], *early)]]])
    high_terms = [Term(part, "h") for part in (shares[0][1], *late, at.shift(low_ready, l=-1))]
    ready = advance(low_ready, ff_out_sum, ff_in_sum, together=True)
    mark = gate(low_ready, late, ready, advance(ready[0], cross_sum))
    first_keep, first_send, second_keep, second_send = weight_grads(
        mark,
        at,
        [[(normed_one, grad)] for grad in self_grads] + [[(out_self, branch_self)]],
        [[0], [1]],
        extra,
    )
    first_sum = Reduction(at, first_keep, first_send, "yxlh")
    second_sum = Reduction(at, second_keep, second_send, SECOND)
    mark = gate(first_send, second_send)

    n, m = width // at.dp, width // at.seq
    cross_ready = advance(mark, cross_sum)
    mark = gate(cross_ready, advance(cross_ready[0], first_sum, second_sum))
    ff_out_grad, ff_in_grad = final(
        mark, at, [ff_out_sum, ff_in_sum], [["rows"], ["plain"]],
        [(ff_out.shape[0] // at.seq, n), (m, ff_in.shape[1] // at.dp)], head_count,
    )
    activated, ff_in_grad = lax.optimization_barrier((activated, ff_in_grad))
    output = (after_cross + dot(activated, ff_out, NN)).astype(half)
    high_ready = totals(ff_in_grad, [[[term.at("h", h) for term in high_terms]] for h in range(1, at.high)])
    last_terms = [term.at("h", 0) for term in high_terms] + [
        Term(at.shift(piece, h=-1 - k), "") for k, piece in enumerate(high_ready)
    ]
    cross_ready = advance(high_ready[0], cross_sum)
    mark = gate(output, cross_ready, advance(cross_ready[0], first_sum, second_sum))
    mark = gate(advance(mark, first_sum, second_sum, together=True))
    small = (m, n)
    cross_query_grad, cross_out_grad, cross_key_grad, cross_value_grad = final(
        mark, at, [cross_sum], [["pair", "pair"]], [small] * 4, head_count
    )
    ready = advance(cross_value_grad, first_sum, second_sum, together=True)
    mark = gate(ready)
    (encoder_grad,) = totals(mark, [[last_terms]], full)
    mark = encoder_grad
    query_grad, key_grad, value_grad, out_grad, *gains, bias_grad = final(
        mark, at, [first_sum, second_sum], [["pair"], ["pair", "extra"]],
        [small] * 4 + [(1, m)] * 3 + [(bucket_count // at.seq, head_count)], head_count,
    )
    return (
        output[None],
        input_grad[None],
        encoder_grad[None],
        *(gain.reshape(-1) for gain in gains),
        query_grad,
        key_grad,
        value_grad,
        out_grad,
        bias_grad,
        cross_query_grad,
        cross_key_grad,
        cross_value_grad,
        cross_out_grad,
        ff_in_grad,
        ff_out_grad,
    )


def solution(mesh):
    placed = (
        P("dp", "seq", None),
        P("dp", "seq", None),
        P("dp", "seq"),
        P("dp", None),
        P("dp", "seq", None),
    ) + (P(),) * 14
    return jax.shard_map(
        functools.partial(shards, dp_size=mesh.shape["dp"], seq_size=mesh.shape["seq"]),
        mesh=mesh,
        in_specs=placed,
        out_specs=(
            P("dp", "seq", None),
            P("dp", "seq", None),
            P("dp", "seq", None),
            P("seq"),
            P("seq"),
            P("seq"),
            P("seq", "dp"),
            P("seq", "dp"),
            P("seq", "dp"),
            P("seq", "dp"),
            P("seq", None),
            P("seq", "dp"),
            P("seq", "dp"),
            P("seq", "dp"),
            P("seq", "dp"),
            P("seq", "dp"),
            P("seq", "dp"),
        ),
        check_vma=False,
    )
```

```python
import functools
import itertools
import math

import jax
import jax.numpy as jnp
import numpy as np
from jax import lax
from jax.experimental import pallas as pl
from jax.experimental.pallas import tpu as pltpu
from jax.sharding import PartitionSpec as P

MAX_REACH = 128
DEC_LEN = 128


epsilon = 1e-06
masked_fill = -1e30
half = jnp.bfloat16
full = jnp.float32


def bucket_map(length, buckets, max_reach):
    exact_span = buckets // 2
    places = np.arange(length)
    distance = places[None, :] - places[:, None]
    passed = np.zeros_like(distance)
    for threshold_index in range(1, buckets - exact_span):
        threshold = int(
            math.ceil(
                exact_span * (max_reach / exact_span) ** (threshold_index / (buckets - exact_span))
            )
        )
        passed = passed + (distance >= threshold)
    bucket_of = np.where(distance < exact_span, distance, exact_span + passed)
    return np.where(distance < 0, -1, bucket_of).astype(np.int32)


def norm_parts(values):
    inverse = lax.rsqrt(jnp.mean(values * values, axis=-1, keepdims=True) + epsilon)
    return values * inverse, inverse


def norm_backward(upstream, normal, inverse, gain_row):
    scaled = upstream * gain_row
    inner = jnp.mean(scaled * normal, axis=-1, keepdims=True)
    return inverse * (scaled - normal * inner), jnp.sum(upstream * normal, axis=0, keepdims=True)


NT = (((1,), (1,)), ((), ()))
NN = (((1,), (0,)), ((), ()))
TN = (((0,), (0,)), ((), ()))
LANES = 128
ONES = 8
MEGA = 2**20
PAIRS = 2
FUSED_ROWS = 2048
SECOND = "xylh"


def dot(left_side, right_side, dims):
    return lax.dot_general(left_side, right_side, dims, preferred_element_type=full)


def three(value):
    first = value.astype(half).astype(full)
    second = (value - first).astype(half).astype(full)
    return first, second, (value - first - second).astype(half).astype(full)


def placed_three(value, index, rest):
    first, second, third = three(value)
    return jnp.where(
        index == ONES, first, jnp.where(index == ONES + 1, second, jnp.where(index == ONES + 2, third, rest))
    )


def low_lanes(rows):
    return lax.broadcasted_iota(jnp.int32, (rows, LANES), 1) < LANES // 2


def stacked(value, low):
    zero = jnp.zeros_like(value)
    return jnp.concatenate([jnp.where(low, value, zero), jnp.where(low, zero, value)], axis=0)


def loop(count, step, start):
    return lax.fori_loop(0, count, step, start, unroll=count <= 4)


light = pl.CostEstimate(flops=1, bytes_accessed=1, transcendentals=0)


heavy = pl.CostEstimate(flops=10**13, bytes_accessed=10**10, transcendentals=0)


def params(megabytes):
    return pltpu.CompilerParams(vmem_limit_bytes=megabytes * MEGA)


def whole(shape):
    return pl.BlockSpec(shape, lambda *_: (0,) * len(shape))


anywhere = pl.BlockSpec(memory_space=pl.ANY)


class Blocks:
    def __init__(self, at):
        self.core, self.ny, self.nx, self.dp, self.seq = at.core, at.ny, at.nx, at.dp, at.seq
        self.high, self.low = at.high, at.low

    def shape(self, rows, columns):
        return (self.ny, self.nx, self.high, self.low, rows, columns)

    def row_place(self, block, place):
        z = lax.div(block, self.nx)
        return (
            lax.rem(lax.rem(block, self.nx) - place[2] + self.nx, self.nx),
            lax.rem(lax.div(z, self.low) - place[3] + self.high, self.high),
            lax.rem(lax.rem(z, self.low) - place[4] + self.low, self.low),
        )

    def column_place(self, y, place):
        return lax.rem(y - place[0] + self.ny, self.ny)

    def paired(self, first, second, place):
        n = first.shape[1] // self.core
        if self.core == 1:
            return jnp.concatenate([first, second], axis=1).astype(half), None
        mine = place[1] == 0
        if n % LANES != LANES // 2:
            cut = [jnp.concatenate([g[:, c * n : (c + 1) * n] for g in (first, second)], axis=1) for c in range(2)]
        else:
            main = n - LANES // 2
            low = lax.broadcasted_iota(jnp.int32, (first.shape[0], LANES), 1) < LANES // 2
            one, two = (g[:, main : main + LANES] for g in (first, second))
            sides = (
                jnp.where(low, one, pltpu.roll(two, LANES // 2, 1)),
                jnp.where(low, pltpu.roll(one, LANES // 2, 1), two),
            )
            cut = [
                jnp.concatenate([first[:, at : at + main], second[:, at : at + main], sides[c]], axis=1)
                for c, at in enumerate((0, main + LANES))
            ]
        return jnp.where(mine, cut[0], cut[1]).astype(half), jnp.where(mine, cut[1], cut[0]).astype(half)


def unpaired(piece, core):
    n = piece.shape[1] // 2
    if n % LANES != LANES // 2:
        return piece[:, :n], piece[:, n:]
    main = n - LANES // 2
    side = piece[:, 2 * main :]
    turned = pltpu.roll(side, LANES // 2, 1)
    out = []
    for k in range(2):
        big = piece[:, k * main : (k + 1) * main]
        first, second = (side, turned) if k == 0 else (turned, side)
        after = jnp.concatenate([big, first], axis=1)
        ahead = pltpu.roll(jnp.concatenate([big, second], axis=1), LANES // 2, 1)
        out.append(jnp.where(core == 0, after, ahead)[:, :n])
    return out


def position_bias(buckets, table, pair):
    out = []
    for head in range(2):
        bias = jnp.full(buckets.shape, masked_fill, full)
        for b in range(table.shape[0]):
            bias = jnp.where(buckets == b, table[b, 2 * pair + head], bias)
        out.append(bias)
    return jnp.concatenate(out, axis=1)


def self_forward_kernel(
    hidden, gain_one, gain_two, weights_q, weights_k, weights_v, weights_o, weights_c, buckets, table,
    query, key, value, mixed, after, normed_two, query_cross, normed, every, *, scale,
):
    step = pl.program_id(0)
    rows = hidden.shape[0]

    @pl.when(step == 0)
    def _():
        normal, _ = norm_parts(hidden[...].astype(full))
        normed[...] = (normal * gain_one[...]).astype(half)

    many = query.shape[1] // LANES
    wide = many * LANES
    weights = jnp.concatenate([weights_q[...], weights_k[...], weights_v[...]], axis=1)
    made = dot(normed[...], weights, NN).astype(half)
    query[...] = made[:, :wide] * scale
    key[...] = made[:, wide : 2 * wide]
    value[...] = made[:, 2 * wide :]
    low = low_lanes(DEC_LEN)
    bias = [position_bias(buckets[...], table, step * many + pair) for pair in range(many)]
    work = [
        (pair, slice(pair * LANES, (pair + 1) * LANES), pl.ds(first, DEC_LEN))
        for pair in range(many)
        for first in range(0, rows, DEC_LEN)
    ]
    scores = [dot(key[at, own], stacked(query[at, own], low), NT) + bias[pair] for pair, own, at in work]
    expos = []
    for score in scores:
        expo = jnp.exp(score - jnp.max(score, axis=0, keepdims=True))
        expos.append((expo / jnp.sum(expo, axis=0, keepdims=True)).astype(half))
    for (pair, own, at), expo in zip(work, expos):
        both = dot(value[at, own], expo, TN).T
        one = jnp.where(low, both[:DEC_LEN], both[DEC_LEN:]).astype(half)
        mixed[at, own] = one
        every[at, pl.ds(pl.multiple_of(step * wide + pair * LANES, LANES), LANES)] = one

    @pl.when(step == pl.num_programs(0) - 1)
    def _():
        total = hidden[...].astype(full) + dot(every[...], weights_o[...], NN)
        after[...] = total
        normal, _ = norm_parts(total)
        again = (normal * gain_two[...]).astype(half)
        normed_two[...] = again
        query_cross[...] = dot(again, weights_c[...], NN).astype(half)


def self_forward(mark, hidden, gain_one, gain_two, weights_q, weights_k, weights_v, weights_o, weights_c, buckets, table, scale):
    rows, width = hidden.shape
    pairs = width // LANES
    many = PAIRS
    column = lambda i: (0, i)
    row_block = pl.BlockSpec((rows, many * LANES), column)
    weight_block = pl.BlockSpec((width, many * LANES), column)
    return pl.pallas_call(
        marked(functools.partial(self_forward_kernel, scale=scale)),
        name="self_forward",
        grid=(pairs // many,),
        in_specs=[anywhere, whole((rows, width)), whole((1, width)), whole((1, width))]
        + [weight_block] * 3
        + [whole((width, width))] * 2
        + [whole((DEC_LEN, DEC_LEN)), pl.BlockSpec(memory_space=pltpu.SMEM)],
        out_specs=[row_block] * 4 + [whole((rows, width))] * 4,
        out_shape=[jax.ShapeDtypeStruct((rows, width), half)] * 4
        + [jax.ShapeDtypeStruct((rows, width), kind) for kind in (full, half, half, half)],
        scratch_shapes=[pltpu.VMEM((rows, width), half)],
        compiler_params=params(56),
        cost_estimate=light,
    )(mark, hidden, gain_one, gain_two, weights_q, weights_k, weights_v, weights_o, weights_c, buckets, table)


def key_value_kernel(*refs, rows, doc_count):
    shards, (own, weights_k, weights_v, keys, values, mask, states) = refs[:-7], refs[-7:]
    for i, shard in enumerate(shards):
        at = pl.ds(i * rows, rows)
        states[at, :] = shard[:rows, :]
        keys[at, :] = dot(shard[:rows, :], weights_k[...], NN).astype(half)
        values[at, :] = dot(shard[:rows, :], weights_v[...], NN).astype(half)
        docs = shard[rows : rows + 1, :rows].astype(full)
        lane = lax.broadcasted_iota(jnp.int32, (LANES, rows), 0)
        ones = ((lane >= ONES) & (lane < ONES + 3)).astype(full)
        extra = jnp.where(lane < doc_count, jnp.where(docs == own[:, :1], 0.0, masked_fill), ones)
        mask[at, :] = extra.T.astype(half)


def key_value(shards, own, weights_k, weights_v, rows, doc_count, begun=(), place=0, places=1):
    width = shards[0].shape[1]
    count = len(shards) * rows
    sizes = (width, width, LANES, width)
    kernel = functools.partial(key_value_kernel, rows=rows, doc_count=doc_count)
    return pl.pallas_call(
        lambda *refs: kernel(*refs[len(begun) :]),
        name="key_value",
        grid=(1,),
        in_specs=[anywhere] * len(begun) + [whole(array.shape) for array in (*shards, own, weights_k, weights_v)],
        out_specs=[pl.BlockSpec((count, size), lambda i: (place, 0)) for size in sizes],
        out_shape=[jax.ShapeDtypeStruct((places * count, size), half) for size in sizes],
        input_output_aliases={i: i for i in range(len(begun))},
        compiler_params=params(56),
        cost_estimate=light,
    )(*begun, *shards, own, weights_k, weights_v)


def cross_forward_kernel(*refs, scale, block, opens, closes):
    query, mark, keys, values, mask = refs[:5]
    refs = refs[5:]
    if not opens:
        state_in, refs = refs[:2], refs[2:]
    if closes:
        (mixed, mixed_half, extended), refs = refs[:3], refs[3:]
    else:
        state_out, refs = refs[:2], refs[2:]
    total, wide = refs
    rows, many = query.shape[0], query.shape[1] // LANES
    low = low_lanes(rows)
    for pair in range(many):
        wide[pair, :, :LANES] = stacked(query[:, pair * LANES : (pair + 1) * LANES] * scale, low)
        wide[pair, :rows, LANES:] = mark[...]
        wide[pair, rows:, LANES:] = mark[...]
    if opens:
        total[...] = jnp.zeros_like(total)
        carry = [(jnp.full((1, 2 * rows), masked_fill, full), jnp.zeros((1, 2 * rows), full)) for _ in range(many)]
    else:
        total[...] = state_in[0][...]
        carry = [(state_in[1][pair, 0:1], state_in[1][pair, 1:2]) for pair in range(many)]

    def step(i, carry):
        at = pl.ds(pl.multiple_of(i * block, block), block)
        scores = [
            dot(jnp.concatenate([keys[at, pair * LANES : (pair + 1) * LANES], mask[at, :]], axis=1), wide[pair], NT)
            for pair in range(many)
        ]
        out = []
        for pair, (peak, amount) in enumerate(carry):
            fresh = jnp.maximum(peak, jnp.max(scores[pair], axis=0, keepdims=True))
            expo = jnp.exp(scores[pair] - fresh)
            fade = jnp.exp(peak - fresh)
            values_here = values[at, pair * LANES : (pair + 1) * LANES]
            total[pair] = total[pair] * fade + dot(values_here, expo.astype(half), TN)
            out.append((fresh, amount * fade + jnp.sum(expo, axis=0, keepdims=True)))
        return out

    carry = loop(keys.shape[0] // block, step, carry)
    if not closes:
        state_out[0][...] = total[...]
        for pair, (peak, amount) in enumerate(carry):
            state_out[1][pair, 0:1] = peak
            state_out[1][pair, 1:2] = amount
        return
    index = lax.broadcasted_iota(jnp.int32, (LANES, 2 * rows), 0)
    for pair, (peak, amount) in enumerate(carry):
        at = slice(pair * LANES, (pair + 1) * LANES)
        both = (total[pair] / amount).T
        one = jnp.where(low, both[:rows], both[rows:])
        mixed[:, at] = one
        mixed_half[:, at] = one.astype(half)
        extra = placed_three(-(peak + jnp.log(amount)), index, 0.0).T
        extended[pair, :, :LANES] = wide[pair, :, :LANES]
        extended[pair, :, LANES:] = (wide[pair, :, LANES:].astype(full) + extra).astype(half)


def cross_forward(query, mark, source, state, closes, scale):
    rows, pairs, many = query.shape[0], query.shape[1] // LANES, PAIRS
    count = source[0].shape[0]
    column = lambda i: (0, i)
    plane = lambda i: (i, 0, 0)
    block = min(1024, count)
    state_specs = [pl.BlockSpec((many, LANES, 2 * rows), plane), pl.BlockSpec((many, 2, 2 * rows), plane)]
    state_shape = [
        jax.ShapeDtypeStruct((pairs, LANES, 2 * rows), full),
        jax.ShapeDtypeStruct((pairs, 2, 2 * rows), full),
    ]
    last_specs = [pl.BlockSpec((rows, many * LANES), column)] * 2 + [pl.BlockSpec((many, 2 * rows, 2 * LANES), plane)]
    last_shape = [
        jax.ShapeDtypeStruct(query.shape, full),
        jax.ShapeDtypeStruct(query.shape, half),
        jax.ShapeDtypeStruct((pairs, 2 * rows, 2 * LANES), half),
    ]
    return pl.pallas_call(
        functools.partial(cross_forward_kernel, scale=scale, block=block, opens=not state, closes=closes),
        name="cross_forward",
        grid=(pairs // many,),
        in_specs=[pl.BlockSpec((rows, many * LANES), column), whole((rows, LANES))]
        + [pl.BlockSpec((count, many * LANES), column), pl.BlockSpec((count, many * LANES), column), whole((count, LANES))]
        + (state_specs if state else []),
        out_specs=last_specs if closes else state_specs,
        out_shape=last_shape if closes else state_shape,
        scratch_shapes=[
            pltpu.VMEM((many, LANES, 2 * rows), full),
            pltpu.VMEM((many, 2 * rows, 2 * LANES), half),
        ],
        compiler_params=params(56),
        cost_estimate=light,
    )(query, mark, *source, *state)


def cross_backward_kernel(*refs, scale, block, parts):
    extended, upstream, mixed = refs[:3]
    sources = [refs[3 + 3 * i : 6 + 3 * i] for i in range(parts)]
    query_grad = refs[3 + 3 * parts]
    grads = [refs[4 + 3 * parts + 2 * i : 6 + 3 * parts + 2 * i] for i in range(parts)]
    wide, total = refs[-2:]
    rows = upstream.shape[0]
    low = low_lanes(rows)
    lane = lax.broadcasted_iota(jnp.int32, (rows, LANES), 1)
    each = upstream[...].astype(full) * mixed[...]
    wide[:, :LANES] = stacked(upstream[...], low)
    for head in range(2):
        inner = jnp.sum(jnp.where(low == (head == 0), each, 0.0), axis=1, keepdims=True)
        wide[head * rows : (head + 1) * rows, LANES:] = placed_three(-inner, lane, 0.0).astype(half)
    total[...] = jnp.zeros_like(total)
    for (keys, values, mask), (key_grad, value_grad) in zip(sources, grads):

        def step(i, carry):
            at = pl.ds(pl.multiple_of(i * block, block), block)
            extra = mask[at, :]
            expo = jnp.exp(dot(jnp.concatenate([keys[at, :], extra], axis=1), extended[0], NT))
            change = dot(jnp.concatenate([values[at, :], extra], axis=1), wide[...], NT)
            score = (expo * change).astype(half)
            value_grad[at, :] = dot(expo.astype(half), wide[:, :LANES], NN).astype(half)
            key_grad[at, :] = dot(score, extended[0, :, :LANES], NN).astype(half)
            total[...] += dot(keys[at, :], score, TN)
            return carry

        loop(keys.shape[0] // block, step, 0)
    both = total[...].T
    query_grad[...] = (jnp.where(low, both[:rows], both[rows:]) * scale).astype(half)


def cross_backward(mark, extended, upstream, mixed, sources, first, pairs, begun, scale):
    rows, width = upstream.shape
    count = sources[0][0].shape[0]
    every = count * len(sources)
    column = lambda i: (0, i + first)
    block = min(1024, count)
    row_block, key_block = pl.BlockSpec((rows, LANES), column), pl.BlockSpec((count, LANES), column)
    operands = [extended, upstream, mixed, *[array for source in sources for array in source]]
    kernel = functools.partial(cross_backward_kernel, scale=scale, block=block, parts=len(sources))
    return pl.pallas_call(
        marked(lambda *refs: kernel(*refs[len(begun) :]), len(begun)),
        name="cross_backward",
        grid=(pairs,),
        in_specs=[anywhere] * (len(begun) + 1)
        + [pl.BlockSpec((1, 2 * rows, 2 * LANES), lambda i: (i + first, 0, 0)), row_block, row_block]
        + [key_block, key_block, whole((count, LANES))] * len(sources),
        out_specs=[row_block] + [key_block] * (2 * len(sources)),
        out_shape=[jax.ShapeDtypeStruct((rows, width), half)]
        + [jax.ShapeDtypeStruct((count, width), half)] * (2 * len(sources)),
        scratch_shapes=[
            pltpu.VMEM((2 * rows, 2 * LANES), half),
            pltpu.VMEM((LANES, 2 * rows), full),
        ],
        input_output_aliases={i: i for i in range(len(begun))},
        compiler_params=params(56),
        cost_estimate=heavy,
    )(*begun, mark, *operands)


def feed_forward_kernel(
    place, after, mixed, weights_o, gain, weights_in, weights_out, cotangent,
    after_cross, activated, resid, branch, mixed_grad, gain_grad, in_keep, in_send, out_keep, out_send,
    normed, total, *, blocks,
):
    step = pl.program_id(0)

    @pl.when(step == 0)
    def _():
        values = after[...] + dot(mixed[...], weights_o[...], NN)
        after_cross[...] = values
        normal, _ = norm_parts(values)
        normed[...] = (normal * gain[...]).astype(half)
        total[...] = jnp.zeros_like(total)

    upstream = cotangent[...]
    pre = dot(normed[...], weights_in[...], NN)
    square = pre * pre
    slope = math.sqrt(2.0 / math.pi)
    bend = jnp.tanh(slope * (pre + 0.044715 * (square * pre)))
    act = (0.5 * pre * (1.0 + bend)).astype(half)
    activated[...] = act
    gelu_grad = 0.5 * (1.0 + bend) + 0.5 * pre * (1.0 - bend * bend) * (slope * (1.0 + 3 * 0.044715 * square))
    pre_grad = (dot(upstream, weights_out[...], NT) * gelu_grad).astype(half)
    total[...] += dot(pre_grad, weights_in[...], NT)

    grad = dot(normed[...], pre_grad, TN).astype(half)
    m = grad.shape[0] // blocks.seq
    to_y = blocks.column_place(lax.div(step, blocks.core), place)
    ours = lax.rem(step, blocks.core) == place[1]

    def fill(target):
        for block in range(blocks.seq):
            to_x, to_h, to_l = blocks.row_place(jnp.int32(block), place)
            target[to_y, to_x, to_h, to_l] = grad[block * m : (block + 1) * m]

    pl.when(ours)(lambda: fill(in_keep))
    pl.when(jnp.logical_not(ours))(lambda: fill(in_send))

    grad = dot(act, upstream, TN)
    wide = grad.shape[1] // blocks.ny
    n = wide // blocks.core
    pieces = out_keep.shape[5] // n
    many = pieces * m
    for y in range(blocks.ny):
        at = slice(y * wide, (y + 1) * wide)
        to_y = blocks.column_place(jnp.int32(y), place)
        for block in range(grad.shape[0] // many):
            to_x, to_h, to_l = blocks.row_place(step * (grad.shape[0] // many) + block, place)
            for piece in range(0, pieces, 2):
                first = block * many + piece * m
                kept, sent = blocks.paired(grad[first : first + m, at], grad[first + m : first + 2 * m, at], place)
                out_keep[to_y, to_x, to_h, to_l, :, piece * n : (piece + 2) * n] = kept
                if sent is not None:
                    out_send[to_y, to_x, to_h, to_l, :, piece * n : (piece + 2) * n] = sent

    @pl.when(step == pl.num_programs(0) - 1)
    def _():
        normal, inverse = norm_parts(after_cross[...])
        change, gain_sum = norm_backward(total[...], normal, inverse, gain[...])
        gain_grad[...] = gain_sum
        change = change + upstream.astype(full)
        resid[...] = change
        rounded = change.astype(half)
        branch[...] = rounded
        mixed_grad[...] = dot(rounded, weights_o[...], NT).astype(half)


def feed_forward(at, after, mixed, weights_o, gain, weights_in, weights_out, cotangent):
    rows, width = after.shape
    depth = weights_in.shape[1]
    blocks = Blocks(at)
    cut = depth // at.dp
    shape = blocks.shape(width // at.seq, cut)
    all_rows = whole((rows, width))
    sized = lambda kind: jax.ShapeDtypeStruct((rows, width), kind)
    return pl.pallas_call(
        functools.partial(feed_forward_kernel, blocks=blocks),
        name="feed_forward",
        grid_spec=pltpu.PrefetchScalarGridSpec(
            num_scalar_prefetch=1,
            grid=(at.dp,),
            in_specs=[
                all_rows,
                all_rows,
                whole((width, width)),
                whole((1, width)),
                pl.BlockSpec((width, cut), lambda i, _: (0, i)),
                pl.BlockSpec((cut, width), lambda i, _: (i, 0)),
                all_rows,
            ],
            out_specs=[all_rows, pl.BlockSpec((rows, cut), lambda i, _: (0, i))]
            + [all_rows] * 3
            + [whole((1, width))]
            + [whole(shape)] * 4,
            scratch_shapes=[pltpu.VMEM((rows, width), half), pltpu.VMEM((rows, width), full)],
        ),
        out_shape=[sized(full), jax.ShapeDtypeStruct((rows, depth), half), sized(full), sized(half), sized(half)]
        + [jax.ShapeDtypeStruct((1, width), full)]
        + [jax.ShapeDtypeStruct(shape, half)] * 4,
        compiler_params=params(56),
        cost_estimate=light,
    )(at.place, after, mixed, weights_o, gain, weights_in, weights_out, cotangent)


def encoder_part_kernel(key_grad, value_grad, weights_k, weights_v, early, late, *, early_steps):
    total = dot(key_grad[...], weights_k[...], NT) + dot(value_grad[...], weights_v[...], NT)
    is_early = pl.program_id(0) < early_steps

    @pl.when(is_early)
    def _():
        early[...] = total.astype(half)

    @pl.when(jnp.logical_not(is_early))
    def _():
        late[...] = total.astype(half)


def encoder_part(mark, at, grads, weights_k, weights_v):
    width = weights_k.shape[0]
    rows = grads[0].shape[0] // at.nz
    early = at.high * (at.low - 1)
    plane = lambda size: jax.ShapeDtypeStruct((size, rows, width), half)
    block = pl.BlockSpec((rows, width), lambda i: (i % at.high * at.low + at.low - 1 - i // at.high, 0))
    return pl.pallas_call(
        marked(functools.partial(encoder_part_kernel, early_steps=early)),
        name="encoder_part",
        grid=(at.nz,),
        in_specs=[anywhere, block, block, whole((width, width)), whole((width, width))],
        out_specs=[
            pl.BlockSpec((None, rows, width), lambda i: (jnp.minimum(i, early - 1), 0, 0)),
            pl.BlockSpec((None, rows, width), lambda i: (jnp.maximum(i - early, 0), 0, 0)),
        ],
        out_shape=[plane(early), plane(at.high)],
        compiler_params=params(56),
        cost_estimate=light,
    )(mark, *grads, weights_k, weights_v)


def weight_grads_kernel(place, *refs, blocks, counts, chunks, extra, wide):
    refs = list(refs)
    sides = [[(refs.pop(0), refs.pop(0)) for _ in range(count)] for count in counts]
    small = refs.pop(0) if extra else None
    made = [sum((dot(left[...], right[...], TN) for left, right in side[1:]), dot(side[0][0][...], side[0][1][...], TN)) for side in sides]
    m = made[0].shape[0] // blocks.seq
    many = made[0].shape[1] // wide
    for chunk, pairs in enumerate(chunks):
        keep, send = refs[2 * chunk], refs[2 * chunk + 1]
        for y in range(many):
            at = slice(y * wide, (y + 1) * wide)
            columns = [blocks.paired(made[2 * pair][:, at], made[2 * pair + 1][:, at], place) for pair in pairs]
            if extra and chunk == len(chunks) - 1:
                columns.append((small[...], small[...]))
            to_y = blocks.column_place(jnp.int32(y), place) if many > 1 else 0
            for block in range(blocks.seq):
                to_x, to_h, to_l = blocks.row_place(jnp.int32(block), place)
                rows = slice(block * m, (block + 1) * m)
                first = 0
                for ours, theirs in columns:
                    to = slice(first, first + ours.shape[1])
                    keep[to_y, to_x, to_h, to_l, :, to] = ours[rows]
                    send[to_y, to_x, to_h, to_l, :, to] = theirs[rows]
                    first += ours.shape[1]


def weight_grads(mark, at, sides, chunks, extra=None):
    blocks = Blocks(at)
    width = sides[0][0][0].shape[1]
    wide, m = width // at.ny, width // at.seq
    shapes = [blocks.shape(m, len(pairs) * 2 * wide // at.core) for pairs in chunks]
    if extra is not None:
        shapes[-1] = (*shapes[-1][:-1], shapes[-1][-1] + extra.shape[1])
    terms = [term for side in sides for term in side]
    steps = at.ny if wide % LANES == 0 else 1
    from_y = lambda i, place: (0, lax.rem(i + place[0], at.ny) if steps > 1 else 0)
    out_block = lambda shape: pl.BlockSpec((shape[0] // steps, *shape[1:]), lambda i, place: (i, 0, 0, 0, 0, 0))
    return pl.pallas_call(
        marked(
            functools.partial(
                weight_grads_kernel,
                blocks=blocks,
                counts=[len(side) for side in sides],
                chunks=chunks,
                extra=extra is not None,
                wide=wide,
            ),
            1,
        ),
        name="weight_grads",
        grid_spec=pltpu.PrefetchScalarGridSpec(
            num_scalar_prefetch=1,
            grid=(steps,),
            in_specs=[anywhere]
            + [
                spec
                for left, right in terms
                for spec in (whole(left.shape), pl.BlockSpec((right.shape[0], width // steps), from_y))
            ]
            + ([whole(extra.shape)] if extra is not None else []),
            out_specs=[out_block(shape) for shape in shapes for _ in range(2)],
        ),
        out_shape=[jax.ShapeDtypeStruct(shape, half) for shape in shapes for _ in range(2)],
        compiler_params=params(60),
        cost_estimate=light,
    )(at.place, mark, *[array for term in terms for array in term], *([extra] if extra is not None else []))


def laid_out(at, grads):
    out = []
    for grad in grads:
        m, n = grad.shape[0] // at.seq, grad.shape[1] // at.dp
        assert n % LANES != LANES // 2
        blocks = grad.astype(half).reshape(at.high, at.low, at.nx, m, at.ny, at.core, n)
        places = ((0, at.z // at.low, at.high), (1, at.z % at.low, at.low), (2, at.x, at.nx), (4, at.y, at.ny), (5, at.c, at.core))
        for axis, own, size in places:
            blocks = jnp.take(blocks, (own + jnp.arange(size)) % size, axis=axis)
        out.append(blocks.transpose(5, 4, 2, 0, 1, 3, 6))
    both = jnp.concatenate(out, axis=-1)
    return both[0], both[1]


def cross_close_kernel(place, *refs, blocks, parts):
    count = 3 * parts + 6
    arrays, refs = refs[:count], refs[count:]
    shares, (keep, send), refs = refs[: 2 * parts], refs[2 * parts : 2 * parts + 2], refs[2 * parts + 2 :]
    held, refs = refs[:count], refs[count:]
    made, (keep_held, send_held, arrived, gone) = refs[:parts], refs[parts:]
    ins = [pltpu.make_async_copy(array, place_held, arrived.at[i]) for i, (array, place_held) in enumerate(zip(arrays, held))]
    grads, (weights_k, weights_v), states = held[: 2 * parts], held[2 * parts : 2 * parts + 2], held[2 * parts + 2 : -4]
    normed, query_grad, mixed, branch = held[-4:]
    outs = []

    def leave(source, target):
        copy = pltpu.make_async_copy(source, target, gone.at[len(outs)])
        copy.start()
        outs.append(copy)

    order = [*range(1, parts), 0]
    first = [i for x in order[:1] for i in (2 * x, 2 * x + 1)] + [2 * parts, 2 * parts + 1]
    for i in first + [i for i in range(count) if i not in first]:
        ins[i].start()
    ins[2 * parts].wait()
    ins[2 * parts + 1].wait()
    rows = grads[0].shape[0] // (blocks.high * blocks.low)
    early_size = blocks.low - 1
    for x in order:
        ins[2 * x].wait()
        ins[2 * x + 1].wait()
        for block in range(blocks.high * blocks.low):
            at = slice(block * rows, (block + 1) * rows)
            total = dot(grads[2 * x][at, :], weights_k[...], NT) + dot(grads[2 * x + 1][at, :], weights_v[...], NT)
            made[x][at, :] = total.astype(half)
        for block in range(blocks.high * blocks.low):
            h, l = divmod(block, blocks.low)
            source = made[x].at[pl.ds(block * rows, rows), :]
            leave(source, shares[2 * x].at[(blocks.low - 1 - l) * blocks.high + h] if l else shares[2 * x + 1].at[h])

    def place_pair(one, two, offset):
        m, wide = one.shape[0] // blocks.seq, one.shape[1] // blocks.ny
        for y in range(blocks.ny):
            at = slice(y * wide, (y + 1) * wide)
            ours, theirs = blocks.paired(one[:, at], two[:, at], place)
            to_y = blocks.column_place(jnp.int32(y), place)
            to = slice(offset, offset + ours.shape[1])
            for block in range(blocks.seq):
                to_x, to_h, to_l = blocks.row_place(jnp.int32(block), place)
                own = slice(block * m, (block + 1) * m)
                keep_held[to_y, to_x, to_h, to_l, :, to] = ours[own]
                send_held[to_y, to_x, to_h, to_l, :, to] = theirs[own]
        for source, target in ((send_held, send), (keep_held, keep)):
            leave(source.at[:, :, :, :, :, to], target.at[:, :, :, :, :, to])

    n = keep_held.shape[5] // 4
    for copy in ins[2 * parts + 2 : -4]:
        copy.wait()
    total = []
    for kind in range(2):
        terms = [dot(states[x][...], grads[2 * x + kind][...], TN) for x in range(parts)]
        total.append(sum(terms[1:], terms[0]))
    place_pair(total[0], total[1], 2 * n)
    for copy in ins[-4:]:
        copy.wait()
    place_pair(dot(normed[...], query_grad[...], TN), dot(mixed[...], branch[...], TN), 0)
    for copy in outs:
        copy.wait()


def cross_close(mark, at, normed, query_grad, mixed, branch, states, grads, weights_k, weights_v):
    blocks, parts = Blocks(at), len(states)
    count, width = states[0].shape
    shape = blocks.shape(width // at.seq, 4 * width // at.dp)
    arrays = [*grads, weights_k, weights_v, *states, normed, query_grad, mixed, branch]
    plane = lambda size: jax.ShapeDtypeStruct((size, count // at.nz, width), half)
    outs = [plane(at.high * (at.low - 1)), plane(at.high)] * parts + [jax.ShapeDtypeStruct(shape, half)] * 2
    made = pl.pallas_call(
        marked(functools.partial(cross_close_kernel, blocks=blocks, parts=parts), 1),
        name="cross_close",
        in_specs=[pl.BlockSpec(memory_space=pltpu.SMEM)] + [anywhere] * (len(arrays) + 1),
        out_specs=[anywhere] * len(outs),
        out_shape=outs,
        scratch_shapes=[pltpu.VMEM(array.shape, half) for array in arrays]
        + [pltpu.VMEM((count, width), half)] * parts
        + [pltpu.VMEM(shape, half)] * 2
        + [pltpu.SemaphoreType.DMA((len(arrays),)), pltpu.SemaphoreType.DMA((parts * at.nz + 4,))],
        compiler_params=params(56),
        cost_estimate=heavy,
    )(at.place, mark, *arrays)
    return [made[2 * x : 2 * x + 2] for x in range(parts)], *made[-2:]


def self_backward_kernel(
    query_cross_grad, weights_c, after, gain_two, resid_in, hidden, gain_one, gain_ffn_grad,
    query, key, value, weights_ob, weights_q, weights_k, weights_v, buckets, table,
    input_grad, branch, query_grad, key_grad, value_grad, extra,
    resid, total, bias_rows, gain_two_grad, columns, *, scale, shares,
):
    step = pl.program_id(0)
    rows, width = hidden.shape

    @pl.when(step == 0)
    def _():
        normal, inverse = norm_parts(after[...])
        up = dot(query_cross_grad[...], weights_c[...], NT)
        change, gain_sum = norm_backward(up, normal, inverse, gain_two[...])
        gain_two_grad[...] = gain_sum
        change = change + resid_in[...]
        resid[...] = change
        branch[...] = change.astype(half)
        total[...] = jnp.zeros_like(total)

    low = low_lanes(DEC_LEN)
    many = query.shape[1] // LANES
    upstream = dot(branch[...], weights_ob[...], NT).astype(half)
    count = bias_rows.shape[1]
    of_pair = jnp.concatenate([buckets[...], buckets[...]], axis=1)
    work = [(pair, pl.ds(first, DEC_LEN)) for pair in range(many) for first in range(0, rows, DEC_LEN)]
    spans = [slice(pair * LANES, (pair + 1) * LANES) for pair in range(many)]
    bias = [position_bias(buckets[...], table, step * many + pair) for pair in range(many)]
    wides = [stacked(query[at, spans[pair]], low) for pair, at in work]
    up = [stacked(upstream[at.start : at.start + DEC_LEN, spans[pair]], low) for pair, at in work]
    scores = [dot(key[at, spans[pair]], wide, NT) + bias[pair] for (pair, at), wide in zip(work, wides)]
    changes = [dot(value[at, spans[pair]], grad, NT) for (pair, at), grad in zip(work, up)]
    summed = [None] * many
    for (pair, at), wide, grad, score, change in zip(work, wides, up, scores, changes):
        own = spans[pair]
        expo = jnp.exp(score - jnp.max(score, axis=0, keepdims=True))
        expo = expo / jnp.sum(expo, axis=0, keepdims=True)
        rounded = (expo * (change - jnp.sum(expo * change, axis=0, keepdims=True))).astype(half)
        both = dot(key[at, own], rounded, TN).T
        query_grad[at, own] = (jnp.where(low, both[:DEC_LEN], both[DEC_LEN:]) * scale).astype(half)
        key_grad[at, own] = dot(rounded, wide, NN).astype(half)
        value_grad[at, own] = dot(expo.astype(half), grad, NN).astype(half)
        summed[pair] = rounded.astype(full) if summed[pair] is None else summed[pair] + rounded.astype(full)
    made = jnp.concatenate([query_grad[...], key_grad[...], value_grad[...]], axis=1)
    total[...] += dot(made, jnp.concatenate([weights_q[...], weights_k[...], weights_v[...]], axis=1), NT)
    for pair in range(many):
        sums = [jnp.sum(jnp.where(of_pair == b, summed[pair], 0.0), axis=0, keepdims=True) for b in range(count)]
        bias_rows[step * many + pair] = jnp.concatenate(sums, axis=0)

    @pl.when(step == pl.num_programs(0) - 1)
    def _():
        normal, inverse = norm_parts(hidden[...].astype(full))
        change, gain_sum = norm_backward(total[...], normal, inverse, gain_one[...])
        input_grad[...] = resid[...] + change

        index = lax.broadcasted_iota(jnp.int32, (LANES, width), 0)
        gains = jnp.where(
            index == 0,
            gain_sum,
            jnp.where(index == 1, gain_two_grad[...], jnp.where(index == 2, gain_ffn_grad[...], 0.0)),
        )
        columns[...] = gains.T
        lane = lax.broadcasted_iota(jnp.int32, (count, LANES), 1)
        sums = jnp.zeros((count, LANES), full)
        for pair in range(bias_rows.shape[0]):
            for head in range(2):
                part = bias_rows[pair, :, head * LANES : (head + 1) * LANES]
                sums = jnp.where(lane == 16 + 2 * pair + head, jnp.sum(part, axis=1, keepdims=True), sums)
        m, each = width // shares, count // shares
        for block in range(shares):
            at = slice(block * m, block * m + each)
            columns[at, :] = columns[at, :] + sums[block * each : (block + 1) * each]
        extra[...] = columns[...].astype(half)


def self_backward(
    mark, shares, query_cross_grad, weights_c, after, gain_two, resid, hidden, gain_one, gain_ffn_grad,
    query, key, value, weights_o, weights_q, weights_k, weights_v, buckets, table, scale,
):
    rows, width = hidden.shape
    pairs, count = width // LANES, table.shape[0]
    many = PAIRS
    row_block = pl.BlockSpec((rows, many * LANES), lambda i: (0, i))
    weight_block = pl.BlockSpec((width, many * LANES), lambda i: (0, i))
    all_rows, line = whole((rows, width)), whole((1, width))
    sized = lambda kind: jax.ShapeDtypeStruct((rows, width), kind)
    return pl.pallas_call(
        marked(functools.partial(self_backward_kernel, scale=scale, shares=shares)),
        name="self_backward",
        grid=(pairs // many,),
        in_specs=[anywhere, all_rows, whole((width, width)), all_rows, line, all_rows, all_rows, line, line]
        + [row_block] * 3
        + [pl.BlockSpec((many * LANES, width), lambda i: (i, 0))]
        + [weight_block] * 3
        + [whole((DEC_LEN, DEC_LEN)), pl.BlockSpec(memory_space=pltpu.SMEM)],
        out_specs=[all_rows, all_rows] + [row_block] * 3 + [whole((width, LANES))],
        out_shape=[sized(full)] + [sized(half)] * 4 + [jax.ShapeDtypeStruct((width, LANES), half)],
        scratch_shapes=[
            pltpu.VMEM((rows, width), full),
            pltpu.VMEM((rows, width), full),
            pltpu.VMEM((pairs, count, 2 * DEC_LEN), full),
            pltpu.VMEM((1, width), full),
            pltpu.VMEM((width, LANES), full),
        ],
        compiler_params=params(56),
        cost_estimate=heavy,
    )(
        mark, query_cross_grad, weights_c, after, gain_two, resid, hidden, gain_one, gain_ffn_grad,
        query, key, value, weights_o, weights_q, weights_k, weights_v, buckets, table,
    )


class Places:
    def __init__(self, dp_size, seq_size):
        self.dp, self.seq = dp_size, seq_size
        self.core = 2 if dp_size % 2 == 0 else 1
        self.ny = dp_size // self.core
        self.nx = self.ny if seq_size % self.ny == 0 else 1
        self.nz = seq_size // self.nx
        self.low = 2 if self.nz % 2 == 0 else 1
        self.high = self.nz // self.low
        dp_index, seq_index = lax.axis_index("dp"), lax.axis_index("seq")
        self.c, self.y = dp_index % self.core, dp_index // self.core
        self.x, self.z = seq_index % self.nx, seq_index // self.nx
        self.place = jnp.stack([self.y, self.c, self.x, self.z // self.low, self.z % self.low]).astype(jnp.int32)

    def shift(self, value, **steps):
        sizes = {"y": self.ny, "c": self.core, "h": self.high, "l": self.low, "x": self.nx}
        flat = lambda p: ((p["y"] * self.core + p["c"]) * self.seq) + (p["h"] * self.low + p["l"]) * self.nx + p["x"]
        pairs = []
        for numbers in itertools.product(*[range(size) for size in sizes.values()]):
            here = dict(zip(sizes, numbers))
            there = {axis: (here[axis] + steps.get(axis, 0)) % size for axis, size in sizes.items()}
            pairs.append((flat(here), flat(there)))
        return lax.ppermute(value, ("dp", "seq"), pairs)


def gate_kernel(*refs):
    refs[-1][...] = jnp.zeros_like(refs[-1])


def gate(*waits):
    arrays = jax.tree.leaves(waits)
    return pl.pallas_call(
        gate_kernel,
        name="gate",
        in_specs=[pl.BlockSpec(memory_space=pl.ANY)] * len(arrays),
        out_shape=jax.ShapeDtypeStruct((8, LANES), full),
        cost_estimate=heavy,
    )(*arrays)


def marked(kernel, scalars=0):
    return lambda *refs: kernel(*refs[:scalars], *refs[scalars + 1 :])


class Term:
    def __init__(self, array, axes, fixed=(), columns=None):
        self.array, self.axes, self.fixed = array, axes, dict(fixed)
        self.columns = columns or (0, array.shape[-1])

    def at(self, axis, place):
        return Term(self.array, self.axes, {**self.fixed, axis: place}, self.columns)

    def free(self):
        sizes = zip(self.axes, self.array.shape)
        return tuple(size for axis, size in sizes if axis not in self.fixed)

    def spec(self):
        shape = [None if axis in self.fixed else size for axis, size in zip(self.axes, self.array.shape)]
        places = [self.fixed.get(axis, 0) for axis in self.axes]
        return pl.BlockSpec((*shape, *self.array.shape[-2:]), lambda i: (*places, 0, 0))


def totals_kernel(*refs, jobs):
    refs = list(refs)
    sources, outs = refs[: -len(jobs)], refs[-len(jobs) :]
    for groups, out in zip(jobs, outs):
        first = 0
        for columns in groups:
            total = None
            for low, high in columns:
                value = sources.pop(0)[..., low:high].astype(full)
                total = value if total is None else total + value
            out[..., first : first + total.shape[-1]] = total.astype(out.dtype)
            first += total.shape[-1]


def totals(mark, jobs, kind=half, cost=light):
    terms = [term for groups in jobs for group in groups for term in group]
    shape = lambda groups: (
        *groups[0][0].free(),
        groups[0][0].array.shape[-2],
        sum(group[0].columns[1] - group[0].columns[0] for group in groups),
    )
    return pl.pallas_call(
        marked(
            functools.partial(totals_kernel, jobs=[[[term.columns for term in group] for group in groups] for groups in jobs])
        ),
        name="totals",
        grid=(1,),
        in_specs=[anywhere] + [term.spec() for term in terms],
        out_specs=[whole(shape(groups)) for groups in jobs],
        out_shape=[jax.ShapeDtypeStruct(shape(groups), kind) for groups in jobs],
        compiler_params=params(56),
        cost_estimate=cost,
    )(mark, *[term.array for term in terms])


def final_kernel(place, *refs, terms, shapes, head_count):
    refs = list(refs)
    sources, outs = refs[: sum(len(columns) for columns in terms)], refs[sum(len(columns) for columns in terms) :]
    for columns, holds in zip(terms, shapes):
        total = None
        for low, high in columns:
            value = sources.pop(0)[..., low:high].astype(full)
            total = value if total is None else total + value
        first = 0
        for hold in holds:
            if hold == "plain":
                outs.pop(0)[...] = total
            elif hold == "pair":
                wide = outs[0].shape[1] * 2
                for out, value in zip(outs[:2], unpaired(total[:, first : first + wide], place[1])):
                    out[...] = value
                outs, first = outs[2:], first + wide
            elif hold == "rows":
                out, m = outs.pop(0), total.shape[0]
                wide = out.shape[1]
                for piece in range(0, out.shape[0] // m, 2):
                    two = unpaired(total[:, piece * wide : (piece + 2) * wide], place[1])
                    out[piece * m : (piece + 1) * m, :] = two[0]
                    out[(piece + 1) * m : (piece + 2) * m, :] = two[1]
            else:
                turned = total[:, first:].T
                for k in range(3):
                    outs.pop(0)[...] = turned[k : k + 1, :]
                bias = outs.pop(0)
                bias[...] = pltpu.roll(total[:, first:], LANES - 16, 1)[: bias.shape[0], :head_count]


def final(mark, at, sums, holds, shapes, head_count, cost=light):
    terms = [part.terms for part in sums]
    arrays = [term for group in terms for term in group]
    as_prefetch = lambda spec: pl.BlockSpec(spec.block_shape, lambda i, _, index=spec.index_map: index(i))
    return pl.pallas_call(
        marked(
            functools.partial(
                final_kernel,
                terms=[[term.columns for term in group] for group in terms],
                shapes=holds,
                head_count=head_count,
            ),
            1,
        ),
        name="final",
        grid_spec=pltpu.PrefetchScalarGridSpec(
            num_scalar_prefetch=1,
            grid=(1,),
            in_specs=[anywhere] + [as_prefetch(term.spec()) for term in arrays],
            out_specs=[whole(shape) for shape in shapes],
        ),
        out_shape=[jax.ShapeDtypeStruct(shape, full) for shape in shapes],
        compiler_params=params(56),
        cost_estimate=cost,
    )(at.place, mark, *[term.array for term in arrays])


class Reduction:
    def __init__(self, at, keep, send, order):
        self.at, self.order = at, order
        self.terms = [Term(keep, "yxhl")]
        if at.core == 2:
            self.terms.append(Term(at.shift(send, c=1), "yxhl"))
        self.left = "yxhl"


def advance(mark, *sums, together=False, cost=light):
    at = sums[0].at
    axes = [part.order[0] for part in sums]
    size = lambda axis: {"y": at.ny, "x": at.nx, "h": at.high, "l": at.low}[axis]
    group = lambda part, k: [term.at(part.order[0], k) for term in part.terms]
    if together:
        places = [(axes[0], k) for k in range(1, size(axes[0]))]
        jobs = [[group(part, k) for part in sums] for _, k in places]
    else:
        places = [(axis, k) for axis in axes for k in range(1, size(axis))]
        jobs = [[group(part, k)] for part, axis in zip(sums, axes) for k in range(1, size(axis))]
    pieces = list(totals(mark, jobs, cost=cost)) if jobs else []
    got = [at.shift(piece, **{axis: k}) for piece, (axis, k) in zip(pieces, places)]
    first = 0
    for part in sums:
        axis, part.order = part.order[0], part.order[1:]
        part.left = part.left.replace(axis, "")
        part.terms = [term.at(axis, 0) for term in part.terms]
        wide = part.terms[0].columns[1] - part.terms[0].columns[0]
        for _ in range(1, size(axis)):
            if together:
                continue
            part.terms.append(Term(got.pop(0), part.left))
        if together:
            part.terms += [Term(piece, part.left, (), (first, first + wide)) for piece in got]
            first += wide
    return pieces


def shards(
    decoder_in,
    encoder_states,
    encoder_doc,
    decoder_doc,
    cotangent,
    gain_self,
    gain_cross,
    gain_ffn,
    self_query,
    self_key,
    self_value,
    self_out,
    bias_table,
    cross_query,
    cross_key,
    cross_value,
    cross_out,
    ff_in,
    ff_out,
    *,
    dp_size,
    seq_size,
):
    at = Places(dp_size, seq_size)
    width = decoder_in.shape[2]
    head_count = bias_table.shape[1]
    bucket_count = bias_table.shape[0]
    score_scale = (width // head_count) ** (-0.5)
    local_rows = decoder_in.shape[1]
    doc_count = local_rows // DEC_LEN
    position = lax.axis_index("seq")
    own_map = lax.dynamic_slice_in_dim(decoder_doc[0], position * doc_count, doc_count, 0)
    gain_self, gain_cross, gain_ffn = (gain[None, :] for gain in (gain_self, gain_cross, gain_ffn))

    enc_rows = encoder_states.shape[1]
    docs = jnp.pad(encoder_doc.astype(half), ((0, 15), (0, width - enc_rows)))
    shard = jnp.concatenate([encoder_states[0], docs], axis=0)
    near = [at.shift(shard, l=l) for l in range(1, at.low)]
    over = [at.shift(shard, x=x) for x in range(1, at.nx)]
    far = [at.shift(shard, h=h) for h in range(1, at.high)]
    mark = gate(shard)
    own = jnp.pad(own_map.astype(full), (0, LANES - doc_count))[:, None]
    lane = jnp.arange(LANES, dtype=jnp.int32)
    mark = (jnp.arange(local_rows, dtype=jnp.int32)[:, None] // DEC_LEN == lane).astype(half)
    buckets = jnp.asarray(bucket_map(DEC_LEN, bucket_count, MAX_REACH))

    query_self, key_self, value_self, out_self, after_self, normed_two, query_cross, normed_one = self_forward(
        mark, decoder_in[0], gain_self, gain_cross, self_query, self_key, self_value, self_out, cross_query,
        buckets, bias_table, score_scale,
    )
    near, over, far, query_cross = lax.optimization_barrier((near, over, far, query_cross))
    ahead = [at.shift(rows, l=l) for rows in far for l in range(1, at.low)]
    far_over = [[at.shift(rows, x=x) for rows in far] for x in range(1, at.nx)]
    near_over = [[at.shift(rows, x=x) for rows in near] for x in range(1, at.nx)]
    make = functools.partial(
        key_value, own=own, weights_k=cross_key, weights_v=cross_value, rows=enc_rows, doc_count=doc_count
    )
    column = [shard, *near]
    if at.high == 2 and at.low == 2:
        made = make(column, place=0, places=2)
        ahead, far_over, made = lax.optimization_barrier((ahead, far_over, made))
        column += [far[0], *ahead]
        made = make(column[2:], begun=made, place=1, places=2)
    else:
        step = at.low - 1
        for h, rows in enumerate(far):
            column += [rows, *ahead[h * step : (h + 1) * step]]
        made = make(column)
    sources, states, state = [], [], []
    for x in range(at.nx):
        if x:
            part = [over[x - 1], *near_over[x - 1]]
            for rows in far_over[x - 1]:
                part += [rows, *[at.shift(rows, l=l) for l in range(1, at.low)]]
            made = make(part)
        *source, rows = made
        sources.append(source)
        states.append(rows)
        state = cross_forward(query_cross, mark, source, state, x == at.nx - 1, score_scale)
    mixed_cross, out_cross, extended = state
    (
        after_cross, activated, resid_grad, branch_cross, mixed_grad, gain_ffn_grad,
        in_keep, in_send, out_keep, out_send,
    ) = feed_forward(at, after_self, out_cross, cross_out, gain_ffn, ff_in, ff_out, cotangent[0])
    ff_out_sum = Reduction(at, out_keep, out_send, "yxlh")
    ff_in_sum = Reduction(at, in_keep, in_send, "xylh")

    pairs = width // LANES
    cut = 1
    mark = in_send
    begun = cross_backward(mark, extended, mixed_grad, mixed_cross, sources, 0, cut, [], score_scale)
    mark = advance(begun[0], ff_out_sum, ff_in_sum)[-1]
    query_grad, *grads = cross_backward(
        mark, extended, mixed_grad, mixed_cross, sources, cut, pairs - cut, begun, score_scale
    )
    mark = advance(query_grad, ff_out_sum, ff_in_sum)[-1]

    if len(states) * states[0].shape[0] <= FUSED_ROWS:
        shares, cross_keep, cross_send = cross_close(
            mark, at, normed_two, query_grad, out_cross, branch_cross, states, grads, cross_key, cross_value
        )
    else:
        shares = [encoder_part(mark, at, grads[2 * x : 2 * x + 2], cross_key, cross_value) for x in range(at.nx)]
        summed = lambda side: sum(dot(rows, grads[2 * x + side], TN) for x, rows in enumerate(states))
        cross_keep, cross_send = laid_out(
            at, [dot(normed_two, query_grad, TN), dot(out_cross, branch_cross, TN), summed(0), summed(1)]
        )
    early = [at.shift(part[0], x=-1 - k) for k, part in enumerate(shares[1:])]
    late = [at.shift(part[1], x=-1 - k) for k, part in enumerate(shares[1:])]
    cross_sum = Reduction(at, cross_keep, cross_send, "yxlh")
    mark = gate(advance(cross_keep, ff_out_sum, ff_in_sum, together=True))
    mark = advance(mark, cross_sum)[-1]

    input_grad, branch_self, *self_grads, extra = self_backward(
        mark, at.seq, query_grad, cross_query, after_self, gain_cross, resid_grad, decoder_in[0], gain_self,
        gain_ffn_grad, query_self, key_self, value_self, self_out, self_query, self_key, self_value,
        buckets, bias_table, score_scale,
    )
    (low_ready,) = totals(input_grad, [[[Term(part, "h") for part in (shares[0][0], *early)]]])
    high_terms = [Term(part, "h") for part in (shares[0][1], *late, at.shift(low_ready, l=-1))]
    ready = advance(low_ready, ff_out_sum, ff_in_sum, together=True)
    mark = gate(low_ready, late, ready, advance(ready[0], cross_sum))
    first_keep, first_send, second_keep, second_send = weight_grads(
        mark,
        at,
        [[(normed_one, grad)] for grad in self_grads] + [[(out_self, branch_self)]],
        [[0], [1]],
        extra,
    )
    first_sum = Reduction(at, first_keep, first_send, "yxlh")
    second_sum = Reduction(at, second_keep, second_send, SECOND)
    mark = second_send

    n, m = width // at.dp, width // at.seq
    cross_ready = advance(mark, cross_sum, cost=heavy)
    mark = gate(cross_ready, advance(cross_ready[0], first_sum, second_sum))
    ff_out_grad, ff_in_grad = final(
        mark, at, [ff_out_sum, ff_in_sum], [["rows"], ["plain"]],
        [(ff_out.shape[0] // at.seq, n), (m, ff_in.shape[1] // at.dp)], head_count,
    )
    high_ready = totals(ff_in_grad, [[[term.at("h", h) for term in high_terms]] for h in range(1, at.high)])
    last_terms = [term.at("h", 0) for term in high_terms] + [
        Term(at.shift(piece, h=-1 - k), "") for k, piece in enumerate(high_ready)
    ]
    cross_ready = advance(high_ready[0], cross_sum)
    mark = gate(cross_ready, advance(cross_ready[0], first_sum, second_sum))
    activated, mark = lax.optimization_barrier((activated, mark))
    output = (after_cross + dot(activated, ff_out, NN)).astype(half)
    mark = advance(mark, first_sum, second_sum, together=True)[-1]
    small = (m, n)
    cross_query_grad, cross_out_grad, cross_key_grad, cross_value_grad = final(
        mark, at, [cross_sum], [["pair", "pair"]], [small] * 4, head_count, heavy
    )
    ready = advance(cross_value_grad, first_sum, second_sum, together=True)
    (encoder_grad,) = totals(ready[-1], [[last_terms]], full, heavy)
    mark = encoder_grad
    query_grad, key_grad, value_grad, out_grad, *gains, bias_grad = final(
        mark, at, [first_sum, second_sum], [["pair"], ["pair", "extra"]],
        [small] * 4 + [(1, m)] * 3 + [(bucket_count // at.seq, head_count)], head_count,
    )
    return (
        output[None],
        input_grad[None],
        encoder_grad[None],
        *(gain.reshape(-1) for gain in gains),
        query_grad,
        key_grad,
        value_grad,
        out_grad,
        bias_grad,
        cross_query_grad,
        cross_key_grad,
        cross_value_grad,
        cross_out_grad,
        ff_in_grad,
        ff_out_grad,
    )


def solution(mesh):
    placed = (
        P("dp", "seq", None),
        P("dp", "seq", None),
        P("dp", "seq"),
        P("dp", None),
        P("dp", "seq", None),
    ) + (P(),) * 14
    return jax.shard_map(
        functools.partial(shards, dp_size=mesh.shape["dp"], seq_size=mesh.shape["seq"]),
        mesh=mesh,
        in_specs=placed,
        out_specs=(
            P("dp", "seq", None),
            P("dp", "seq", None),
            P("dp", "seq", None),
            P("seq"),
            P("seq"),
            P("seq"),
            P("seq", "dp"),
            P("seq", "dp"),
            P("seq", "dp"),
            P("seq", "dp"),
            P("seq", None),
            P("seq", "dp"),
            P("seq", "dp"),
            P("seq", "dp"),
            P("seq", "dp"),
            P("seq", "dp"),
            P("seq", "dp"),
        ),
        check_vma=False,
    )
```

```python
import functools
import itertools
import math

import jax
import jax.numpy as jnp
import numpy as np
from jax import lax
from jax.experimental import pallas as pl
from jax.experimental.pallas import tpu as pltpu
from jax.sharding import PartitionSpec as P

MAX_REACH = 128
DEC_LEN = 128


epsilon = 1e-06
masked_fill = -1e30
half = jnp.bfloat16
full = jnp.float32


def bucket_map(length, buckets, max_reach):
    exact_span = buckets // 2
    places = np.arange(length)
    distance = places[None, :] - places[:, None]
    passed = np.zeros_like(distance)
    for threshold_index in range(1, buckets - exact_span):
        threshold = int(
            math.ceil(
                exact_span * (max_reach / exact_span) ** (threshold_index / (buckets - exact_span))
            )
        )
        passed = passed + (distance >= threshold)
    bucket_of = np.where(distance < exact_span, distance, exact_span + passed)
    return np.where(distance < 0, -1, bucket_of).astype(np.int32)


def norm_parts(values):
    inverse = lax.rsqrt(jnp.mean(values * values, axis=-1, keepdims=True) + epsilon)
    return values * inverse, inverse


def norm_backward(upstream, normal, inverse, gain_row):
    scaled = upstream * gain_row
    inner = jnp.mean(scaled * normal, axis=-1, keepdims=True)
    return inverse * (scaled - normal * inner), jnp.sum(upstream * normal, axis=0, keepdims=True)


NT = (((1,), (1,)), ((), ()))
NN = (((1,), (0,)), ((), ()))
TN = (((0,), (0,)), ((), ()))
LANES = 128
ONES = 8
MEGA = 2**20
PAIRS = 2
FUSED_ROWS = 2048
SECOND = "xylh"


def dot(left_side, right_side, dims):
    return lax.dot_general(left_side, right_side, dims, preferred_element_type=full)


def three(value):
    first = value.astype(half).astype(full)
    second = (value - first).astype(half).astype(full)
    return first, second, (value - first - second).astype(half).astype(full)


def placed_three(value, index, rest):
    first, second, third = three(value)
    return jnp.where(
        index == ONES, first, jnp.where(index == ONES + 1, second, jnp.where(index == ONES + 2, third, rest))
    )


def low_lanes(rows):
    return lax.broadcasted_iota(jnp.int32, (rows, LANES), 1) < LANES // 2


def stacked(value, low):
    zero = jnp.zeros_like(value)
    return jnp.concatenate([jnp.where(low, value, zero), jnp.where(low, zero, value)], axis=0)


def loop(count, step, start):
    return lax.fori_loop(0, count, step, start, unroll=count <= 4)


light = pl.CostEstimate(flops=1, bytes_accessed=1, transcendentals=0)


def params(megabytes):
    return pltpu.CompilerParams(vmem_limit_bytes=megabytes * MEGA)


def whole(shape):
    return pl.BlockSpec(shape, lambda *_: (0,) * len(shape))


anywhere = pl.BlockSpec(memory_space=pl.ANY)


class Blocks:
    def __init__(self, at):
        self.core, self.ny, self.nx, self.dp, self.seq = at.core, at.ny, at.nx, at.dp, at.seq
        self.high, self.low = at.high, at.low

    def shape(self, rows, columns):
        return (self.ny, self.nx, self.high, self.low, rows, columns)

    def row_place(self, block, place):
        z = lax.div(block, self.nx)
        return (
            lax.rem(lax.rem(block, self.nx) - place[2] + self.nx, self.nx),
            lax.rem(lax.div(z, self.low) - place[3] + self.high, self.high),
            lax.rem(lax.rem(z, self.low) - place[4] + self.low, self.low),
        )

    def column_place(self, y, place):
        return lax.rem(y - place[0] + self.ny, self.ny)

    def paired(self, first, second, place):
        n = first.shape[1] // self.core
        if self.core == 1:
            return jnp.concatenate([first, second], axis=1).astype(half), None
        mine = place[1] == 0
        if n % LANES != LANES // 2:
            cut = [jnp.concatenate([g[:, c * n : (c + 1) * n] for g in (first, second)], axis=1) for c in range(2)]
        else:
            main = n - LANES // 2
            low = lax.broadcasted_iota(jnp.int32, (first.shape[0], LANES), 1) < LANES // 2
            one, two = (g[:, main : main + LANES] for g in (first, second))
            sides = (
                jnp.where(low, one, pltpu.roll(two, LANES // 2, 1)),
                jnp.where(low, pltpu.roll(one, LANES // 2, 1), two),
            )
            cut = [
                jnp.concatenate([first[:, at : at + main], second[:, at : at + main], sides[c]], axis=1)
                for c, at in enumerate((0, main + LANES))
            ]
        return jnp.where(mine, cut[0], cut[1]).astype(half), jnp.where(mine, cut[1], cut[0]).astype(half)


def unpaired(piece, core):
    n = piece.shape[1] // 2
    if n % LANES != LANES // 2:
        return piece[:, :n], piece[:, n:]
    main = n - LANES // 2
    side = piece[:, 2 * main :]
    turned = pltpu.roll(side, LANES // 2, 1)
    out = []
    for k in range(2):
        big = piece[:, k * main : (k + 1) * main]
        first, second = (side, turned) if k == 0 else (turned, side)
        after = jnp.concatenate([big, first], axis=1)
        ahead = pltpu.roll(jnp.concatenate([big, second], axis=1), LANES // 2, 1)
        out.append(jnp.where(core == 0, after, ahead)[:, :n])
    return out


def position_bias(buckets, table, pair):
    out = []
    for head in range(2):
        bias = jnp.full(buckets.shape, masked_fill, full)
        for b in range(table.shape[0]):
            bias = jnp.where(buckets == b, table[b, 2 * pair + head], bias)
        out.append(bias)
    return jnp.concatenate(out, axis=1)


def self_forward_kernel(
    hidden, gain_one, gain_two, weights_q, weights_k, weights_v, weights_o, weights_c, buckets, table,
    query, key, value, mixed, after, normed_two, query_cross, normed, every, *, scale,
):
    step = pl.program_id(0)
    rows = hidden.shape[0]

    @pl.when(step == 0)
    def _():
        normal, _ = norm_parts(hidden[...].astype(full))
        normed[...] = (normal * gain_one[...]).astype(half)

    many = query.shape[1] // LANES
    wide = many * LANES
    weights = jnp.concatenate([weights_q[...], weights_k[...], weights_v[...]], axis=1)
    made = dot(normed[...], weights, NN).astype(half)
    query[...] = made[:, :wide] * scale
    key[...] = made[:, wide : 2 * wide]
    value[...] = made[:, 2 * wide :]
    low = low_lanes(DEC_LEN)
    bias = [position_bias(buckets[...], table, step * many + pair) for pair in range(many)]
    work = [
        (pair, slice(pair * LANES, (pair + 1) * LANES), pl.ds(first, DEC_LEN))
        for pair in range(many)
        for first in range(0, rows, DEC_LEN)
    ]
    scores = [dot(key[at, own], stacked(query[at, own], low), NT) + bias[pair] for pair, own, at in work]
    expos = []
    for score in scores:
        expo = jnp.exp(score - jnp.max(score, axis=0, keepdims=True))
        expos.append((expo / jnp.sum(expo, axis=0, keepdims=True)).astype(half))
    for (pair, own, at), expo in zip(work, expos):
        both = dot(value[at, own], expo, TN).T
        one = jnp.where(low, both[:DEC_LEN], both[DEC_LEN:]).astype(half)
        mixed[at, own] = one
        every[at, pl.ds(pl.multiple_of(step * wide + pair * LANES, LANES), LANES)] = one

    @pl.when(step == pl.num_programs(0) - 1)
    def _():
        total = hidden[...].astype(full) + dot(every[...], weights_o[...], NN)
        after[...] = total
        normal, _ = norm_parts(total)
        again = (normal * gain_two[...]).astype(half)
        normed_two[...] = again
        query_cross[...] = dot(again, weights_c[...], NN).astype(half)


def self_forward(mark, hidden, gain_one, gain_two, weights_q, weights_k, weights_v, weights_o, weights_c, buckets, table, scale):
    rows, width = hidden.shape
    pairs = width // LANES
    many = PAIRS
    column = lambda i: (0, i)
    row_block = pl.BlockSpec((rows, many * LANES), column)
    weight_block = pl.BlockSpec((width, many * LANES), column)
    return pl.pallas_call(
        marked(functools.partial(self_forward_kernel, scale=scale)),
        name="self_forward",
        grid=(pairs // many,),
        in_specs=[anywhere, whole((rows, width)), whole((1, width)), whole((1, width))]
        + [weight_block] * 3
        + [whole((width, width))] * 2
        + [whole((DEC_LEN, DEC_LEN)), pl.BlockSpec(memory_space=pltpu.SMEM)],
        out_specs=[row_block] * 4 + [whole((rows, width))] * 4,
        out_shape=[jax.ShapeDtypeStruct((rows, width), half)] * 4
        + [jax.ShapeDtypeStruct((rows, width), kind) for kind in (full, half, half, half)],
        scratch_shapes=[pltpu.VMEM((rows, width), half)],
        compiler_params=params(56),
        cost_estimate=light,
    )(mark, hidden, gain_one, gain_two, weights_q, weights_k, weights_v, weights_o, weights_c, buckets, table)


def key_value_kernel(*refs, rows, doc_count):
    shards, (own, weights_k, weights_v, keys, values, mask, states) = refs[:-7], refs[-7:]
    for i, shard in enumerate(shards):
        at = pl.ds(i * rows, rows)
        states[at, :] = shard[:rows, :]
        keys[at, :] = dot(shard[:rows, :], weights_k[...], NN).astype(half)
        values[at, :] = dot(shard[:rows, :], weights_v[...], NN).astype(half)
        docs = shard[rows : rows + 1, :rows].astype(full)
        lane = lax.broadcasted_iota(jnp.int32, (LANES, rows), 0)
        ones = ((lane >= ONES) & (lane < ONES + 3)).astype(full)
        extra = jnp.where(lane < doc_count, jnp.where(docs == own[:, :1], 0.0, masked_fill), ones)
        mask[at, :] = extra.T.astype(half)


def key_value(shards, own, weights_k, weights_v, rows, doc_count, begun=(), place=0, places=1):
    width = shards[0].shape[1]
    count = len(shards) * rows
    sizes = (width, width, LANES, width)
    kernel = functools.partial(key_value_kernel, rows=rows, doc_count=doc_count)
    return pl.pallas_call(
        lambda *refs: kernel(*refs[len(begun) :]),
        name="key_value",
        grid=(1,),
        in_specs=[anywhere] * len(begun) + [whole(array.shape) for array in (*shards, own, weights_k, weights_v)],
        out_specs=[pl.BlockSpec((count, size), lambda i: (place, 0)) for size in sizes],
        out_shape=[jax.ShapeDtypeStruct((places * count, size), half) for size in sizes],
        input_output_aliases={i: i for i in range(len(begun))},
        compiler_params=params(56),
        cost_estimate=light,
    )(*begun, *shards, own, weights_k, weights_v)


def cross_forward_kernel(*refs, scale, block, opens, closes):
    query, mark, keys, values, mask = refs[:5]
    refs = refs[5:]
    if not opens:
        state_in, refs = refs[:2], refs[2:]
    if closes:
        (mixed, mixed_half, extended), refs = refs[:3], refs[3:]
    else:
        state_out, refs = refs[:2], refs[2:]
    total, wide = refs
    rows, many = query.shape[0], query.shape[1] // LANES
    low = low_lanes(rows)
    for pair in range(many):
        wide[pair, :, :LANES] = stacked(query[:, pair * LANES : (pair + 1) * LANES] * scale, low)
        wide[pair, :rows, LANES:] = mark[...]
        wide[pair, rows:, LANES:] = mark[...]
    if opens:
        total[...] = jnp.zeros_like(total)
        carry = [(jnp.full((1, 2 * rows), masked_fill, full), jnp.zeros((1, 2 * rows), full)) for _ in range(many)]
    else:
        total[...] = state_in[0][...]
        carry = [(state_in[1][pair, 0:1], state_in[1][pair, 1:2]) for pair in range(many)]

    def step(i, carry):
        at = pl.ds(pl.multiple_of(i * block, block), block)
        scores = [
            dot(jnp.concatenate([keys[at, pair * LANES : (pair + 1) * LANES], mask[at, :]], axis=1), wide[pair], NT)
            for pair in range(many)
        ]
        out = []
        for pair, (peak, amount) in enumerate(carry):
            fresh = jnp.maximum(peak, jnp.max(scores[pair], axis=0, keepdims=True))
            expo = jnp.exp(scores[pair] - fresh)
            fade = jnp.exp(peak - fresh)
            values_here = values[at, pair * LANES : (pair + 1) * LANES]
            total[pair] = total[pair] * fade + dot(values_here, expo.astype(half), TN)
            out.append((fresh, amount * fade + jnp.sum(expo, axis=0, keepdims=True)))
        return out

    carry = loop(keys.shape[0] // block, step, carry)
    if not closes:
        state_out[0][...] = total[...]
        for pair, (peak, amount) in enumerate(carry):
            state_out[1][pair, 0:1] = peak
            state_out[1][pair, 1:2] = amount
        return
    index = lax.broadcasted_iota(jnp.int32, (LANES, 2 * rows), 0)
    for pair, (peak, amount) in enumerate(carry):
        at = slice(pair * LANES, (pair + 1) * LANES)
        both = (total[pair] / amount).T
        one = jnp.where(low, both[:rows], both[rows:])
        mixed[:, at] = one
        mixed_half[:, at] = one.astype(half)
        extra = placed_three(-(peak + jnp.log(amount)), index, 0.0).T
        extended[pair, :, :LANES] = wide[pair, :, :LANES]
        extended[pair, :, LANES:] = (wide[pair, :, LANES:].astype(full) + extra).astype(half)


def cross_forward(query, mark, source, state, closes, scale):
    rows, pairs, many = query.shape[0], query.shape[1] // LANES, PAIRS
    count = source[0].shape[0]
    column = lambda i: (0, i)
    plane = lambda i: (i, 0, 0)
    block = min(1024, count)
    state_specs = [pl.BlockSpec((many, LANES, 2 * rows), plane), pl.BlockSpec((many, 2, 2 * rows), plane)]
    state_shape = [
        jax.ShapeDtypeStruct((pairs, LANES, 2 * rows), full),
        jax.ShapeDtypeStruct((pairs, 2, 2 * rows), full),
    ]
    last_specs = [pl.BlockSpec((rows, many * LANES), column)] * 2 + [pl.BlockSpec((many, 2 * rows, 2 * LANES), plane)]
    last_shape = [
        jax.ShapeDtypeStruct(query.shape, full),
        jax.ShapeDtypeStruct(query.shape, half),
        jax.ShapeDtypeStruct((pairs, 2 * rows, 2 * LANES), half),
    ]
    return pl.pallas_call(
        functools.partial(cross_forward_kernel, scale=scale, block=block, opens=not state, closes=closes),
        name="cross_forward",
        grid=(pairs // many,),
        in_specs=[pl.BlockSpec((rows, many * LANES), column), whole((rows, LANES))]
        + [pl.BlockSpec((count, many * LANES), column), pl.BlockSpec((count, many * LANES), column), whole((count, LANES))]
        + (state_specs if state else []),
        out_specs=last_specs if closes else state_specs,
        out_shape=last_shape if closes else state_shape,
        scratch_shapes=[
            pltpu.VMEM((many, LANES, 2 * rows), full),
            pltpu.VMEM((many, 2 * rows, 2 * LANES), half),
        ],
        compiler_params=params(56),
        cost_estimate=light,
    )(query, mark, *source, *state)


def cross_backward_kernel(*refs, scale, block, parts):
    extended, upstream, mixed = refs[:3]
    sources = [refs[3 + 3 * i : 6 + 3 * i] for i in range(parts)]
    query_grad = refs[3 + 3 * parts]
    grads = [refs[4 + 3 * parts + 2 * i : 6 + 3 * parts + 2 * i] for i in range(parts)]
    wide, total = refs[-2:]
    rows = upstream.shape[0]
    low = low_lanes(rows)
    lane = lax.broadcasted_iota(jnp.int32, (rows, LANES), 1)
    each = upstream[...].astype(full) * mixed[...]
    wide[:, :LANES] = stacked(upstream[...], low)
    for head in range(2):
        inner = jnp.sum(jnp.where(low == (head == 0), each, 0.0), axis=1, keepdims=True)
        wide[head * rows : (head + 1) * rows, LANES:] = placed_three(-inner, lane, 0.0).astype(half)
    total[...] = jnp.zeros_like(total)
    for (keys, values, mask), (key_grad, value_grad) in zip(sources, grads):

        def step(i, carry):
            at = pl.ds(pl.multiple_of(i * block, block), block)
            extra = mask[at, :]
            expo = jnp.exp(dot(jnp.concatenate([keys[at, :], extra], axis=1), extended[0], NT))
            change = dot(jnp.concatenate([values[at, :], extra], axis=1), wide[...], NT)
            score = (expo * change).astype(half)
            value_grad[at, :] = dot(expo.astype(half), wide[:, :LANES], NN).astype(half)
            key_grad[at, :] = dot(score, extended[0, :, :LANES], NN).astype(half)
            total[...] += dot(keys[at, :], score, TN)
            return carry

        loop(keys.shape[0] // block, step, 0)
    both = total[...].T
    query_grad[...] = (jnp.where(low, both[:rows], both[rows:]) * scale).astype(half)


def cross_backward(mark, extended, upstream, mixed, sources, first, pairs, begun, scale):
    rows, width = upstream.shape
    count = sources[0][0].shape[0]
    every = count * len(sources)
    column = lambda i: (0, i + first)
    block = min(1024, count)
    row_block, key_block = pl.BlockSpec((rows, LANES), column), pl.BlockSpec((count, LANES), column)
    operands = [extended, upstream, mixed, *[array for source in sources for array in source]]
    kernel = functools.partial(cross_backward_kernel, scale=scale, block=block, parts=len(sources))
    return pl.pallas_call(
        marked(lambda *refs: kernel(*refs[len(begun) :]), len(begun)),
        name="cross_backward",
        grid=(pairs,),
        in_specs=[anywhere] * (len(begun) + 1)
        + [pl.BlockSpec((1, 2 * rows, 2 * LANES), lambda i: (i + first, 0, 0)), row_block, row_block]
        + [key_block, key_block, whole((count, LANES))] * len(sources),
        out_specs=[row_block] + [key_block] * (2 * len(sources)),
        out_shape=[jax.ShapeDtypeStruct((rows, width), half)]
        + [jax.ShapeDtypeStruct((count, width), half)] * (2 * len(sources)),
        scratch_shapes=[
            pltpu.VMEM((2 * rows, 2 * LANES), half),
            pltpu.VMEM((LANES, 2 * rows), full),
        ],
        input_output_aliases={i: i for i in range(len(begun))},
        compiler_params=params(56),
        cost_estimate=light,
    )(*begun, mark, *operands)


def feed_forward_kernel(
    place, after, mixed, weights_o, gain, weights_in, weights_out, cotangent,
    after_cross, activated, resid, branch, mixed_grad, gain_grad, in_keep, in_send, out_keep, out_send,
    normed, total, *, blocks,
):
    step = pl.program_id(0)

    @pl.when(step == 0)
    def _():
        values = after[...] + dot(mixed[...], weights_o[...], NN)
        after_cross[...] = values
        normal, _ = norm_parts(values)
        normed[...] = (normal * gain[...]).astype(half)
        total[...] = jnp.zeros_like(total)

    upstream = cotangent[...]
    pre = dot(normed[...], weights_in[...], NN)
    square = pre * pre
    slope = math.sqrt(2.0 / math.pi)
    bend = jnp.tanh(slope * (pre + 0.044715 * (square * pre)))
    act = (0.5 * pre * (1.0 + bend)).astype(half)
    activated[...] = act
    gelu_grad = 0.5 * (1.0 + bend) + 0.5 * pre * (1.0 - bend * bend) * (slope * (1.0 + 3 * 0.044715 * square))
    pre_grad = (dot(upstream, weights_out[...], NT) * gelu_grad).astype(half)
    total[...] += dot(pre_grad, weights_in[...], NT)

    grad = dot(normed[...], pre_grad, TN).astype(half)
    m = grad.shape[0] // blocks.seq
    to_y = blocks.column_place(lax.div(step, blocks.core), place)
    ours = lax.rem(step, blocks.core) == place[1]

    def fill(target):
        for block in range(blocks.seq):
            to_x, to_h, to_l = blocks.row_place(jnp.int32(block), place)
            target[to_y, to_x, to_h, to_l] = grad[block * m : (block + 1) * m]

    pl.when(ours)(lambda: fill(in_keep))
    pl.when(jnp.logical_not(ours))(lambda: fill(in_send))

    grad = dot(act, upstream, TN)
    wide = grad.shape[1] // blocks.ny
    n = wide // blocks.core
    pieces = out_keep.shape[5] // n
    many = pieces * m
    for y in range(blocks.ny):
        at = slice(y * wide, (y + 1) * wide)
        to_y = blocks.column_place(jnp.int32(y), place)
        for block in range(grad.shape[0] // many):
            to_x, to_h, to_l = blocks.row_place(step * (grad.shape[0] // many) + block, place)
            for piece in range(0, pieces, 2):
                first = block * many + piece * m
                kept, sent = blocks.paired(grad[first : first + m, at], grad[first + m : first + 2 * m, at], place)
                out_keep[to_y, to_x, to_h, to_l, :, piece * n : (piece + 2) * n] = kept
                if sent is not None:
                    out_send[to_y, to_x, to_h, to_l, :, piece * n : (piece + 2) * n] = sent

    @pl.when(step == pl.num_programs(0) - 1)
    def _():
        normal, inverse = norm_parts(after_cross[...])
        change, gain_sum = norm_backward(total[...], normal, inverse, gain[...])
        gain_grad[...] = gain_sum
        change = change + upstream.astype(full)
        resid[...] = change
        rounded = change.astype(half)
        branch[...] = rounded
        mixed_grad[...] = dot(rounded, weights_o[...], NT).astype(half)


def feed_forward(at, after, mixed, weights_o, gain, weights_in, weights_out, cotangent):
    rows, width = after.shape
    depth = weights_in.shape[1]
    blocks = Blocks(at)
    cut = depth // at.dp
    shape = blocks.shape(width // at.seq, cut)
    all_rows = whole((rows, width))
    sized = lambda kind: jax.ShapeDtypeStruct((rows, width), kind)
    return pl.pallas_call(
        functools.partial(feed_forward_kernel, blocks=blocks),
        name="feed_forward",
        grid_spec=pltpu.PrefetchScalarGridSpec(
            num_scalar_prefetch=1,
            grid=(at.dp,),
            in_specs=[
                all_rows,
                all_rows,
                whole((width, width)),
                whole((1, width)),
                pl.BlockSpec((width, cut), lambda i, _: (0, i)),
                pl.BlockSpec((cut, width), lambda i, _: (i, 0)),
                all_rows,
            ],
            out_specs=[all_rows, pl.BlockSpec((rows, cut), lambda i, _: (0, i))]
            + [all_rows] * 3
            + [whole((1, width))]
            + [whole(shape)] * 4,
            scratch_shapes=[pltpu.VMEM((rows, width), half), pltpu.VMEM((rows, width), full)],
        ),
        out_shape=[sized(full), jax.ShapeDtypeStruct((rows, depth), half), sized(full), sized(half), sized(half)]
        + [jax.ShapeDtypeStruct((1, width), full)]
        + [jax.ShapeDtypeStruct(shape, half)] * 4,
        compiler_params=params(56),
        cost_estimate=light,
    )(at.place, after, mixed, weights_o, gain, weights_in, weights_out, cotangent)


def encoder_part_kernel(key_grad, value_grad, weights_k, weights_v, early, late, *, early_steps):
    total = dot(key_grad[...], weights_k[...], NT) + dot(value_grad[...], weights_v[...], NT)
    is_early = pl.program_id(0) < early_steps

    @pl.when(is_early)
    def _():
        early[...] = total.astype(half)

    @pl.when(jnp.logical_not(is_early))
    def _():
        late[...] = total.astype(half)


def encoder_part(mark, at, grads, weights_k, weights_v):
    width = weights_k.shape[0]
    rows = grads[0].shape[0] // at.nz
    early = at.high * (at.low - 1)
    plane = lambda size: jax.ShapeDtypeStruct((size, rows, width), half)
    block = pl.BlockSpec((rows, width), lambda i: (i % at.high * at.low + at.low - 1 - i // at.high, 0))
    return pl.pallas_call(
        marked(functools.partial(encoder_part_kernel, early_steps=early)),
        name="encoder_part",
        grid=(at.nz,),
        in_specs=[anywhere, block, block, whole((width, width)), whole((width, width))],
        out_specs=[
            pl.BlockSpec((None, rows, width), lambda i: (jnp.minimum(i, early - 1), 0, 0)),
            pl.BlockSpec((None, rows, width), lambda i: (jnp.maximum(i - early, 0), 0, 0)),
        ],
        out_shape=[plane(early), plane(at.high)],
        compiler_params=params(56),
        cost_estimate=light,
    )(mark, *grads, weights_k, weights_v)


def weight_grads_kernel(place, *refs, blocks, counts, chunks, extra, wide):
    refs = list(refs)
    sides = [[(refs.pop(0), refs.pop(0)) for _ in range(count)] for count in counts]
    small = refs.pop(0) if extra else None
    made = [sum((dot(left[...], right[...], TN) for left, right in side[1:]), dot(side[0][0][...], side[0][1][...], TN)) for side in sides]
    m = made[0].shape[0] // blocks.seq
    many = made[0].shape[1] // wide
    for chunk, pairs in enumerate(chunks):
        keep, send = refs[2 * chunk], refs[2 * chunk + 1]
        for y in range(many):
            at = slice(y * wide, (y + 1) * wide)
            columns = [blocks.paired(made[2 * pair][:, at], made[2 * pair + 1][:, at], place) for pair in pairs]
            if extra and chunk == len(chunks) - 1:
                columns.append((small[...], small[...]))
            to_y = blocks.column_place(jnp.int32(y), place) if many > 1 else 0
            for block in range(blocks.seq):
                to_x, to_h, to_l = blocks.row_place(jnp.int32(block), place)
                rows = slice(block * m, (block + 1) * m)
                first = 0
                for ours, theirs in columns:
                    to = slice(first, first + ours.shape[1])
                    keep[to_y, to_x, to_h, to_l, :, to] = ours[rows]
                    send[to_y, to_x, to_h, to_l, :, to] = theirs[rows]
                    first += ours.shape[1]


def weight_grads(mark, at, sides, chunks, extra=None):
    blocks = Blocks(at)
    width = sides[0][0][0].shape[1]
    wide, m = width // at.ny, width // at.seq
    shapes = [blocks.shape(m, len(pairs) * 2 * wide // at.core) for pairs in chunks]
    if extra is not None:
        shapes[-1] = (*shapes[-1][:-1], shapes[-1][-1] + extra.shape[1])
    terms = [term for side in sides for term in side]
    steps = at.ny if wide % LANES == 0 else 1
    from_y = lambda i, place: (0, lax.rem(i + place[0], at.ny) if steps > 1 else 0)
    out_block = lambda shape: pl.BlockSpec((shape[0] // steps, *shape[1:]), lambda i, place: (i, 0, 0, 0, 0, 0))
    return pl.pallas_call(
        marked(
            functools.partial(
                weight_grads_kernel,
                blocks=blocks,
                counts=[len(side) for side in sides],
                chunks=chunks,
                extra=extra is not None,
                wide=wide,
            ),
            1,
        ),
        name="weight_grads",
        grid_spec=pltpu.PrefetchScalarGridSpec(
            num_scalar_prefetch=1,
            grid=(steps,),
            in_specs=[anywhere]
            + [
                spec
                for left, right in terms
                for spec in (whole(left.shape), pl.BlockSpec((right.shape[0], width // steps), from_y))
            ]
            + ([whole(extra.shape)] if extra is not None else []),
            out_specs=[out_block(shape) for shape in shapes for _ in range(2)],
        ),
        out_shape=[jax.ShapeDtypeStruct(shape, half) for shape in shapes for _ in range(2)],
        compiler_params=params(60),
        cost_estimate=light,
    )(at.place, mark, *[array for term in terms for array in term], *([extra] if extra is not None else []))


def laid_out(at, grads):
    out = []
    for grad in grads:
        m, n = grad.shape[0] // at.seq, grad.shape[1] // at.dp
        assert n % LANES != LANES // 2
        blocks = grad.astype(half).reshape(at.high, at.low, at.nx, m, at.ny, at.core, n)
        places = ((0, at.z // at.low, at.high), (1, at.z % at.low, at.low), (2, at.x, at.nx), (4, at.y, at.ny), (5, at.c, at.core))
        for axis, own, size in places:
            blocks = jnp.take(blocks, (own + jnp.arange(size)) % size, axis=axis)
        out.append(blocks.transpose(5, 4, 2, 0, 1, 3, 6))
    both = jnp.concatenate(out, axis=-1)
    return both[0], both[1]


def cross_close_kernel(place, *refs, blocks, parts):
    count = 3 * parts + 6
    arrays, refs = refs[:count], refs[count:]
    shares, (keep, send), refs = refs[: 2 * parts], refs[2 * parts : 2 * parts + 2], refs[2 * parts + 2 :]
    held, refs = refs[:count], refs[count:]
    made, (keep_held, send_held, arrived, gone) = refs[:parts], refs[parts:]
    ins = [pltpu.make_async_copy(array, place_held, arrived.at[i]) for i, (array, place_held) in enumerate(zip(arrays, held))]
    grads, (weights_k, weights_v), states = held[: 2 * parts], held[2 * parts : 2 * parts + 2], held[2 * parts + 2 : -4]
    normed, query_grad, mixed, branch = held[-4:]
    outs = []

    def leave(source, target):
        copy = pltpu.make_async_copy(source, target, gone.at[len(outs)])
        copy.start()
        outs.append(copy)

    order = [*range(1, parts), 0]
    first = [i for x in order[:1] for i in (2 * x, 2 * x + 1)] + [2 * parts, 2 * parts + 1]
    for i in first + [i for i in range(count) if i not in first]:
        ins[i].start()
    ins[2 * parts].wait()
    ins[2 * parts + 1].wait()
    rows = grads[0].shape[0] // (blocks.high * blocks.low)
    early_size = blocks.low - 1
    for x in order:
        ins[2 * x].wait()
        ins[2 * x + 1].wait()
        for block in range(blocks.high * blocks.low):
            at = slice(block * rows, (block + 1) * rows)
            total = dot(grads[2 * x][at, :], weights_k[...], NT) + dot(grads[2 * x + 1][at, :], weights_v[...], NT)
            made[x][at, :] = total.astype(half)
        for block in range(blocks.high * blocks.low):
            h, l = divmod(block, blocks.low)
            source = made[x].at[pl.ds(block * rows, rows), :]
            leave(source, shares[2 * x].at[(blocks.low - 1 - l) * blocks.high + h] if l else shares[2 * x + 1].at[h])

    def place_pair(one, two, offset):
        m, wide = one.shape[0] // blocks.seq, one.shape[1] // blocks.ny
        for y in range(blocks.ny):
            at = slice(y * wide, (y + 1) * wide)
            ours, theirs = blocks.paired(one[:, at], two[:, at], place)
            to_y = blocks.column_place(jnp.int32(y), place)
            to = slice(offset, offset + ours.shape[1])
            for block in range(blocks.seq):
                to_x, to_h, to_l = blocks.row_place(jnp.int32(block), place)
                own = slice(block * m, (block + 1) * m)
                keep_held[to_y, to_x, to_h, to_l, :, to] = ours[own]
                send_held[to_y, to_x, to_h, to_l, :, to] = theirs[own]
        for source, target in ((send_held, send), (keep_held, keep)):
            leave(source.at[:, :, :, :, :, to], target.at[:, :, :, :, :, to])

    n = keep_held.shape[5] // 4
    for copy in ins[2 * parts + 2 : -4]:
        copy.wait()
    total = []
    for kind in range(2):
        terms = [dot(states[x][...], grads[2 * x + kind][...], TN) for x in range(parts)]
        total.append(sum(terms[1:], terms[0]))
    place_pair(total[0], total[1], 2 * n)
    for copy in ins[-4:]:
        copy.wait()
    place_pair(dot(normed[...], query_grad[...], TN), dot(mixed[...], branch[...], TN), 0)
    for copy in outs:
        copy.wait()


def cross_close(mark, at, normed, query_grad, mixed, branch, states, grads, weights_k, weights_v):
    blocks, parts = Blocks(at), len(states)
    count, width = states[0].shape
    shape = blocks.shape(width // at.seq, 4 * width // at.dp)
    arrays = [*grads, weights_k, weights_v, *states, normed, query_grad, mixed, branch]
    plane = lambda size: jax.ShapeDtypeStruct((size, count // at.nz, width), half)
    outs = [plane(at.high * (at.low - 1)), plane(at.high)] * parts + [jax.ShapeDtypeStruct(shape, half)] * 2
    made = pl.pallas_call(
        marked(functools.partial(cross_close_kernel, blocks=blocks, parts=parts), 1),
        name="cross_close",
        in_specs=[pl.BlockSpec(memory_space=pltpu.SMEM)] + [anywhere] * (len(arrays) + 1),
        out_specs=[anywhere] * len(outs),
        out_shape=outs,
        scratch_shapes=[pltpu.VMEM(array.shape, half) for array in arrays]
        + [pltpu.VMEM((count, width), half)] * parts
        + [pltpu.VMEM(shape, half)] * 2
        + [pltpu.SemaphoreType.DMA((len(arrays),)), pltpu.SemaphoreType.DMA((parts * at.nz + 4,))],
        compiler_params=params(56),
        cost_estimate=light,
    )(at.place, mark, *arrays)
    return [made[2 * x : 2 * x + 2] for x in range(parts)], *made[-2:]


def self_backward_kernel(
    query_cross_grad, weights_c, after, gain_two, resid_in, hidden, gain_one, gain_ffn_grad,
    query, key, value, weights_ob, weights_q, weights_k, weights_v, buckets, table,
    input_grad, branch, query_grad, key_grad, value_grad, extra,
    resid, total, bias_rows, gain_two_grad, columns, *, scale, shares,
):
    step = pl.program_id(0)
    rows, width = hidden.shape

    @pl.when(step == 0)
    def _():
        normal, inverse = norm_parts(after[...])
        up = dot(query_cross_grad[...], weights_c[...], NT)
        change, gain_sum = norm_backward(up, normal, inverse, gain_two[...])
        gain_two_grad[...] = gain_sum
        change = change + resid_in[...]
        resid[...] = change
        branch[...] = change.astype(half)
        total[...] = jnp.zeros_like(total)

    low = low_lanes(DEC_LEN)
    many = query.shape[1] // LANES
    upstream = dot(branch[...], weights_ob[...], NT).astype(half)
    count = bias_rows.shape[1]
    of_pair = jnp.concatenate([buckets[...], buckets[...]], axis=1)
    work = [(pair, pl.ds(first, DEC_LEN)) for pair in range(many) for first in range(0, rows, DEC_LEN)]
    spans = [slice(pair * LANES, (pair + 1) * LANES) for pair in range(many)]
    bias = [position_bias(buckets[...], table, step * many + pair) for pair in range(many)]
    wides = [stacked(query[at, spans[pair]], low) for pair, at in work]
    up = [stacked(upstream[at.start : at.start + DEC_LEN, spans[pair]], low) for pair, at in work]
    scores = [dot(key[at, spans[pair]], wide, NT) + bias[pair] for (pair, at), wide in zip(work, wides)]
    changes = [dot(value[at, spans[pair]], grad, NT) for (pair, at), grad in zip(work, up)]
    summed = [None] * many
    for (pair, at), wide, grad, score, change in zip(work, wides, up, scores, changes):
        own = spans[pair]
        expo = jnp.exp(score - jnp.max(score, axis=0, keepdims=True))
        expo = expo / jnp.sum(expo, axis=0, keepdims=True)
        rounded = (expo * (change - jnp.sum(expo * change, axis=0, keepdims=True))).astype(half)
        both = dot(key[at, own], rounded, TN).T
        query_grad[at, own] = (jnp.where(low, both[:DEC_LEN], both[DEC_LEN:]) * scale).astype(half)
        key_grad[at, own] = dot(rounded, wide, NN).astype(half)
        value_grad[at, own] = dot(expo.astype(half), grad, NN).astype(half)
        summed[pair] = rounded.astype(full) if summed[pair] is None else summed[pair] + rounded.astype(full)
    made = jnp.concatenate([query_grad[...], key_grad[...], value_grad[...]], axis=1)
    total[...] += dot(made, jnp.concatenate([weights_q[...], weights_k[...], weights_v[...]], axis=1), NT)
    for pair in range(many):
        sums = [jnp.sum(jnp.where(of_pair == b, summed[pair], 0.0), axis=0, keepdims=True) for b in range(count)]
        bias_rows[step * many + pair] = jnp.concatenate(sums, axis=0)

    @pl.when(step == pl.num_programs(0) - 1)
    def _():
        normal, inverse = norm_parts(hidden[...].astype(full))
        change, gain_sum = norm_backward(total[...], normal, inverse, gain_one[...])
        input_grad[...] = resid[...] + change

        index = lax.broadcasted_iota(jnp.int32, (LANES, width), 0)
        gains = jnp.where(
            index == 0,
            gain_sum,
            jnp.where(index == 1, gain_two_grad[...], jnp.where(index == 2, gain_ffn_grad[...], 0.0)),
        )
        columns[...] = gains.T
        lane = lax.broadcasted_iota(jnp.int32, (count, LANES), 1)
        sums = jnp.zeros((count, LANES), full)
        for pair in range(bias_rows.shape[0]):
            for head in range(2):
                part = bias_rows[pair, :, head * LANES : (head + 1) * LANES]
                sums = jnp.where(lane == 16 + 2 * pair + head, jnp.sum(part, axis=1, keepdims=True), sums)
        m, each = width // shares, count // shares
        for block in range(shares):
            at = slice(block * m, block * m + each)
            columns[at, :] = columns[at, :] + sums[block * each : (block + 1) * each]
        extra[...] = columns[...].astype(half)


def self_backward(
    mark, shares, query_cross_grad, weights_c, after, gain_two, resid, hidden, gain_one, gain_ffn_grad,
    query, key, value, weights_o, weights_q, weights_k, weights_v, buckets, table, scale,
):
    rows, width = hidden.shape
    pairs, count = width // LANES, table.shape[0]
    many = PAIRS
    row_block = pl.BlockSpec((rows, many * LANES), lambda i: (0, i))
    weight_block = pl.BlockSpec((width, many * LANES), lambda i: (0, i))
    all_rows, line = whole((rows, width)), whole((1, width))
    sized = lambda kind: jax.ShapeDtypeStruct((rows, width), kind)
    return pl.pallas_call(
        marked(functools.partial(self_backward_kernel, scale=scale, shares=shares)),
        name="self_backward",
        grid=(pairs // many,),
        in_specs=[anywhere, all_rows, whole((width, width)), all_rows, line, all_rows, all_rows, line, line]
        + [row_block] * 3
        + [pl.BlockSpec((many * LANES, width), lambda i: (i, 0))]
        + [weight_block] * 3
        + [whole((DEC_LEN, DEC_LEN)), pl.BlockSpec(memory_space=pltpu.SMEM)],
        out_specs=[all_rows, all_rows] + [row_block] * 3 + [whole((width, LANES))],
        out_shape=[sized(full)] + [sized(half)] * 4 + [jax.ShapeDtypeStruct((width, LANES), half)],
        scratch_shapes=[
            pltpu.VMEM((rows, width), full),
            pltpu.VMEM((rows, width), full),
            pltpu.VMEM((pairs, count, 2 * DEC_LEN), full),
            pltpu.VMEM((1, width), full),
            pltpu.VMEM((width, LANES), full),
        ],
        compiler_params=params(56),
        cost_estimate=light,
    )(
        mark, query_cross_grad, weights_c, after, gain_two, resid, hidden, gain_one, gain_ffn_grad,
        query, key, value, weights_o, weights_q, weights_k, weights_v, buckets, table,
    )


class Places:
    def __init__(self, dp_size, seq_size):
        self.dp, self.seq = dp_size, seq_size
        self.core = 2 if dp_size % 2 == 0 else 1
        self.ny = dp_size // self.core
        self.nx = self.ny if seq_size % self.ny == 0 else 1
        self.nz = seq_size // self.nx
        self.low = 2 if self.nz % 2 == 0 else 1
        self.high = self.nz // self.low
        dp_index, seq_index = lax.axis_index("dp"), lax.axis_index("seq")
        self.c, self.y = dp_index % self.core, dp_index // self.core
        self.x, self.z = seq_index % self.nx, seq_index // self.nx
        self.place = jnp.stack([self.y, self.c, self.x, self.z // self.low, self.z % self.low]).astype(jnp.int32)

    def shift(self, value, **steps):
        sizes = {"y": self.ny, "c": self.core, "h": self.high, "l": self.low, "x": self.nx}
        flat = lambda p: ((p["y"] * self.core + p["c"]) * self.seq) + (p["h"] * self.low + p["l"]) * self.nx + p["x"]
        pairs = []
        for numbers in itertools.product(*[range(size) for size in sizes.values()]):
            here = dict(zip(sizes, numbers))
            there = {axis: (here[axis] + steps.get(axis, 0)) % size for axis, size in sizes.items()}
            pairs.append((flat(here), flat(there)))
        return lax.ppermute(value, ("dp", "seq"), pairs)


def gate_kernel(*refs):
    refs[-1][...] = jnp.zeros_like(refs[-1])


def gate(*waits):
    arrays = jax.tree.leaves(waits)
    return pl.pallas_call(
        gate_kernel,
        name="gate",
        in_specs=[pl.BlockSpec(memory_space=pl.ANY)] * len(arrays),
        out_shape=jax.ShapeDtypeStruct((8, LANES), full),
        cost_estimate=pl.CostEstimate(flops=10**13, bytes_accessed=10**10, transcendentals=0),
    )(*arrays)


def marked(kernel, scalars=0):
    return lambda *refs: kernel(*refs[:scalars], *refs[scalars + 1 :])


class Term:
    def __init__(self, array, axes, fixed=(), columns=None):
        self.array, self.axes, self.fixed = array, axes, dict(fixed)
        self.columns = columns or (0, array.shape[-1])

    def at(self, axis, place):
        return Term(self.array, self.axes, {**self.fixed, axis: place}, self.columns)

    def free(self):
        sizes = zip(self.axes, self.array.shape)
        return tuple(size for axis, size in sizes if axis not in self.fixed)

    def spec(self):
        shape = [None if axis in self.fixed else size for axis, size in zip(self.axes, self.array.shape)]
        places = [self.fixed.get(axis, 0) for axis in self.axes]
        return pl.BlockSpec((*shape, *self.array.shape[-2:]), lambda i: (*places, 0, 0))


def totals_kernel(*refs, jobs):
    refs = list(refs)
    sources, outs = refs[: -len(jobs)], refs[-len(jobs) :]
    for groups, out in zip(jobs, outs):
        first = 0
        for columns in groups:
            total = None
            for low, high in columns:
                value = sources.pop(0)[..., low:high].astype(full)
                total = value if total is None else total + value
            out[..., first : first + total.shape[-1]] = total.astype(out.dtype)
            first += total.shape[-1]


def totals(mark, jobs, kind=half):
    terms = [term for groups in jobs for group in groups for term in group]
    shape = lambda groups: (
        *groups[0][0].free(),
        groups[0][0].array.shape[-2],
        sum(group[0].columns[1] - group[0].columns[0] for group in groups),
    )
    return pl.pallas_call(
        marked(
            functools.partial(totals_kernel, jobs=[[[term.columns for term in group] for group in groups] for groups in jobs])
        ),
        name="totals",
        grid=(1,),
        in_specs=[anywhere] + [term.spec() for term in terms],
        out_specs=[whole(shape(groups)) for groups in jobs],
        out_shape=[jax.ShapeDtypeStruct(shape(groups), kind) for groups in jobs],
        compiler_params=params(56),
        cost_estimate=light,
    )(mark, *[term.array for term in terms])


def final_kernel(place, *refs, terms, shapes, head_count):
    refs = list(refs)
    sources, outs = refs[: sum(len(columns) for columns in terms)], refs[sum(len(columns) for columns in terms) :]
    for columns, holds in zip(terms, shapes):
        total = None
        for low, high in columns:
            value = sources.pop(0)[..., low:high].astype(full)
            total = value if total is None else total + value
        first = 0
        for hold in holds:
            if hold == "plain":
                outs.pop(0)[...] = total
            elif hold == "pair":
                wide = outs[0].shape[1] * 2
                for out, value in zip(outs[:2], unpaired(total[:, first : first + wide], place[1])):
                    out[...] = value
                outs, first = outs[2:], first + wide
            elif hold == "rows":
                out, pieces = outs.pop(0), []
                wide = out.shape[0]
                for piece in range(0, total.shape[1] // wide, 2):
                    pieces += unpaired(total[:, piece * wide : (piece + 2) * wide], place[1])
                out[...] = jnp.concatenate(pieces, axis=0).T
            else:
                turned = total[:, first:].T
                for k in range(3):
                    outs.pop(0)[...] = turned[k : k + 1, :]
                bias = outs.pop(0)
                bias[...] = pltpu.roll(total[:, first:], LANES - 16, 1)[: bias.shape[0], :head_count]


def final(mark, at, sums, holds, shapes, head_count):
    terms = [part.terms for part in sums]
    arrays = [term for group in terms for term in group]
    as_prefetch = lambda spec: pl.BlockSpec(spec.block_shape, lambda i, _, index=spec.index_map: index(i))
    return pl.pallas_call(
        marked(
            functools.partial(
                final_kernel,
                terms=[[term.columns for term in group] for group in terms],
                shapes=holds,
                head_count=head_count,
            ),
            1,
        ),
        name="final",
        grid_spec=pltpu.PrefetchScalarGridSpec(
            num_scalar_prefetch=1,
            grid=(1,),
            in_specs=[anywhere] + [as_prefetch(term.spec()) for term in arrays],
            out_specs=[whole(shape) for shape in shapes],
        ),
        out_shape=[jax.ShapeDtypeStruct(shape, full) for shape in shapes],
        compiler_params=params(56),
        cost_estimate=light,
    )(at.place, mark, *[term.array for term in arrays])


class Reduction:
    def __init__(self, at, keep, send, order):
        self.at, self.order = at, order
        self.terms = [Term(keep, "yxhl")]
        if at.core == 2:
            self.terms.append(Term(at.shift(send, c=1), "yxhl"))
        self.left = "yxhl"


def advance(mark, *sums, together=False):
    at = sums[0].at
    axes = [part.order[0] for part in sums]
    size = lambda axis: {"y": at.ny, "x": at.nx, "h": at.high, "l": at.low}[axis]
    group = lambda part, k: [term.at(part.order[0], k) for term in part.terms]
    if together:
        places = [(axes[0], k) for k in range(1, size(axes[0]))]
        jobs = [[group(part, k) for part in sums] for _, k in places]
    else:
        places = [(axis, k) for axis in axes for k in range(1, size(axis))]
        jobs = [[group(part, k)] for part, axis in zip(sums, axes) for k in range(1, size(axis))]
    pieces = list(totals(mark, jobs)) if jobs else []
    got = [at.shift(piece, **{axis: k}) for piece, (axis, k) in zip(pieces, places)]
    first = 0
    for part in sums:
        axis, part.order = part.order[0], part.order[1:]
        part.left = part.left.replace(axis, "")
        part.terms = [term.at(axis, 0) for term in part.terms]
        wide = part.terms[0].columns[1] - part.terms[0].columns[0]
        for _ in range(1, size(axis)):
            if together:
                continue
            part.terms.append(Term(got.pop(0), part.left))
        if together:
            part.terms += [Term(piece, part.left, (), (first, first + wide)) for piece in got]
            first += wide
    return pieces


def shards(
    decoder_in,
    encoder_states,
    encoder_doc,
    decoder_doc,
    cotangent,
    gain_self,
    gain_cross,
    gain_ffn,
    self_query,
    self_key,
    self_value,
    self_out,
    bias_table,
    cross_query,
    cross_key,
    cross_value,
    cross_out,
    ff_in,
    ff_out,
    *,
    dp_size,
    seq_size,
):
    at = Places(dp_size, seq_size)
    width = decoder_in.shape[2]
    head_count = bias_table.shape[1]
    bucket_count = bias_table.shape[0]
    score_scale = (width // head_count) ** (-0.5)
    local_rows = decoder_in.shape[1]
    doc_count = local_rows // DEC_LEN
    position = lax.axis_index("seq")
    own_map = lax.dynamic_slice_in_dim(decoder_doc[0], position * doc_count, doc_count, 0)
    gain_self, gain_cross, gain_ffn = (gain[None, :] for gain in (gain_self, gain_cross, gain_ffn))

    enc_rows = encoder_states.shape[1]
    docs = jnp.pad(encoder_doc.astype(half), ((0, 15), (0, width - enc_rows)))
    shard = jnp.concatenate([encoder_states[0], docs], axis=0)
    near = [at.shift(shard, l=l) for l in range(1, at.low)]
    over = [at.shift(shard, x=x) for x in range(1, at.nx)]
    far = [at.shift(shard, h=h) for h in range(1, at.high)]
    mark = gate(shard)
    own = jnp.pad(own_map.astype(full), (0, LANES - doc_count))[:, None]
    lane = jnp.arange(LANES, dtype=jnp.int32)
    mark = (jnp.arange(local_rows, dtype=jnp.int32)[:, None] // DEC_LEN == lane).astype(half)
    buckets = jnp.asarray(bucket_map(DEC_LEN, bucket_count, MAX_REACH))

    query_self, key_self, value_self, out_self, after_self, normed_two, query_cross, normed_one = self_forward(
        mark, decoder_in[0], gain_self, gain_cross, self_query, self_key, self_value, self_out, cross_query,
        buckets, bias_table, score_scale,
    )
    near, over, far, query_cross = lax.optimization_barrier((near, over, far, query_cross))
    ahead = [at.shift(rows, l=l) for rows in far for l in range(1, at.low)]
    far_over = [[at.shift(rows, x=x) for rows in far] for x in range(1, at.nx)]
    near_over = [[at.shift(rows, x=x) for rows in near] for x in range(1, at.nx)]
    make = functools.partial(
        key_value, own=own, weights_k=cross_key, weights_v=cross_value, rows=enc_rows, doc_count=doc_count
    )
    column = [shard, *near]
    if at.high == 2 and at.low == 2:
        made = make(column, place=0, places=2)
        ahead, far_over, made = lax.optimization_barrier((ahead, far_over, made))
        column += [far[0], *ahead]
        made = make(column[2:], begun=made, place=1, places=2)
    else:
        step = at.low - 1
        for h, rows in enumerate(far):
            column += [rows, *ahead[h * step : (h + 1) * step]]
        made = make(column)
    sources, states, state = [], [], []
    for x in range(at.nx):
        if x:
            part = [over[x - 1], *near_over[x - 1]]
            for rows in far_over[x - 1]:
                part += [rows, *[at.shift(rows, l=l) for l in range(1, at.low)]]
            made = make(part)
        *source, rows = made
        sources.append(source)
        states.append(rows)
        state = cross_forward(query_cross, mark, source, state, x == at.nx - 1, score_scale)
    mixed_cross, out_cross, extended = state
    (
        after_cross, activated, resid_grad, branch_cross, mixed_grad, gain_ffn_grad,
        in_keep, in_send, out_keep, out_send,
    ) = feed_forward(at, after_self, out_cross, cross_out, gain_ffn, ff_in, ff_out, cotangent[0])
    ff_out_sum = Reduction(at, out_keep, out_send, "yxlh")
    ff_in_sum = Reduction(at, in_keep, in_send, "xylh")

    pairs = width // LANES
    cut = 1
    mark = gate(out_send, in_send)
    begun = cross_backward(mark, extended, mixed_grad, mixed_cross, sources, 0, cut, [], score_scale)
    mark = gate(advance(begun[0], ff_out_sum, ff_in_sum))
    query_grad, *grads = cross_backward(
        mark, extended, mixed_grad, mixed_cross, sources, cut, pairs - cut, begun, score_scale
    )
    mark = gate(advance(query_grad, ff_out_sum, ff_in_sum))

    if len(states) * states[0].shape[0] <= FUSED_ROWS:
        shares, cross_keep, cross_send = cross_close(
            mark, at, normed_two, query_grad, out_cross, branch_cross, states, grads, cross_key, cross_value
        )
    else:
        shares = [encoder_part(mark, at, grads[2 * x : 2 * x + 2], cross_key, cross_value) for x in range(at.nx)]
        summed = lambda side: sum(dot(rows, grads[2 * x + side], TN) for x, rows in enumerate(states))
        cross_keep, cross_send = laid_out(
            at, [dot(normed_two, query_grad, TN), dot(out_cross, branch_cross, TN), summed(0), summed(1)]
        )
    early = [at.shift(part[0], x=-1 - k) for k, part in enumerate(shares[1:])]
    late = [at.shift(part[1], x=-1 - k) for k, part in enumerate(shares[1:])]
    cross_sum = Reduction(at, cross_keep, cross_send, "yxlh")
    mark = gate(advance(cross_keep, ff_out_sum, ff_in_sum, together=True))
    mark = gate(shares[1:], cross_send, advance(mark, cross_sum))

    input_grad, branch_self, *self_grads, extra = self_backward(
        mark, at.seq, query_grad, cross_query, after_self, gain_cross, resid_grad, decoder_in[0], gain_self,
        gain_ffn_grad, query_self, key_self, value_self, self_out, self_query, self_key, self_value,
        buckets, bias_table, score_scale,
    )
    (low_ready,) = totals(input_grad, [[[Term(part, "h") for part in (shares[0][0], *early)]]])
    high_terms = [Term(part, "h") for part in (shares[0][1], *late, at.shift(low_ready, l=-1))]
    ready = advance(low_ready, ff_out_sum, ff_in_sum, together=True)
    mark = gate(low_ready, late, ready, advance(ready[0], cross_sum))
    first_keep, first_send, second_keep, second_send = weight_grads(
        mark,
        at,
        [[(normed_one, grad)] for grad in self_grads] + [[(out_self, branch_self)]],
        [[0], [1]],
        extra,
    )
    first_sum = Reduction(at, first_keep, first_send, "yxlh")
    second_sum = Reduction(at, second_keep, second_send, SECOND)
    mark = gate(first_send, second_send)

    n, m = width // at.dp, width // at.seq
    cross_ready = advance(mark, cross_sum)
    mark = gate(cross_ready, advance(cross_ready[0], first_sum, second_sum))
    ff_out_grad, ff_in_grad = final(
        mark, at, [ff_out_sum, ff_in_sum], [["rows"], ["plain"]],
        [(n, ff_out.shape[0] // at.seq), (m, ff_in.shape[1] // at.dp)], head_count,
    )
    activated, ff_in_grad = lax.optimization_barrier((activated, ff_in_grad))
    output = (after_cross + dot(activated, ff_out, NN)).astype(half)
    high_ready = totals(ff_in_grad, [[[term.at("h", h) for term in high_terms]] for h in range(1, at.high)])
    last_terms = [term.at("h", 0) for term in high_terms] + [
        Term(at.shift(piece, h=-1 - k), "") for k, piece in enumerate(high_ready)
    ]
    cross_ready = advance(high_ready[0], cross_sum)
    mark = gate(output, cross_ready, advance(cross_ready[0], first_sum, second_sum))
    mark = gate(advance(mark, first_sum, second_sum, together=True))
    small = (m, n)
    cross_query_grad, cross_out_grad, cross_key_grad, cross_value_grad = final(
        mark, at, [cross_sum], [["pair", "pair"]], [small] * 4, head_count
    )
    ready = advance(cross_value_grad, first_sum, second_sum, together=True)
    mark = gate(ready)
    (encoder_grad,) = totals(mark, [[last_terms]], full)
    mark = encoder_grad
    query_grad, key_grad, value_grad, out_grad, *gains, bias_grad = final(
        mark, at, [first_sum, second_sum], [["pair"], ["pair", "extra"]],
        [small] * 4 + [(1, m)] * 3 + [(bucket_count // at.seq, head_count)], head_count,
    )
    return (
        output[None],
        input_grad[None],
        encoder_grad[None],
        *(gain.reshape(-1) for gain in gains),
        query_grad,
        key_grad,
        value_grad,
        out_grad,
        bias_grad,
        cross_query_grad,
        cross_key_grad,
        cross_value_grad,
        cross_out_grad,
        ff_in_grad,
        ff_out_grad.T,
    )


def solution(mesh):
    placed = (
        P("dp", "seq", None),
        P("dp", "seq", None),
        P("dp", "seq"),
        P("dp", None),
        P("dp", "seq", None),
    ) + (P(),) * 14
    return jax.shard_map(
        functools.partial(shards, dp_size=mesh.shape["dp"], seq_size=mesh.shape["seq"]),
        mesh=mesh,
        in_specs=placed,
        out_specs=(
            P("dp", "seq", None),
            P("dp", "seq", None),
            P("dp", "seq", None),
            P("seq"),
            P("seq"),
            P("seq"),
            P("seq", "dp"),
            P("seq", "dp"),
            P("seq", "dp"),
            P("seq", "dp"),
            P("seq", None),
            P("seq", "dp"),
            P("seq", "dp"),
            P("seq", "dp"),
            P("seq", "dp"),
            P("seq", "dp"),
            P("seq", "dp"),
        ),
        check_vma=False,
    )
```
